256 devices in a mesh: rows: 16 (over x, z_hi, core), cols: 16 (over y, z_lo).
Axes of the slice: x: 4, y: 4, z: 8 (z_hi: 2, z_lo: 4; z = z_hi * 4 + z_lo), core: 2. Of those that a mesh axis runs over, the one named last changes fastest.
Arguments:
- elevation: float32 [2048, 16384], P('rows', 'cols'), may hold values from -6 to 6
- data_mask: int32 [2048, 16384], P('rows', 'cols'), may hold values 0 or 1
- tie_order: int32 [8], replicated, may hold values from 0 to 7, each once
Outputs:
- inflow: float32 [2048, 16384], P('rows', 'cols')
The draws below stay inside these ranges and needn't reach their ends.
Inputs may be any that keep to these rules, and one draw needn't show every extreme that they name: tie_order holds each of 0 to 7 once.
All inputs are finite; a program needn't handle non-finite values. No bound on the sum of `data_mask` on one device may be relied on, other than what follows from the above.
Results may differ from the reference program's by a relative error of at most 0.0003.
Values sent between devices are 32-bit elements; how exact they have to be, the bound alone decides.
No kernel may reach another device: no remote copies, remote signals or barrier semaphores. Data moves between devices by JAX's collectives and lax.ppermute only.
A program may use at most 64 MiB of HBM per device.

```python
import jax
import jax.numpy as jnp
from jax import lax

TILE_COLUMNS = 1024
ITERS = 8
NR = 2048
NC = 16384
N_COLS = 16


def plant(drawn, stream_key, low, high):
    spot = [jax.random.randint(jax.random.fold_in(stream_key, axis), (), 0, length) for axis, length in enumerate(drawn.shape)]
    widest = drawn.shape.index(max(drawn.shape))
    next_to = spot[:widest] + [(spot[widest] + 1) % drawn.shape[widest]] + spot[widest + 1:]
    return drawn.at[tuple(spot)].set(low).at[tuple(next_to)].set(high)


def block_levels(key, dims, shards, smallest, high):
    def one(axis_at, shards_of):
        heights = jax.random.uniform(jax.random.fold_in(jax.random.fold_in(key, 6), axis_at), (shards_of,), jnp.float32, smallest / len(shards), high / len(shards))
        return jnp.repeat(jnp.exp(heights), dims[axis_at] // shards_of).reshape((-1,) + (1,) * (len(dims) - axis_at - 1))

    level = one(*shards[0])
    for cut in shards[1:]:
        level = level * one(*cut)
    return level


def gaussian(key, shape, width, limit, shards=(), kind=jnp.bfloat16):
    drawn = jax.random.normal(key, shape, jnp.float32) * width
    if len(shards) > 0:
        drawn = block_levels(key, shape, shards, -0.22, 0.18) * drawn
    return jnp.clip(drawn, min=-limit, max=limit).astype(kind)


def setup_inputs(seed: int = 0) -> dict:
    key_list = jax.random.split(jax.random.key(seed), 4)
    return {
        "elevation": gaussian(key_list[0], (NR, NC), 1.0, 6.0, ((0, 16), (1, 16)), jnp.float32),
        "data_mask": plant((jax.random.randint(key_list[1], (NR, NC), 0, 4) < 3).astype(jnp.int32), jax.random.fold_in(key_list[1], 1), 0, 1),
        "tie_order": jax.random.permutation(key_list[2], 8).astype(jnp.int32),
    }


OFFSETS = ((0, 1), (1, 1), (1, 0), (1, -1), (0, -1), (-1, -1), (-1, 0), (-1, 1))
RECIPROCAL = (1.0, 0.7071067811865476, 1.0, 0.7071067811865476, 1.0, 0.7071067811865476, 1.0, 0.7071067811865476)
RETENTION = 0.1


def priorities(tie_order):
    places = jnp.arange(8, dtype=jnp.float32)
    values = 1.0 + 0.5 * (7.0 - places) / 7.0
    matches = (tie_order[:, None] == jnp.arange(8, dtype=jnp.int32)[None, :]).astype(jnp.float32)
    return jnp.sum(matches * values[:, None], axis=0)


def outflow_weight_matrix(height_pad, valid_pad, ranking_order):
    height = height_pad.shape[0] - 2
    breadth = height_pad.shape[1] - 2
    centre = height_pad[1:-1, 1:-1]
    slopes = []
    for number, (step_row, step_col) in enumerate(OFFSETS):
        beside = height_pad[1 + step_row:1 + step_row + height, 1 + step_col:1 + step_col + breadth]
        beside_ok = valid_pad[1 + step_row:1 + step_row + height, 1 + step_col:1 + step_col + breadth]
        slopes.append(beside_ok * ranking_order[number] * jnp.maximum(centre - beside, 0.0) * RECIPROCAL[number])
    slopes = jnp.stack(slopes)
    totals = jnp.sum(slopes, axis=0) + RETENTION
    return slopes / totals


def gather_inflow(weights, field_pad):
    height = field_pad.shape[0] - 2
    breadth = field_pad.shape[1] - 2
    summed_in = jnp.zeros((height, breadth), jnp.float32)
    for number, (step_row, step_col) in enumerate(OFFSETS):
        term = weights[number] * field_pad
        summed_in = summed_in + term[1 - step_row:1 - step_row + height, 1 - step_col:1 - step_col + breadth]
    return summed_in


def reference(elevation, data_mask, tie_order):
    ranking_order = priorities(tie_order)
    full_rows, full_cols = elevation.shape
    valid_flag = data_mask.astype(jnp.float32)
    over_rows, over_cols = full_rows // 8, full_cols // 8
    summed = (valid_flag * elevation).reshape(over_rows, 8, over_cols, 8).sum(axis=(1, 3))
    counts = valid_flag.reshape(over_rows, 8, over_cols, 8).sum(axis=(1, 3))
    overview = summed / (counts + 1.0)
    runoff = counts / 64.0
    coarse_w = outflow_weight_matrix(jnp.pad(overview, 2), jnp.pad(jnp.ones_like(overview), 2), ranking_order)
    flow_now = runoff
    for sweep in range(ITERS):
        flow_now = runoff + gather_inflow(coarse_w, jnp.pad(flow_now, 1))
    upsampled = jnp.repeat(jnp.repeat(flow_now, 8, axis=0), 8, axis=1)
    up_window = jnp.pad(upsampled, 1)
    elevation_window = jnp.pad(elevation, 2)
    valid_cols = jnp.pad(jnp.ones((full_cols,), jnp.float32), 2)
    valid_rows = jnp.pad(jnp.ones((full_rows,), jnp.float32), 2)

    def one_block(column_block):
        start_offset = (column_block * TILE_COLUMNS).astype(jnp.int32)
        height_values = lax.dynamic_slice_in_dim(elevation_window, start_offset, TILE_COLUMNS + 4, 1)
        valid_pad = valid_rows[:, None] * lax.dynamic_slice_in_dim(valid_cols, start_offset, TILE_COLUMNS + 4, 0)[None, :]
        ups = lax.dynamic_slice_in_dim(up_window, start_offset, TILE_COLUMNS + 2, 1)
        flags = lax.dynamic_slice_in_dim(valid_flag, start_offset, TILE_COLUMNS, 1)
        detailed_weight = outflow_weight_matrix(height_values, valid_pad, ranking_order)
        return flags + gather_inflow(detailed_weight, ups)

    blocks = lax.map(one_block, jnp.arange(N_COLS, dtype=jnp.int32))
    return jnp.moveaxis(blocks, 0, 1).reshape(full_rows, full_cols)
```

```python
import functools

import jax
import jax.numpy as jnp
from jax import lax
from jax.experimental import pallas as pl
from jax.experimental.pallas import tpu as pltpu
from jax.sharding import PartitionSpec as P

ITERS = 8
OFFSETS = ((0, 1), (1, 1), (1, 0), (1, -1), (0, -1), (-1, -1), (-1, 0), (-1, 1))
DIAGONAL = 0.7071067811865476
RETENTION = 0.1
OUTSIDE = 1e30
LANES = 128
VMEM = pltpu.VMEM
LIMIT = 48 * 1024 * 1024


def iota(shape, dim):
    return lax.broadcasted_iota(jnp.int32, shape, dim)


def coefficients(tie_ref, coef_ref):
    for place in range(8):
        k = tie_ref[place]
        value = 1.0 + 0.5 * (7.0 - place) / 7.0
        coef_ref[k] = jnp.where(k % 2 == 0, value, value * DIAGONAL).astype(jnp.float32)
    return [coef_ref[k] for k in range(8)]


def beside(left, mid, right):
    lane = iota(mid.shape, 1)
    west = jnp.where(lane == 0, pltpu.roll(left, 1, 1), pltpu.roll(mid, 1, 1))
    east = jnp.where(lane == LANES - 1, pltpu.roll(right, LANES - 1, 1), pltpu.roll(mid, LANES - 1, 1))
    return west, east


def neighbour(planes, j, row, k):
    step_row, step_col = OFFSETS[k]
    ref = planes[{0: 0, -1: 1, 1: 2}[step_col]]
    return ref[j, pl.ds(row + step_row, 8), :]


def spread(planes, chunks, first, count):
    centre, west, east = planes
    for j in range(chunks):
        w, e = beside(
            centre[(j - 1) % chunks, pl.ds(first, count), :],
            centre[j, pl.ds(first, count), :],
            centre[(j + 1) % chunks, pl.ds(first, count), :],
        )
        west[j, pl.ds(first, count), :] = w
        east[j, pl.ds(first, count), :] = e


def reciprocal_total(planes, j, row, coef):
    z = planes[0][j, pl.ds(row, 8), :]
    parts = [coef[k] * jnp.maximum(z - neighbour(planes, j, row, k), 0.0) for k in range(8)]
    total = ((parts[0] + parts[1]) + (parts[2] + parts[3])) + ((parts[4] + parts[5]) + (parts[6] + parts[7]))
    return 1.0 / (total + RETENTION)


def inward(planes, j, row, k, coef):
    z = planes[0][j, pl.ds(row, 8), :]
    return coef[(k + 4) % 8] * jnp.maximum(neighbour(planes, j, row, k) - z, 0.0)


def fields(z_planes, r_planes, j, row, coef):
    lane = iota((8, LANES), 1) % 8
    sub = iota((8, LANES), 0)
    at_east, at_west = lane == 7, lane == 0
    first, last = sub == 0, sub == 7
    t = [inward(z_planes, j, row, k, coef) * neighbour(r_planes, j, row, k) for k in range(8)]

    def split(east, west):
        own = jnp.where(at_east, west, jnp.where(at_west, east, east + west))
        other = jnp.where(at_east, east, jnp.where(at_west, west, 0.0))
        return own, other

    own0, other0 = split(t[0], t[4])
    own_down, other_down = split(t[1], t[3])
    own_down = own_down + t[2]
    own_up, other_up = split(t[7], t[5])
    own_up = own_up + t[6]
    a00 = own0 + jnp.where(first, 0.0, own_up) + jnp.where(last, 0.0, own_down)
    a01 = other0 + jnp.where(first, 0.0, other_up) + jnp.where(last, 0.0, other_down)
    a10 = jnp.where(first, own_up, jnp.where(last, own_down, 0.0))
    a11 = jnp.where(first, other_up, jnp.where(last, other_down, 0.0))
    return a00, a01, a10, a11


def block_rows(tiles):
    sub = iota(tiles[0].shape, 0)
    level = [tiles[t] for t in (0, 4, 2, 6, 1, 5, 3, 7)]
    for shift in (4, 2, 1):
        low = (sub & shift) == 0
        level = [
            jnp.where(low, a + pltpu.roll(a, 8 - shift, 0), b + pltpu.roll(b, shift, 0))
            for a, b in zip(level[0::2], level[1::2])
        ]
    return level[0]


def overview_kernel(el, mk, msg, edge):
    rows, cols = el.shape
    chunks = cols // LANES
    col = iota((cols, LANES), 0) // 8
    pick = jnp.where(col == iota((cols, LANES), 1), 1.0, 0.0).astype(jnp.bfloat16)
    sums, counts = [], []
    for g in range(rows // 64):
        s_parts, n_parts = [], []
        for j in range(chunks):
            s_tiles, n_tiles = [], []
            for t in range(8):
                at = (slice(64 * g + 8 * t, 64 * g + 8 * t + 8), slice(LANES * j, LANES * j + LANES))
                m = mk[at].astype(jnp.float32)
                n_tiles.append(m)
                s_tiles.append(m * el[at])
            s_parts.append(block_rows(s_tiles))
            n_parts.append(block_rows(n_tiles))
        sums.append(jnp.concatenate(s_parts, axis=1))
        counts.append(jnp.concatenate(n_parts, axis=1))
    s = jnp.concatenate(sums, axis=0)
    n = jnp.concatenate(counts, axis=0)
    hi = s.astype(jnp.bfloat16)
    rest = s - hi.astype(jnp.float32)
    mid = rest.astype(jnp.bfloat16)
    low = (rest - mid.astype(jnp.float32)).astype(jnp.bfloat16)
    left = jnp.concatenate([hi, mid, low, n.astype(jnp.bfloat16)], axis=0)
    out = lax.dot_general(left, pick, (((1,), (0,)), ((), ())), preferred_element_type=jnp.float32)
    k = rows // 8
    summed = out[0:k] + (out[k : 2 * k] + out[2 * k : 3 * k])
    count = out[3 * k : 4 * k]
    msg[0:k, :] = summed / (count + 1.0)
    msg[k : 2 * k, :] = count * (1.0 / 64.0)
    first = jnp.transpose(el[:, 0:LANES])
    last = jnp.transpose(el[:, cols - LANES : cols])
    msg[2 * k : 2 * k + 4, :] = first[0:4]
    msg[2 * k + 4 : 2 * k + 8, :] = last[LANES - 4 : LANES]
    edge[0:4, :] = el[0:4, :]
    edge[4:8, :] = el[rows - 4 : rows, :]


def row_message_kernel(own, from_a, from_b, edge, coarse, side, to_n, to_f):
    k = (own.shape[0] - 8) // 2
    cols = edge.shape[1]
    chunks = cols // LANES
    r, c = lax.axis_index("rows"), lax.axis_index("cols")
    count = lax.axis_size("cols")
    even = c % 2 == 0
    shape = own.shape
    a, b = from_a[...], from_b[...]
    line = iota(shape, 0)
    missing = jnp.where((line >= k) & (line < 2 * k), 0.0, OUTSIDE)
    right = jnp.where(jnp.full(shape, c == count - 1), missing, jnp.where(jnp.full(shape, even), a, b))
    left = jnp.where(jnp.full(shape, c == 0), missing, jnp.where(jnp.full(shape, even), b, a))
    lane = iota((2 * k, LANES), 1)
    near = jnp.where(lane < LANES // 2, right[0 : 2 * k], left[0 : 2 * k])
    mine = own[...]
    c4 = (mine[0:k], near[0:k], mine[k : 2 * k], near[k : 2 * k])
    for i, part in enumerate(c4):
        coarse[i * k : (i + 1) * k, :] = part
        to_n[i * k : (i + 1) * k, :] = part
        to_f[i * k : (i + 1) * k, :] = part
    cols_t = jnp.concatenate(
        [right[2 * k : 2 * k + 4], jnp.zeros((LANES - 8, LANES), jnp.float32), left[2 * k + 4 : 2 * k + 8]], axis=0
    )
    beyond = jnp.transpose(cols_t)
    side[...] = beyond
    rows = beyond.shape[0]
    upper = r % 2 == 0
    for j in range(chunks + 1):
        if j < chunks:
            top, bottom = edge[0:2, LANES * j : LANES * j + LANES], edge[6:8, LANES * j : LANES * j + LANES]
        else:
            top, bottom = beyond[0:2], beyond[rows - 2 : rows]
        cond = jnp.full((2, LANES), upper)
        to_n[4 * k + 2 * j : 4 * k + 2 * j + 2, :] = jnp.where(cond, bottom, top)
        to_f[4 * k + 2 * j : 4 * k + 2 * j + 2, :] = jnp.where(cond, top, bottom)


def coefficient_kernel(tie, el, side, out, coef_ref, zc, zw, ze, rc, rw, re):
    rows, cols = el.shape
    chunks = cols // LANES
    coef = coefficients(tie, coef_ref)
    z_planes, r_planes = (zc, zw, ze), (rc, rw, re)
    for j in range(chunks + 1):
        for at in (0, rows + 8):
            zc[j, at : at + 8, :] = jnp.zeros((8, LANES), jnp.float32)
            rc[j, at : at + 8, :] = jnp.zeros((8, LANES), jnp.float32)
        zc[j, 8 : 8 + rows, :] = el[:, LANES * j : LANES * j + LANES] if j < chunks else side[...]
    spread(z_planes, chunks + 1, 0, rows + 16)

    def totals(t, carry):
        row = pl.multiple_of(8 + 8 * t, 8)
        for j in range(chunks + 1):
            rc[j, pl.ds(row, 8), :] = reciprocal_total(z_planes, j, row, coef)
        return carry

    lax.fori_loop(0, rows // 8, totals, 0)
    spread(r_planes, chunks + 1, 0, rows + 16)

    def combine(t, carry):
        row = pl.multiple_of(8 + 8 * t, 8)
        for j in range(chunks):
            for i, field in enumerate(fields(z_planes, r_planes, j, row, coef)):
                out[i, pl.ds(pl.multiple_of(8 * t, 8), 8), LANES * j : LANES * j + LANES] = field
        return carry

    lax.fori_loop(0, rows // 8, combine, 0)


def inflow_kernel(
    tie, coarse, from_n, from_f, ends, side, given, mk, out,
    coef_ref, kc, kw, ke, sc, sw, se, run, gain, flow, zc, zw, ze, rc, rw, re, edge_fields, up_ref, vv_ref,
):
    k = coarse.shape[0] // 4
    rows, cols = mk.shape
    chunks = cols // LANES
    r, count = lax.axis_index("rows"), lax.axis_size("rows")
    upper = r % 2 == 0
    coef = coefficients(tie, coef_ref)
    n, f = from_n[...], from_f[...]
    shape = n.shape
    line = iota(shape, 0)
    missing = jnp.where((line >= 2 * k) & (line < 4 * k), 0.0, OUTSIDE)
    cond = jnp.full(shape, upper)
    above = jnp.where(jnp.full(shape, r == 0), missing, jnp.where(cond, f, n))
    below = jnp.where(jnp.full(shape, r == count - 1), missing, jnp.where(cond, n, f))

    k_planes, s_planes = (kc, kw, ke), (sc, sw, se)
    for j in range(2):
        kc[j, 0:8, :] = jnp.zeros((8, LANES), jnp.float32)
        kc[j, 8 + 3 * k : 16 + 3 * k, :] = jnp.zeros((8, LANES), jnp.float32)
        for ref, base, first in ((kc, 0, 8), (run, 2 * k, 0)):
            lo = base + j * k
            ref[j, first : first + k, :] = above[lo : lo + k]
            ref[j, first + k : first + 2 * k, :] = coarse[lo : lo + k, :]
            ref[j, first + 2 * k : first + 3 * k, :] = below[lo : lo + k]
    spread(k_planes, 2, 0, 3 * k + 16)
    recip = {}
    for j in range(2):
        for t in range(3 * k // 8):
            recip[j, t] = reciprocal_total(k_planes, j, 8 + 8 * t, coef)
    inner = range(1, 3 * k // 8 - 1)
    for j in range(2):
        for t in inner:
            for d in range(8):
                gain[d, j, 8 * t : 8 * t + 8, :] = inward(k_planes, j, 8 + 8 * t, d, coef)

    z_planes, r_planes = (zc, zw, ze), (rc, rw, re)
    for top in (True, False):
        halo = above if top else below
        for j in range(chunks + 1):
            lines = halo[4 * k + 2 * j : 4 * k + 2 * j + 2]
            pad = jnp.zeros((6, LANES), jnp.float32)
            if j < chunks:
                known = ends[0:16, LANES * j : LANES * j + LANES] if top else ends[16:32, LANES * j : LANES * j + LANES]
            else:
                known = side[0:16, :] if top else side[rows - 16 : rows, :]
            blank = jnp.zeros((8, LANES), jnp.float32)
            zc[j, 0:8, :] = blank
            zc[j, 32:40, :] = blank
            if top:
                zc[j, 8:16, :] = jnp.concatenate([pad, lines], axis=0)
                zc[j, 16:32, :] = known
            else:
                zc[j, 8:24, :] = known
                zc[j, 24:32, :] = jnp.concatenate([lines, pad], axis=0)
        spread(z_planes, chunks + 1, 0, 40)
        for j in range(chunks + 1):
            for t in range(3):
                rc[j, 8 + 8 * t : 16 + 8 * t, :] = reciprocal_total(z_planes, j, 8 + 8 * t, coef)
        spread(r_planes, chunks + 1, 8, 24)
        for j in range(chunks):
            for i, field in enumerate(fields(z_planes, r_planes, j, 16, coef)):
                edge_fields[0 if top else 1, i, :, LANES * j : LANES * j + LANES] = field

    for j in range(2):
        for t in range(3 * k // 8):
            sc[j, 8 * t : 8 * t + 8, :] = recip[j, t] * run[j, 8 * t : 8 * t + 8, :]
    spread(s_planes, 2, 0, 3 * k)
    for sweep in range(ITERS):
        for j in range(2):
            for t in inner:
                parts = [gain[d, j, 8 * t : 8 * t + 8, :] * neighbour(s_planes, j, 8 * t, d) for d in range(8)]
                total = ((parts[0] + parts[1]) + (parts[2] + parts[3])) + (
                    (parts[4] + parts[5]) + (parts[6] + parts[7])
                )
                flow[j, 8 * t : 8 * t + 8, :] = run[j, 8 * t : 8 * t + 8, :] + total
        if sweep < ITERS - 1:
            for j in range(2):
                for t in inner:
                    sc[j, 8 * t : 8 * t + 8, :] = recip[j, t] * flow[j, 8 * t : 8 * t + 8, :]
            spread(s_planes, 2, 8, 3 * k - 16)

    lane = iota((8, LANES), 1)
    block = lane // 8
    step = jnp.where(lane % 8 == 7, 1, jnp.where(lane % 8 == 0, -1, 0))
    per = LANES // 8
    for t in inner:
        main = flow[0, 8 * t : 8 * t + 8, :]
        apart = flow[1, 8 * t : 8 * t + 8, :]
        for j in range(chunks):
            here = block + per * j
            over = here + step
            up_ref[j, 8 * t : 8 * t + 8, :] = jnp.take_along_axis(main, here, axis=1, mode="promise_in_bounds")
            v = jnp.take_along_axis(main, over & (LANES - 1), axis=1, mode="promise_in_bounds")
            if j == 0:
                far = jnp.take_along_axis(apart, over & (LANES - 1), axis=1, mode="promise_in_bounds")
                v = jnp.where(lane == 0, far, v)
            if j == chunks - 1:
                far = jnp.take_along_axis(apart, over & (LANES - 1), axis=1, mode="promise_in_bounds")
                v = jnp.where(lane == LANES - 1, far, v)
            vv_ref[j, 8 * t : 8 * t + 8, :] = v

    high = iota((8, LANES), 0) < 4
    for j in range(chunks):
        for b in range(rows // 8):
            at = (slice(8 * b, 8 * b + 8), slice(LANES * j, LANES * j + LANES))
            row = k + b
            wide = [jnp.broadcast_to(up_ref[j, row + i : row + i + 1, :], (8, LANES)) for i in (-1, 0, 1)]
            apart = [jnp.broadcast_to(vv_ref[j, row + i : row + i + 1, :], (8, LANES)) for i in (-1, 0, 1)]
            if b == 0 or b == rows // 8 - 1:
                which = 0 if b == 0 else 1
                a = [edge_fields[which, i, :, at[1]] for i in range(4)]
            else:
                a = [given[i, at[0], at[1]] for i in range(4)]
            out[at] = mk[at].astype(jnp.float32) + (
                (a[0] * wide[1] + a[1] * apart[1])
                + (a[2] * jnp.where(high, wide[0], wide[2]) + a[3] * jnp.where(high, apart[0], apart[2]))
            )


def swap(x, axis, far):
    count = lax.axis_size(axis)
    if far:
        pairs = [(i, (i + 1) % count if i % 2 else (i - 1) % count) for i in range(count)]
    else:
        pairs = [(i, i ^ 1) for i in range(count)]
    return lax.ppermute(x, axis, pairs)


def f32(*shape):
    return jax.ShapeDtypeStruct(shape, jnp.float32)


def whole(count):
    return [pl.BlockSpec(memory_space=VMEM)] * count


def on_device(elevation, data_mask, tie_order):
    rows, cols = elevation.shape
    k, chunks = rows // 8, cols // LANES
    params = pltpu.CompilerParams(vmem_limit_bytes=LIMIT)
    msg, edge = pl.pallas_call(
        overview_kernel,
        out_shape=[f32(2 * k + 8, LANES), f32(8, cols)],
        in_specs=whole(2),
        out_specs=whole(2),
        compiler_params=params,
        name="overview",
    )(elevation, data_mask)
    from_b = swap(msg, "cols", True)
    from_a = swap(msg, "cols", False)
    size = 4 * k + 24
    coarse, side, to_n, to_f = pl.pallas_call(
        row_message_kernel,
        out_shape=[f32(4 * k, LANES), f32(rows, LANES), f32(size, LANES), f32(size, LANES)],
        in_specs=whole(4),
        out_specs=whole(4),
        compiler_params=params,
        name="row_message",
    )(msg, from_a, from_b, edge)
    from_n = swap(to_n, "rows", False)
    from_f = swap(to_f, "rows", True)
    smem = pl.BlockSpec(memory_space=pltpu.SMEM)
    fine = lambda height: [VMEM((chunks + 1, height, LANES), jnp.float32)] * 6
    given = pl.pallas_call(
        coefficient_kernel,
        out_shape=f32(4, rows, cols),
        in_specs=[smem] + whole(2),
        out_specs=pl.BlockSpec(memory_space=VMEM),
        scratch_shapes=[pltpu.SMEM((8,), jnp.float32)] + fine(rows + 16),
        compiler_params=params,
        cost_estimate=pl.CostEstimate(flops=20_000_000, bytes_accessed=4_000_000, transcendentals=0),
        name="coefficient_fields",
    )(tie_order, elevation, side)
    ends = jnp.concatenate([elevation[0:16], elevation[rows - 16 : rows]], axis=0)
    coarse_plane = lambda height: VMEM((2, height, LANES), jnp.float32)
    return pl.pallas_call(
        inflow_kernel,
        out_shape=f32(rows, cols),
        in_specs=[smem] + whole(7),
        out_specs=pl.BlockSpec(memory_space=VMEM),
        scratch_shapes=[pltpu.SMEM((8,), jnp.float32)]
        + [coarse_plane(3 * k + 16)] * 3
        + [coarse_plane(3 * k)] * 3
        + [coarse_plane(3 * k), VMEM((8, 2, 3 * k, LANES), jnp.float32), coarse_plane(3 * k)]
        + fine(40)
        + [VMEM((2, 4, 8, cols), jnp.float32)]
        + [VMEM((chunks, 3 * k, LANES), jnp.float32)] * 2,
        compiler_params=params,
        name="inflow",
    )(tie_order, coarse, from_n, from_f, ends, side, given, data_mask)


def solution(mesh):
    in_specs = (P("rows", "cols"), P("rows", "cols"), P())
    out_specs = P("rows", "cols")
    return jax.shard_map(
        on_device, mesh=mesh, in_specs=in_specs, out_specs=out_specs, check_vma=False
    )
```

```python
import jax
import jax.numpy as jnp
from jax import lax
from jax.experimental import pallas as pl
from jax.experimental.pallas import tpu as pltpu
from jax.sharding import PartitionSpec as P

ITERS = 8
OFFSETS = ((0, 1), (1, 1), (1, 0), (1, -1), (0, -1), (-1, -1), (-1, 0), (-1, 1))
DIAGONAL = 0.7071067811865476
RETENTION = 0.1
OUTSIDE = 1e30
LANES = 128
VMEM = pltpu.VMEM
LIMIT = 40 * 1024 * 1024


def iota(shape, dim):
    return lax.broadcasted_iota(jnp.int32, shape, dim)


def coefficients(tie_ref, coef_ref):
    for place in range(8):
        k = tie_ref[place]
        value = 1.0 + 0.5 * (7.0 - place) / 7.0
        scaled = jnp.where(k % 2 == 0, value, value * DIAGONAL).astype(jnp.float32)
        coef_ref[pl.ds(k, 1), :] = jnp.full((1, LANES), scaled)


def coefficient_tiles(coef_ref):
    return [jnp.broadcast_to(coef_ref[k : k + 1, :], (8, LANES)) for k in range(8)]


def neighbour(planes, j, row, k):
    step_row, step_col = OFFSETS[k]
    ref = planes[{0: 0, -1: 1, 1: 2}[step_col]]
    return ref[j, pl.ds(row + step_row, 8), :]


def spread(planes, wanted, row, ring=None):
    centre, west, east = planes
    lane = iota((8, LANES), 1)
    at = pl.ds(row, 8)
    ring = ring or (lambda j: j)
    to_east, to_west = {}, {}
    for j in wanted:
        for i in (ring(j - 1), j):
            if i not in to_east:
                to_east[i] = pltpu.roll(centre[i, at, :], 1, 1)
        for i in (j, ring(j + 1)):
            if i not in to_west:
                to_west[i] = pltpu.roll(centre[i, at, :], LANES - 1, 1)
        west[j, at, :] = jnp.where(lane == 0, to_east[ring(j - 1)], to_east[j])
        east[j, at, :] = jnp.where(lane == LANES - 1, to_west[ring(j + 1)], to_west[j])


def reciprocal_total(planes, j, row, coef):
    z = planes[0][j, pl.ds(row, 8), :]
    parts = [coef[k] * jnp.maximum(z - neighbour(planes, j, row, k), 0.0) for k in range(8)]
    total = ((parts[0] + parts[1]) + (parts[2] + parts[3])) + ((parts[4] + parts[5]) + (parts[6] + parts[7]))
    return 1.0 / (total + RETENTION)


def inward(planes, j, row, k, coef):
    z = planes[0][j, pl.ds(row, 8), :]
    return coef[(k + 4) % 8] * jnp.maximum(neighbour(planes, j, row, k) - z, 0.0)


def fields(z_planes, r_planes, j, row, coef, top=0, bottom=7):
    lane = iota((8, LANES), 1) % 8
    sub = iota((8, LANES), 0)
    at_east, at_west = lane == 7, lane == 0
    first, last = sub == top, sub == bottom
    t = [inward(z_planes, j, row, k, coef) * neighbour(r_planes, j, row, k) for k in range(8)]

    def split(east, west):
        own = jnp.where(at_east, west, jnp.where(at_west, east, east + west))
        other = jnp.where(at_east, east, jnp.where(at_west, west, 0.0))
        return own, other

    own0, other0 = split(t[0], t[4])
    own_down, other_down = split(t[1], t[3])
    own_down = own_down + t[2]
    own_up, other_up = split(t[7], t[5])
    own_up = own_up + t[6]
    a00 = own0 + jnp.where(first, 0.0, own_up) + jnp.where(last, 0.0, own_down)
    a01 = other0 + jnp.where(first, 0.0, other_up) + jnp.where(last, 0.0, other_down)
    a10 = jnp.where(first, own_up, jnp.where(last, own_down, 0.0))
    a11 = jnp.where(first, other_up, jnp.where(last, other_down, 0.0))
    return a00, a01, a10, a11


def block_rows(tiles):
    sub = iota(tiles[0].shape, 0)
    level = [tiles[t] for t in (0, 4, 2, 6, 1, 5, 3, 7)]
    for shift in (4, 2, 1):
        low = (sub & shift) == 0
        level = [
            jnp.where(low, a + pltpu.roll(a, 8 - shift, 0), b + pltpu.roll(b, shift, 0))
            for a, b in zip(level[0::2], level[1::2])
        ]
    return level[0]


PIECES = 4
PARTS = 4


def overview_kernel(tie_hbm, el_hbm, mk_hbm, msg, el, mk, coef, tie, tie_sem, el_sem, mk_sem):
    rows, cols = el.shape
    chunks = cols // LANES
    size = rows // PIECES
    fetch = []
    for p in range(PIECES):
        at = pl.ds(p * size, size)
        fetch.append(
            (
                pltpu.make_async_copy(el_hbm.at[at, :], el.at[at, :], el_sem.at[p]),
                pltpu.make_async_copy(mk_hbm.at[at, :], mk.at[at, :], mk_sem.at[p]),
            )
        )
    for pair in fetch:
        for copy in pair:
            copy.start()
    tie_copy = pltpu.make_async_copy(tie_hbm, tie, tie_sem)
    tie_copy.start()
    col = iota((cols, LANES), 0) // 8
    pick = jnp.where(col == iota((cols, LANES), 1), 1.0, 0.0).astype(jnp.bfloat16)
    tie_copy.wait()
    coefficients(tie, coef)
    sums, counts = [], []
    waited = 0
    for g in range(rows // 64):
        while waited * size < 64 * (g + 1):
            for copy in fetch[waited]:
                copy.wait()
            waited += 1
        s_parts, n_parts = [], []
        for j in range(chunks):
            s_tiles, n_tiles = [], []
            for t in range(8):
                at = (slice(64 * g + 8 * t, 64 * g + 8 * t + 8), slice(LANES * j, LANES * j + LANES))
                m = mk[at].astype(jnp.float32)
                n_tiles.append(m)
                s_tiles.append(m * el[at])
            s_parts.append(block_rows(s_tiles))
            n_parts.append(block_rows(n_tiles))
        sums.append(jnp.concatenate(s_parts, axis=1))
        counts.append(jnp.concatenate(n_parts, axis=1))
    s = jnp.concatenate(sums, axis=0)
    n = jnp.concatenate(counts, axis=0)
    hi = s.astype(jnp.bfloat16)
    rest = s - hi.astype(jnp.float32)
    mid = rest.astype(jnp.bfloat16)
    low = (rest - mid.astype(jnp.float32)).astype(jnp.bfloat16)
    left = jnp.concatenate([hi, mid, low, n.astype(jnp.bfloat16)], axis=0)
    out = lax.dot_general(left, pick, (((1,), (0,)), ((), ())), preferred_element_type=jnp.float32)
    k = rows // 8
    summed = out[0:k] + (out[k : 2 * k] + out[2 * k : 3 * k])
    count = out[3 * k : 4 * k]
    msg[0:k, :] = summed / (count + 1.0)
    msg[k : 2 * k, :] = count * (1.0 / 64.0)
    first = jnp.transpose(el[:, 0:LANES])
    last = jnp.transpose(el[:, cols - LANES : cols])
    msg[2 * k : 2 * k + 4, :] = first[0:4]
    msg[2 * k + 4 : 2 * k + 8, :] = last[LANES - 4 : LANES]


def row_message_kernel(own, from_a, from_b, el, coarse, side, to_n, to_f):
    k = (own.shape[0] - 8) // 2
    rows, cols = el.shape
    chunks = cols // LANES
    r, c = lax.axis_index("rows"), lax.axis_index("cols")
    count = lax.axis_size("cols")
    even = c % 2 == 0
    shape = own.shape
    a, b = from_a[...], from_b[...]
    line = iota(shape, 0)
    missing = jnp.where((line >= k) & (line < 2 * k), 0.0, OUTSIDE)
    right = jnp.where(jnp.full(shape, c == count - 1), missing, jnp.where(jnp.full(shape, even), a, b))
    left = jnp.where(jnp.full(shape, c == 0), missing, jnp.where(jnp.full(shape, even), b, a))
    lane = iota((2 * k, LANES), 1)
    near = jnp.where(lane < LANES // 2, right[0 : 2 * k], left[0 : 2 * k])
    mine = own[...]
    c4 = (mine[0:k], near[0:k], mine[k : 2 * k], near[k : 2 * k])
    for i, part in enumerate(c4):
        coarse[i * k : (i + 1) * k, :] = part
        to_n[i * k : (i + 1) * k, :] = part
        to_f[i * k : (i + 1) * k, :] = part
    cols_t = jnp.concatenate(
        [right[2 * k : 2 * k + 4], jnp.zeros((LANES - 8, LANES), jnp.float32), left[2 * k + 4 : 2 * k + 8]], axis=0
    )
    beyond = jnp.transpose(cols_t)
    side[...] = beyond
    upper = r % 2 == 0
    for j in range(chunks + 1):
        if j < chunks:
            lanes = slice(LANES * j, LANES * j + LANES)
            top, bottom = el[0:2, lanes], el[rows - 2 : rows, lanes]
        else:
            top, bottom = beyond[0:2], beyond[rows - 2 : rows]
        cond = jnp.full((2, LANES), upper)
        to_n[4 * k + 2 * j : 4 * k + 2 * j + 2, :] = jnp.where(cond, bottom, top)
        to_f[4 * k + 2 * j : 4 * k + 2 * j + 2, :] = jnp.where(cond, top, bottom)


def middle_kernel(coefs, el, out, recip, zc, zw, ze, rc, rw, re):
    rows, cols = el.shape
    chunks = cols // LANES
    coef = coefficient_tiles(coefs)
    z_planes, r_planes = (zc, zw, ze), (rc, rw, re)
    inner, core = range(1, chunks - 1), range(2, chunks - 2)
    blank = jnp.zeros((8, LANES), jnp.float32)
    for at in (0, rows + 8):
        for j in inner:
            for ref in z_planes + r_planes:
                ref[j, at : at + 8, :] = blank

    def lift(t, carry):
        row = pl.multiple_of(8 + 8 * t, 8)
        for j in range(chunks):
            zc[j, pl.ds(row, 8), :] = el[pl.ds(pl.multiple_of(8 * t, 8), 8), LANES * j : LANES * j + LANES]
        spread(z_planes, inner, row)
        return carry

    lax.fori_loop(0, rows // 8, lift, 0)

    def totals(t, carry):
        row = pl.multiple_of(8 + 8 * t, 8)
        for j in inner:
            total = reciprocal_total(z_planes, j, row, coef)
            rc[j, pl.ds(row, 8), :] = total
            recip[j - 1, pl.ds(pl.multiple_of(8 * t, 8), 8), :] = total
        spread(r_planes, core, row)
        return carry

    lax.fori_loop(0, rows // 8, totals, 0)

    def combine(t, carry):
        row = pl.multiple_of(8 + 8 * t, 8)
        for j in core:
            for i, field in enumerate(fields(z_planes, r_planes, j, row, coef)):
                out[i, j - 2, pl.ds(pl.multiple_of(8 * t, 8), 8), :] = field
        return carry

    lax.fori_loop(0, rows // 8, combine, 0)


def outer_kernel(coefs, el, side, known, out, recip, zc, zw, ze, rc, rw, re):
    rows, cols = el.shape
    chunks = cols // LANES
    coef = coefficient_tiles(coefs)
    z_planes, r_planes = (zc, zw, ze), (rc, rw, re)
    order = (chunks - 3, chunks - 2, chunks - 1, chunks, 0, 1, 2)
    blank = jnp.zeros((8, LANES), jnp.float32)
    for at in (0, rows + 8):
        for i in range(1, 6):
            for ref in z_planes + r_planes:
                ref[i, at : at + 8, :] = blank

    def lift(t, carry):
        row = pl.multiple_of(8 + 8 * t, 8)
        at = pl.ds(pl.multiple_of(8 * t, 8), 8)
        for i, j in enumerate(order):
            zc[i, pl.ds(row, 8), :] = el[at, LANES * j : LANES * j + LANES] if j < chunks else side[at, :]
        spread(z_planes, range(1, 6), row)
        return carry

    lax.fori_loop(0, rows // 8, lift, 0)

    def totals(t, carry):
        row = pl.multiple_of(8 + 8 * t, 8)
        at = pl.ds(pl.multiple_of(8 * t, 8), 8)
        for i, j in enumerate(order):
            if i in (2, 3, 4):
                total = reciprocal_total(z_planes, i, row, coef)
                recip[i - 2, at, :] = total
            else:
                total = known[j - 1, at, :]
            rc[i, pl.ds(row, 8), :] = total
        spread(r_planes, (1, 2, 4, 5), row)
        return carry

    lax.fori_loop(0, rows // 8, totals, 0)

    def combine(t, carry):
        row = pl.multiple_of(8 + 8 * t, 8)
        for n, i in enumerate((4, 5, 1, 2)):
            for which, field in enumerate(fields(z_planes, r_planes, i, row, coef)):
                out[which, n, pl.ds(pl.multiple_of(8 * t, 8), 8), :] = field
        return carry

    lax.fori_loop(0, rows // 8, combine, 0)


def inflow_kernel(
    coefs, coarse, from_n, from_f, el, side, middle, outer, middle_recip, outer_recip, mk, out_hbm,
    kc, kw, ke, sc, sw, se, run, gain, flow, zc, zw, ze, rc, rw, re, up_ref, vv_ref, out, out_sem,
):
    k = coarse.shape[0] // 4
    rows, cols = mk.shape
    chunks = cols // LANES
    r, count = lax.axis_index("rows"), lax.axis_size("rows")
    upper = r % 2 == 0
    coef = coefficient_tiles(coefs)
    n, f = from_n[...], from_f[...]
    shape = n.shape
    line = iota(shape, 0)
    missing = jnp.where((line >= 2 * k) & (line < 4 * k), 0.0, OUTSIDE)
    cond = jnp.full(shape, upper)
    above = jnp.where(jnp.full(shape, r == 0), missing, jnp.where(cond, f, n))
    below = jnp.where(jnp.full(shape, r == count - 1), missing, jnp.where(cond, n, f))

    k_planes, s_planes = (kc, kw, ke), (sc, sw, se)
    around = lambda size: (lambda j: j % size)
    for j in range(2):
        kc[j, 0:8, :] = jnp.zeros((8, LANES), jnp.float32)
        kc[j, 8 + 3 * k : 16 + 3 * k, :] = jnp.zeros((8, LANES), jnp.float32)
        for ref, base, first in ((kc, 0, 8), (run, 2 * k, 0)):
            lo = base + j * k
            ref[j, first : first + k, :] = above[lo : lo + k]
            ref[j, first + k : first + 2 * k, :] = coarse[lo : lo + k, :]
            ref[j, first + 2 * k : first + 3 * k, :] = below[lo : lo + k]
    for t in range(3 * k // 8 + 2):
        spread(k_planes, range(2), 8 * t, around(2))
    recip = {}
    for j in range(2):
        for t in range(3 * k // 8):
            recip[j, t] = reciprocal_total(k_planes, j, 8 + 8 * t, coef)
    inner = range(1, 3 * k // 8 - 1)
    for j in range(2):
        for t in inner:
            for d in range(8):
                gain[d, j, 8 * t : 8 * t + 8, :] = inward(k_planes, j, 8 + 8 * t, d, coef)

    z_planes, r_planes = (zc, zw, ze), (rc, rw, re)
    ring = around(chunks + 1)
    every = range(chunks + 1)
    for j in every:
        up2, down2 = above[4 * k + 2 * j : 4 * k + 2 * j + 2], below[4 * k + 2 * j : 4 * k + 2 * j + 2]
        if j < chunks:
            first, last = el[0:8, LANES * j : LANES * j + LANES], el[rows - 8 : rows, LANES * j : LANES * j + LANES]
        else:
            first, last = side[0:8, :], side[rows - 8 : rows, :]
        blank = jnp.zeros((8, LANES), jnp.float32)
        for at in (0, 16, 32):
            zc[j, at : at + 8, :] = blank
        zc[j, 8:16, :] = jnp.concatenate([up2, first[0:2], last[6:8], down2], axis=0)
        zc[j, 24:32, :] = jnp.concatenate([up2[1:2], first[0:3], last[5:8], down2[0:1]], axis=0)
    for row in (0, 8, 16, 24, 32):
        spread(z_planes, every, row, ring)
    for j in every:
        total = reciprocal_total(z_planes, j, 8, coef)
        if 1 <= j < chunks - 1:
            near = middle_recip.at[j - 1]
        else:
            near = outer_recip.at[{chunks - 1: 0, chunks: 1, 0: 2}[j]]
        first, last = near[0:8, :], near[rows - 8 : rows, :]
        for at in (0, 16):
            rc[j, at : at + 8, :] = jnp.zeros((8, LANES), jnp.float32)
        rc[j, 8:16, :] = jnp.concatenate([total[1:3], first[1:3], last[5:7], total[5:7]], axis=0)
    for row in (0, 8, 16):
        spread(r_planes, every, row, ring)
    border = {}
    for j in range(chunks):
        border[j] = fields((zc.at[:, 16:40, :], zw.at[:, 16:40, :], ze.at[:, 16:40, :]), r_planes, j, 8, coef, 1, 6)

    for j in range(2):
        for t in range(3 * k // 8):
            sc[j, 8 * t : 8 * t + 8, :] = recip[j, t] * run[j, 8 * t : 8 * t + 8, :]
    for t in range(3 * k // 8):
        spread(s_planes, range(2), 8 * t, around(2))
    for sweep in range(ITERS):
        for j in range(2):
            for t in inner:
                parts = [gain[d, j, 8 * t : 8 * t + 8, :] * neighbour(s_planes, j, 8 * t, d) for d in range(8)]
                total = ((parts[0] + parts[1]) + (parts[2] + parts[3])) + (
                    (parts[4] + parts[5]) + (parts[6] + parts[7])
                )
                flow[j, 8 * t : 8 * t + 8, :] = run[j, 8 * t : 8 * t + 8, :] + total
        if sweep < ITERS - 1:
            for j in range(2):
                for t in inner:
                    sc[j, 8 * t : 8 * t + 8, :] = recip[j, t] * flow[j, 8 * t : 8 * t + 8, :]
            for t in inner:
                spread(s_planes, range(2), 8 * t, around(2))

    lane = iota((8, LANES), 1)
    block = lane // 8
    step = jnp.where(lane % 8 == 7, 1, jnp.where(lane % 8 == 0, -1, 0))
    per = LANES // 8
    for t in inner:
        main = flow[0, 8 * t : 8 * t + 8, :]
        apart = flow[1, 8 * t : 8 * t + 8, :]
        for j in range(chunks):
            here = block + per * j
            over = here + step
            up_ref[j, 8 * t : 8 * t + 8, :] = jnp.take_along_axis(main, here, axis=1, mode="promise_in_bounds")
            v = jnp.take_along_axis(main, over & (LANES - 1), axis=1, mode="promise_in_bounds")
            if j == 0:
                far = jnp.take_along_axis(apart, over & (LANES - 1), axis=1, mode="promise_in_bounds")
                v = jnp.where(lane == 0, far, v)
            if j == chunks - 1:
                far = jnp.take_along_axis(apart, over & (LANES - 1), axis=1, mode="promise_in_bounds")
                v = jnp.where(lane == LANES - 1, far, v)
            vv_ref[j, 8 * t : 8 * t + 8, :] = v

    sub = iota((8, LANES), 0)
    high = sub < 4
    writes = []
    for b in range(rows // 8):
        for j in range(chunks):
            lanes = slice(LANES * j, LANES * j + LANES)
            at = slice(8 * b, 8 * b + 8)
            row = k + b
            wide = [jnp.broadcast_to(up_ref[j, row + i : row + i + 1, :], (8, LANES)) for i in (-1, 0, 1)]
            apart = [jnp.broadcast_to(vv_ref[j, row + i : row + i + 1, :], (8, LANES)) for i in (-1, 0, 1)]
            if 2 <= j < chunks - 2:
                a = [middle[i, j - 2, at, :] for i in range(4)]
            else:
                a = [outer[i, j if j < 2 else j - chunks + 4, at, :] for i in range(4)]
            if b == 0:
                a = [jnp.where(sub < 2, pltpu.roll(border[j][i], 7, 0), a[i]) for i in range(4)]
            if b == rows // 8 - 1:
                a = [jnp.where(sub > 5, pltpu.roll(border[j][i], 1, 0), a[i]) for i in range(4)]
            out[at, lanes] = mk[at, lanes].astype(jnp.float32) + (
                (a[0] * wide[1] + a[1] * apart[1])
                + (a[2] * jnp.where(high, wide[0], wide[2]) + a[3] * jnp.where(high, apart[0], apart[2]))
            )
        size = rows // PARTS
        if (8 * b + 8) % size == 0:
            p = 8 * b // size
            lines = pl.ds(p * size, size)
            copy = pltpu.make_async_copy(out.at[lines, :], out_hbm.at[lines, :], out_sem.at[p])
            copy.start()
            writes.append(copy)
    for copy in writes:
        copy.wait()


def swap(x, axis, far):
    count = lax.axis_size(axis)
    if far:
        pairs = [(i, (i + 1) % count if i % 2 else (i - 1) % count) for i in range(count)]
    else:
        pairs = [(i, i ^ 1) for i in range(count)]
    return lax.ppermute(x, axis, pairs)


def f32(*shape):
    return jax.ShapeDtypeStruct(shape, jnp.float32)


def whole(count):
    return [pl.BlockSpec(memory_space=VMEM)] * count


def on_device(elevation, data_mask, tie_order):
    rows, cols = elevation.shape
    k, chunks = rows // 8, cols // LANES
    params = pltpu.CompilerParams(vmem_limit_bytes=LIMIT)
    dma = pltpu.SemaphoreType.DMA
    hbm = pl.BlockSpec(memory_space=pltpu.HBM)
    msg, el, mk, coefs = pl.pallas_call(
        overview_kernel,
        out_shape=[f32(2 * k + 8, LANES), f32(rows, cols), jax.ShapeDtypeStruct((rows, cols), jnp.int32), f32(8, LANES)],
        in_specs=[hbm] * 3,
        out_specs=whole(4),
        scratch_shapes=[pltpu.SMEM((8,), jnp.int32), dma, dma((PIECES,)), dma((PIECES,))],
        compiler_params=params,
        name="overview",
    )(tie_order, elevation, data_mask)
    from_b = swap(msg, "cols", True)
    from_a = swap(msg, "cols", False)
    plane = lambda count, height: VMEM((count, height, LANES), jnp.float32)
    cost = pl.CostEstimate(flops=10_000_000, bytes_accessed=3_000_000, transcendentals=0)
    middle, middle_recip = pl.pallas_call(
        middle_kernel,
        out_shape=[f32(4, chunks - 4, rows, LANES), f32(chunks - 2, rows, LANES)],
        in_specs=whole(2),
        out_specs=whole(2),
        scratch_shapes=[plane(chunks, rows + 16)] * 6,
        compiler_params=params,
        cost_estimate=cost,
        name="middle_fields",
    )(coefs, el)
    size = 4 * k + 24
    coarse, side, to_n, to_f = pl.pallas_call(
        row_message_kernel,
        out_shape=[f32(4 * k, LANES), f32(rows, LANES), f32(size, LANES), f32(size, LANES)],
        in_specs=whole(4),
        out_specs=whole(4),
        compiler_params=params,
        name="row_message",
    )(msg, from_a, from_b, el)
    from_n = swap(to_n, "rows", False)
    from_f = swap(to_f, "rows", True)
    outer, outer_recip = pl.pallas_call(
        outer_kernel,
        out_shape=[f32(4, 4, rows, LANES), f32(3, rows, LANES)],
        in_specs=whole(4),
        out_specs=whole(2),
        scratch_shapes=[plane(7, rows + 16)] * 6,
        compiler_params=params,
        cost_estimate=cost,
        name="outer_fields",
    )(coefs, el, side, middle_recip)
    return pl.pallas_call(
        inflow_kernel,
        out_shape=f32(rows, cols),
        in_specs=whole(11),
        out_specs=hbm,
        scratch_shapes=[plane(2, 3 * k + 16)] * 3
        + [plane(2, 3 * k)] * 4
        + [VMEM((8, 2, 3 * k, LANES), jnp.float32), plane(2, 3 * k)]
        + [plane(chunks + 1, 40)] * 3
        + [plane(chunks + 1, 24)] * 3
        + [plane(chunks, 3 * k)] * 2
        + [VMEM((rows, cols), jnp.float32), dma((PARTS,))],
        compiler_params=params,
        name="inflow",
    )(coefs, coarse, from_n, from_f, el, side, middle, outer, middle_recip, outer_recip, mk)


def solution(mesh):
    in_specs = (P("rows", "cols"), P("rows", "cols"), P())
    out_specs = P("rows", "cols")
    return jax.shard_map(
        on_device, mesh=mesh, in_specs=in_specs, out_specs=out_specs, check_vma=False
    )
```

```python
import jax
import jax.numpy as jnp
from jax import lax
from jax.experimental import pallas as pl
from jax.experimental.pallas import tpu as pltpu
from jax.sharding import PartitionSpec as P

ITERS = 8
OFFSETS = ((0, 1), (1, 1), (1, 0), (1, -1), (0, -1), (-1, -1), (-1, 0), (-1, 1))
DIAGONAL = 0.7071067811865476
RETENTION = 0.1
OUTSIDE = 1e30
LANES = 128
VMEM = pltpu.VMEM
LIMIT = 40 * 1024 * 1024


def iota(shape, dim):
    return lax.broadcasted_iota(jnp.int32, shape, dim)


def coefficients(tie_ref, coef_ref):
    for place in range(8):
        k = tie_ref[place]
        value = 1.0 + 0.5 * (7.0 - place) / 7.0
        scaled = jnp.where(k % 2 == 0, value, value * DIAGONAL).astype(jnp.float32)
        coef_ref[pl.ds(k, 1), :] = jnp.full((1, LANES), scaled)


def coefficient_tiles(coef_ref):
    return [jnp.broadcast_to(coef_ref[k : k + 1, :], (8, LANES)) for k in range(8)]


def neighbour(planes, j, row, k):
    step_row, step_col = OFFSETS[k]
    ref = planes[{0: 0, -1: 1, 1: 2}[step_col]]
    return ref[j, pl.ds(row + step_row, 8), :]


def spread(planes, wanted, row, ring=None):
    centre, west, east = planes
    lane = iota((8, LANES), 1)
    at = pl.ds(row, 8)
    ring = ring or (lambda j: j)
    to_east, to_west = {}, {}
    for j in wanted:
        for i in (ring(j - 1), j):
            if i not in to_east:
                to_east[i] = pltpu.roll(centre[i, at, :], 1, 1)
        for i in (j, ring(j + 1)):
            if i not in to_west:
                to_west[i] = pltpu.roll(centre[i, at, :], LANES - 1, 1)
        west[j, at, :] = jnp.where(lane == 0, to_east[ring(j - 1)], to_east[j])
        east[j, at, :] = jnp.where(lane == LANES - 1, to_west[ring(j + 1)], to_west[j])


def reciprocal_total(planes, j, row, coef):
    z = planes[0][j, pl.ds(row, 8), :]
    parts = [coef[k] * jnp.maximum(z - neighbour(planes, j, row, k), 0.0) for k in range(8)]
    total = ((parts[0] + parts[1]) + (parts[2] + parts[3])) + ((parts[4] + parts[5]) + (parts[6] + parts[7]))
    return 1.0 / (total + RETENTION)


def inward(planes, j, row, k, coef):
    z = planes[0][j, pl.ds(row, 8), :]
    return coef[(k + 4) % 8] * jnp.maximum(neighbour(planes, j, row, k) - z, 0.0)


def fields(z_planes, r_planes, j, row, coef, top=0, bottom=7):
    lane = iota((8, LANES), 1) % 8
    sub = iota((8, LANES), 0)
    at_east, at_west = lane == 7, lane == 0
    first, last = sub == top, sub == bottom
    t = [inward(z_planes, j, row, k, coef) * neighbour(r_planes, j, row, k) for k in range(8)]

    def split(east, west):
        own = jnp.where(at_east, west, jnp.where(at_west, east, east + west))
        other = jnp.where(at_east, east, jnp.where(at_west, west, 0.0))
        return own, other

    own0, other0 = split(t[0], t[4])
    own_down, other_down = split(t[1], t[3])
    own_down = own_down + t[2]
    own_up, other_up = split(t[7], t[5])
    own_up = own_up + t[6]
    a00 = own0 + jnp.where(first, 0.0, own_up) + jnp.where(last, 0.0, own_down)
    a01 = other0 + jnp.where(first, 0.0, other_up) + jnp.where(last, 0.0, other_down)
    a10 = jnp.where(first, own_up, jnp.where(last, own_down, 0.0))
    a11 = jnp.where(first, other_up, jnp.where(last, other_down, 0.0))
    return a00, a01, a10, a11


def block_rows(tiles):
    sub = iota(tiles[0].shape, 0)
    level = [tiles[t] for t in (0, 4, 2, 6, 1, 5, 3, 7)]
    for shift in (4, 2, 1):
        low = (sub & shift) == 0
        level = [
            jnp.where(low, a + pltpu.roll(a, 8 - shift, 0), b + pltpu.roll(b, shift, 0))
            for a, b in zip(level[0::2], level[1::2])
        ]
    return level[0]


PIECES = 8
PARTS = 4


def overview_kernel(tie_hbm, el_hbm, mk_hbm, msg, el, mk, coef, tie, tie_sem, el_sem, mk_sem):
    rows, cols = el.shape
    chunks = cols // LANES
    size = rows // PIECES
    fetch = []
    for p in range(PIECES):
        at = pl.ds(p * size, size)
        fetch.append(
            (
                pltpu.make_async_copy(el_hbm.at[at, :], el.at[at, :], el_sem.at[p]),
                pltpu.make_async_copy(mk_hbm.at[at, :], mk.at[at, :], mk_sem.at[p]),
            )
        )
    for pair in fetch:
        for copy in pair:
            copy.start()
    tie_copy = pltpu.make_async_copy(tie_hbm, tie, tie_sem)
    tie_copy.start()
    col = iota((cols, LANES), 0) // 8
    pick = jnp.where(col == iota((cols, LANES), 1), 1.0, 0.0).astype(jnp.bfloat16)
    tie_copy.wait()
    coefficients(tie, coef)
    sums, counts = [], []
    waited = 0
    for g in range(rows // 64):
        while waited * size < 64 * (g + 1):
            for copy in fetch[waited]:
                copy.wait()
            waited += 1
        s_parts, n_parts = [], []
        for j in range(chunks):
            s_tiles, n_tiles = [], []
            for t in range(8):
                at = (slice(64 * g + 8 * t, 64 * g + 8 * t + 8), slice(LANES * j, LANES * j + LANES))
                m = mk[at].astype(jnp.float32)
                n_tiles.append(m)
                s_tiles.append(m * el[at])
            s_parts.append(block_rows(s_tiles))
            n_parts.append(block_rows(n_tiles))
        sums.append(jnp.concatenate(s_parts, axis=1))
        counts.append(jnp.concatenate(n_parts, axis=1))
    s = jnp.concatenate(sums, axis=0)
    n = jnp.concatenate(counts, axis=0)
    hi = s.astype(jnp.bfloat16)
    rest = s - hi.astype(jnp.float32)
    mid = rest.astype(jnp.bfloat16)
    low = (rest - mid.astype(jnp.float32)).astype(jnp.bfloat16)
    left = jnp.concatenate([hi, mid, low, n.astype(jnp.bfloat16)], axis=0)
    out = lax.dot_general(left, pick, (((1,), (0,)), ((), ())), preferred_element_type=jnp.float32)
    k = rows // 8
    summed = out[0:k] + (out[k : 2 * k] + out[2 * k : 3 * k])
    count = out[3 * k : 4 * k]
    msg[0:k, :] = summed / (count + 1.0)
    msg[k : 2 * k, :] = count * (1.0 / 64.0)
    first = jnp.transpose(el[:, 0:LANES])
    last = jnp.transpose(el[:, cols - LANES : cols])
    msg[2 * k : 2 * k + 4, :] = first[0:4]
    msg[2 * k + 4 : 2 * k + 8, :] = last[LANES - 4 : LANES]


def row_message_kernel(own, from_a, from_b, el, after, coarse, side, to_n, to_f):
    k = (own.shape[0] - 8) // 2
    rows, cols = el.shape
    chunks = cols // LANES
    r, c = lax.axis_index("rows"), lax.axis_index("cols")
    count = lax.axis_size("cols")
    even = c % 2 == 0
    shape = own.shape
    a, b = from_a[...], from_b[...]
    line = iota(shape, 0)
    missing = jnp.where((line >= k) & (line < 2 * k), 0.0, OUTSIDE)
    right = jnp.where(jnp.full(shape, c == count - 1), missing, jnp.where(jnp.full(shape, even), a, b))
    left = jnp.where(jnp.full(shape, c == 0), missing, jnp.where(jnp.full(shape, even), b, a))
    lane = iota((2 * k, LANES), 1)
    near = jnp.where(lane < LANES // 2, right[0 : 2 * k], left[0 : 2 * k])
    mine = own[...]
    c4 = (mine[0:k], near[0:k], mine[k : 2 * k], near[k : 2 * k])
    for i, part in enumerate(c4):
        coarse[i * k : (i + 1) * k, :] = part
        to_n[i * k : (i + 1) * k, :] = part
        to_f[i * k : (i + 1) * k, :] = part
    cols_t = jnp.concatenate(
        [right[2 * k : 2 * k + 4], jnp.zeros((LANES - 8, LANES), jnp.float32), left[2 * k + 4 : 2 * k + 8]], axis=0
    )
    beyond = jnp.transpose(cols_t)
    side[...] = beyond
    upper = r % 2 == 0
    for j in range(chunks + 1):
        if j < chunks:
            lanes = slice(LANES * j, LANES * j + LANES)
            top, bottom = el[0:2, lanes], el[rows - 2 : rows, lanes]
        else:
            top, bottom = beyond[0:2], beyond[rows - 2 : rows]
        cond = jnp.full((2, LANES), upper)
        to_n[4 * k + 2 * j : 4 * k + 2 * j + 2, :] = jnp.where(cond, bottom, top)
        to_f[4 * k + 2 * j : 4 * k + 2 * j + 2, :] = jnp.where(cond, top, bottom)


def middle_kernel(coefs, el, out, recip, zc, zw, ze, rc, rw, re):
    rows, cols = el.shape
    chunks = cols // LANES
    coef = coefficient_tiles(coefs)
    z_planes, r_planes = (zc, zw, ze), (rc, rw, re)
    inner, core = range(1, chunks - 1), range(2, chunks - 2)
    blank = jnp.zeros((8, LANES), jnp.float32)
    for at in (0, rows + 8):
        for j in inner:
            for ref in z_planes + r_planes:
                ref[j, at : at + 8, :] = blank

    for t in range(rows // 8):
        row = 8 + 8 * t
        for j in range(chunks):
            zc[j, pl.ds(row, 8), :] = el[pl.ds(8 * t, 8), LANES * j : LANES * j + LANES]
        spread(z_planes, inner, row)

    for t in range(rows // 8):
        row = 8 + 8 * t
        for j in inner:
            total = reciprocal_total(z_planes, j, row, coef)
            rc[j, pl.ds(row, 8), :] = total
            recip[j - 1, pl.ds(8 * t, 8), :] = total
        spread(r_planes, core, row)

    for t in range(rows // 8):
        row = 8 + 8 * t
        for j in core:
            for i, field in enumerate(fields(z_planes, r_planes, j, row, coef)):
                out[i, j - 2, pl.ds(8 * t, 8), :] = field


def outer_kernel(coefs, el, side, known, out, recip, zc, zw, ze, rc, rw, re):
    rows, cols = el.shape
    chunks = cols // LANES
    coef = coefficient_tiles(coefs)
    z_planes, r_planes = (zc, zw, ze), (rc, rw, re)
    order = (chunks - 3, chunks - 2, chunks - 1, chunks, 0, 1, 2)
    blank = jnp.zeros((8, LANES), jnp.float32)
    for at in (0, rows + 8):
        for i in range(1, 6):
            for ref in z_planes + r_planes:
                ref[i, at : at + 8, :] = blank

    for t in range(rows // 8):
        row = 8 + 8 * t
        at = pl.ds(8 * t, 8)
        for i, j in enumerate(order):
            zc[i, pl.ds(row, 8), :] = el[at, LANES * j : LANES * j + LANES] if j < chunks else side[at, :]
        spread(z_planes, range(1, 6), row)

    for t in range(rows // 8):
        row = 8 + 8 * t
        at = pl.ds(8 * t, 8)
        for i, j in enumerate(order):
            if i in (2, 3, 4):
                total = reciprocal_total(z_planes, i, row, coef)
                recip[i - 2, at, :] = total
            else:
                total = known[j - 1, at, :]
            rc[i, pl.ds(row, 8), :] = total
        spread(r_planes, (1, 2, 4, 5), row)

    for t in range(rows // 8):
        row = 8 + 8 * t
        for n, i in enumerate((4, 5, 1, 2)):
            for which, field in enumerate(fields(z_planes, r_planes, i, row, coef)):
                out[which, n, pl.ds(8 * t, 8), :] = field


def inflow_kernel(
    coefs, coarse, from_n, from_f, el, side, middle, outer, middle_recip, outer_recip, mk, out_hbm,
    kc, kw, ke, sc, sw, se, run, gain, flow, zc, zw, ze, rc, rw, re, up_ref, vv_ref, out, out_sem,
):
    k = coarse.shape[0] // 4
    rows, cols = mk.shape
    chunks = cols // LANES
    r, count = lax.axis_index("rows"), lax.axis_size("rows")
    upper = r % 2 == 0
    coef = coefficient_tiles(coefs)
    n, f = from_n[...], from_f[...]
    shape = n.shape
    line = iota(shape, 0)
    missing = jnp.where((line >= 2 * k) & (line < 4 * k), 0.0, OUTSIDE)
    cond = jnp.full(shape, upper)
    above = jnp.where(jnp.full(shape, r == 0), missing, jnp.where(cond, f, n))
    below = jnp.where(jnp.full(shape, r == count - 1), missing, jnp.where(cond, n, f))

    k_planes, s_planes = (kc, kw, ke), (sc, sw, se)
    around = lambda size: (lambda j: j % size)
    for j in range(2):
        kc[j, 0:8, :] = jnp.zeros((8, LANES), jnp.float32)
        kc[j, 8 + 3 * k : 16 + 3 * k, :] = jnp.zeros((8, LANES), jnp.float32)
        for ref, base, first in ((kc, 0, 8), (run, 2 * k, 0)):
            lo = base + j * k
            ref[j, first : first + k, :] = above[lo : lo + k]
            ref[j, first + k : first + 2 * k, :] = coarse[lo : lo + k, :]
            ref[j, first + 2 * k : first + 3 * k, :] = below[lo : lo + k]
    for t in range(3 * k // 8 + 2):
        spread(k_planes, range(2), 8 * t, around(2))
    recip = {}
    for j in range(2):
        for t in range(3 * k // 8):
            recip[j, t] = reciprocal_total(k_planes, j, 8 + 8 * t, coef)
    inner = range(1, 3 * k // 8 - 1)
    for j in range(2):
        for t in inner:
            for d in range(8):
                gain[d, j, 8 * t : 8 * t + 8, :] = inward(k_planes, j, 8 + 8 * t, d, coef)

    z_planes, r_planes = (zc, zw, ze), (rc, rw, re)
    ring = around(chunks + 1)
    every = range(chunks + 1)
    for j in every:
        up2, down2 = above[4 * k + 2 * j : 4 * k + 2 * j + 2], below[4 * k + 2 * j : 4 * k + 2 * j + 2]
        if j < chunks:
            first, last = el[0:8, LANES * j : LANES * j + LANES], el[rows - 8 : rows, LANES * j : LANES * j + LANES]
        else:
            first, last = side[0:8, :], side[rows - 8 : rows, :]
        blank = jnp.zeros((8, LANES), jnp.float32)
        for at in (0, 16, 32):
            zc[j, at : at + 8, :] = blank
        zc[j, 8:16, :] = jnp.concatenate([up2, first[0:2], last[6:8], down2], axis=0)
        zc[j, 24:32, :] = jnp.concatenate([up2[1:2], first[0:3], last[5:8], down2[0:1]], axis=0)
    for row in (0, 8, 16, 24, 32):
        spread(z_planes, every, row, ring)
    for j in every:
        total = reciprocal_total(z_planes, j, 8, coef)
        if 1 <= j < chunks - 1:
            near = middle_recip.at[j - 1]
        else:
            near = outer_recip.at[{chunks - 1: 0, chunks: 1, 0: 2}[j]]
        first, last = near[0:8, :], near[rows - 8 : rows, :]
        for at in (0, 16):
            rc[j, at : at + 8, :] = jnp.zeros((8, LANES), jnp.float32)
        rc[j, 8:16, :] = jnp.concatenate([total[1:3], first[1:3], last[5:7], total[5:7]], axis=0)
    for row in (0, 8, 16):
        spread(r_planes, every, row, ring)
    border = {}
    for j in range(chunks):
        border[j] = fields((zc.at[:, 16:40, :], zw.at[:, 16:40, :], ze.at[:, 16:40, :]), r_planes, j, 8, coef, 1, 6)

    for j in range(2):
        for t in range(3 * k // 8):
            sc[j, 8 * t : 8 * t + 8, :] = recip[j, t] * run[j, 8 * t : 8 * t + 8, :]
    for t in range(3 * k // 8):
        spread(s_planes, range(2), 8 * t, around(2))
    for sweep in range(ITERS):
        for j in range(2):
            for t in inner:
                parts = [gain[d, j, 8 * t : 8 * t + 8, :] * neighbour(s_planes, j, 8 * t, d) for d in range(8)]
                total = ((parts[0] + parts[1]) + (parts[2] + parts[3])) + (
                    (parts[4] + parts[5]) + (parts[6] + parts[7])
                )
                flow[j, 8 * t : 8 * t + 8, :] = run[j, 8 * t : 8 * t + 8, :] + total
        if sweep < ITERS - 1:
            for j in range(2):
                for t in inner:
                    sc[j, 8 * t : 8 * t + 8, :] = recip[j, t] * flow[j, 8 * t : 8 * t + 8, :]
            for t in inner:
                spread(s_planes, range(2), 8 * t, around(2))

    lane = iota((8, LANES), 1)
    block = lane // 8
    step = jnp.where(lane % 8 == 7, 1, jnp.where(lane % 8 == 0, -1, 0))
    per = LANES // 8
    for t in inner:
        main = flow[0, 8 * t : 8 * t + 8, :]
        apart = flow[1, 8 * t : 8 * t + 8, :]
        for j in range(chunks):
            here = block + per * j
            over = here + step
            up_ref[j, 8 * t : 8 * t + 8, :] = jnp.take_along_axis(main, here, axis=1, mode="promise_in_bounds")
            v = jnp.take_along_axis(main, over & (LANES - 1), axis=1, mode="promise_in_bounds")
            if j == 0:
                far = jnp.take_along_axis(apart, over & (LANES - 1), axis=1, mode="promise_in_bounds")
                v = jnp.where(lane == 0, far, v)
            if j == chunks - 1:
                far = jnp.take_along_axis(apart, over & (LANES - 1), axis=1, mode="promise_in_bounds")
                v = jnp.where(lane == LANES - 1, far, v)
            vv_ref[j, 8 * t : 8 * t + 8, :] = v

    sub = iota((8, LANES), 0)
    high = sub < 4
    writes = []
    for b in range(rows // 8):
        for j in range(chunks):
            lanes = slice(LANES * j, LANES * j + LANES)
            at = slice(8 * b, 8 * b + 8)
            row = k + b
            wide = [jnp.broadcast_to(up_ref[j, row + i : row + i + 1, :], (8, LANES)) for i in (-1, 0, 1)]
            apart = [jnp.broadcast_to(vv_ref[j, row + i : row + i + 1, :], (8, LANES)) for i in (-1, 0, 1)]
            if 2 <= j < chunks - 2:
                a = [middle[i, j - 2, at, :] for i in range(4)]
            else:
                a = [outer[i, j if j < 2 else j - chunks + 4, at, :] for i in range(4)]
            if b == 0:
                a = [jnp.where(sub < 2, pltpu.roll(border[j][i], 7, 0), a[i]) for i in range(4)]
            if b == rows // 8 - 1:
                a = [jnp.where(sub > 5, pltpu.roll(border[j][i], 1, 0), a[i]) for i in range(4)]
            out[at, lanes] = mk[at, lanes].astype(jnp.float32) + (
                (a[0] * wide[1] + a[1] * apart[1])
                + (a[2] * jnp.where(high, wide[0], wide[2]) + a[3] * jnp.where(high, apart[0], apart[2]))
            )
        size = rows // PARTS
        if (8 * b + 8) % size == 0:
            p = 8 * b // size
            lines = pl.ds(p * size, size)
            copy = pltpu.make_async_copy(out.at[lines, :], out_hbm.at[lines, :], out_sem.at[p])
            copy.start()
            writes.append(copy)
    for copy in writes:
        copy.wait()


def swap(x, axis, far):
    count = lax.axis_size(axis)
    if far:
        pairs = [(i, (i + 1) % count if i % 2 else (i - 1) % count) for i in range(count)]
    else:
        pairs = [(i, i ^ 1) for i in range(count)]
    return lax.ppermute(x, axis, pairs)


def f32(*shape):
    return jax.ShapeDtypeStruct(shape, jnp.float32)


def whole(count):
    return [pl.BlockSpec(memory_space=VMEM)] * count


def on_device(elevation, data_mask, tie_order):
    rows, cols = elevation.shape
    k, chunks = rows // 8, cols // LANES
    params = pltpu.CompilerParams(vmem_limit_bytes=LIMIT)
    dma = pltpu.SemaphoreType.DMA
    hbm = pl.BlockSpec(memory_space=pltpu.HBM)
    msg, el, mk, coefs = pl.pallas_call(
        overview_kernel,
        out_shape=[f32(2 * k + 8, LANES), f32(rows, cols), jax.ShapeDtypeStruct((rows, cols), jnp.int32), f32(8, LANES)],
        in_specs=[hbm] * 3,
        out_specs=whole(4),
        scratch_shapes=[pltpu.SMEM((8,), jnp.int32), dma, dma((PIECES,)), dma((PIECES,))],
        compiler_params=params,
        name="overview",
    )(*(pltpu.with_memory_space_constraint(x, pltpu.HBM) for x in (tie_order, elevation, data_mask)))
    from_b = swap(msg, "cols", True)
    from_a = swap(msg, "cols", False)
    plane = lambda count, height: VMEM((count, height, LANES), jnp.float32)
    cost = pl.CostEstimate(flops=10_000_000, bytes_accessed=3_000_000, transcendentals=0)
    middle, middle_recip = pl.pallas_call(
        middle_kernel,
        out_shape=[f32(4, chunks - 4, rows, LANES), f32(chunks - 2, rows, LANES)],
        in_specs=whole(2),
        out_specs=whole(2),
        scratch_shapes=[plane(chunks, rows + 16)] * 6,
        compiler_params=params,
        cost_estimate=cost,
        name="middle_fields",
    )(coefs, el)
    size = 4 * k + 24
    coarse, side, to_n, to_f = pl.pallas_call(
        row_message_kernel,
        out_shape=[f32(4 * k, LANES), f32(rows, LANES), f32(size, LANES), f32(size, LANES)],
        in_specs=whole(5),
        out_specs=whole(4),
        compiler_params=params,
        name="row_message",
    )(msg, from_a, from_b, el, middle_recip)
    from_n = swap(to_n, "rows", False)
    from_f = swap(to_f, "rows", True)
    outer, outer_recip = pl.pallas_call(
        outer_kernel,
        out_shape=[f32(4, 4, rows, LANES), f32(3, rows, LANES)],
        in_specs=whole(4),
        out_specs=whole(2),
        scratch_shapes=[plane(7, rows + 16)] * 6,
        compiler_params=params,
        cost_estimate=cost,
        name="outer_fields",
    )(coefs, el, side, middle_recip)
    return pl.pallas_call(
        inflow_kernel,
        out_shape=f32(rows, cols),
        in_specs=whole(11),
        out_specs=hbm,
        scratch_shapes=[plane(2, 3 * k + 16)] * 3
        + [plane(2, 3 * k)] * 4
        + [VMEM((8, 2, 3 * k, LANES), jnp.float32), plane(2, 3 * k)]
        + [plane(chunks + 1, 40)] * 3
        + [plane(chunks + 1, 24)] * 3
        + [plane(chunks, 3 * k)] * 2
        + [VMEM((rows, cols), jnp.float32), dma((PARTS,))],
        compiler_params=params,
        name="inflow",
    )(coefs, coarse, from_n, from_f, el, side, middle, outer, middle_recip, outer_recip, mk)


def solution(mesh):
    in_specs = (P("rows", "cols"), P("rows", "cols"), P())
    out_specs = P("rows", "cols")
    return jax.shard_map(
        on_device, mesh=mesh, in_specs=in_specs, out_specs=out_specs, check_vma=False
    )
```

```python
import jax
import jax.numpy as jnp
from jax import lax
from jax.experimental import pallas as pl
from jax.experimental.pallas import tpu as pltpu
from jax.sharding import PartitionSpec as P

ITERS = 8
OFFSETS = ((0, 1), (1, 1), (1, 0), (1, -1), (0, -1), (-1, -1), (-1, 0), (-1, 1))
DIAGONAL = 0.7071067811865476
RETENTION = 0.1
OUTSIDE = 1e30
LANES = 128
VMEM = pltpu.VMEM
LIMIT = 40 * 1024 * 1024


def iota(shape, dim):
    return lax.broadcasted_iota(jnp.int32, shape, dim)


def coefficients(tie_ref, coef_ref):
    for place in range(8):
        k = tie_ref[place]
        value = 1.0 + 0.5 * (7.0 - place) / 7.0
        scaled = jnp.where(k % 2 == 0, value, value * DIAGONAL).astype(jnp.float32)
        coef_ref[pl.ds(k, 1), :] = jnp.full((1, LANES), scaled)


def coefficient_tiles(coef_ref):
    return [jnp.broadcast_to(coef_ref[k : k + 1, :], (8, LANES)) for k in range(8)]


def neighbour(planes, j, row, k):
    step_row, step_col = OFFSETS[k]
    ref = planes[{0: 0, -1: 1, 1: 2}[step_col]]
    return ref[j, pl.ds(row + step_row, 8), :]


def spread(planes, wanted, row, ring=None):
    centre, west, east = planes
    lane = iota((8, LANES), 1)
    at = pl.ds(row, 8)
    ring = ring or (lambda j: j)
    to_east, to_west = {}, {}
    for j in wanted:
        for i in (ring(j - 1), j):
            if i not in to_east:
                to_east[i] = pltpu.roll(centre[i, at, :], 1, 1)
        for i in (j, ring(j + 1)):
            if i not in to_west:
                to_west[i] = pltpu.roll(centre[i, at, :], LANES - 1, 1)
        west[j, at, :] = jnp.where(lane == 0, to_east[ring(j - 1)], to_east[j])
        east[j, at, :] = jnp.where(lane == LANES - 1, to_west[ring(j + 1)], to_west[j])


def reciprocal_total(planes, j, row, coef):
    z = planes[0][j, pl.ds(row, 8), :]
    parts = [coef[k] * jnp.maximum(z - neighbour(planes, j, row, k), 0.0) for k in range(8)]
    total = ((parts[0] + parts[1]) + (parts[2] + parts[3])) + ((parts[4] + parts[5]) + (parts[6] + parts[7]))
    return 1.0 / (total + RETENTION)


def inward(planes, j, row, k, coef):
    z = planes[0][j, pl.ds(row, 8), :]
    return coef[(k + 4) % 8] * jnp.maximum(neighbour(planes, j, row, k) - z, 0.0)


def fields(z_planes, r_planes, j, row, coef, top=0, bottom=7):
    lane = iota((8, LANES), 1) % 8
    sub = iota((8, LANES), 0)
    at_east, at_west = lane == 7, lane == 0
    first, last = sub == top, sub == bottom
    t = [inward(z_planes, j, row, k, coef) * neighbour(r_planes, j, row, k) for k in range(8)]

    def split(east, west):
        own = jnp.where(at_east, west, jnp.where(at_west, east, east + west))
        other = jnp.where(at_east, east, jnp.where(at_west, west, 0.0))
        return own, other

    own0, other0 = split(t[0], t[4])
    own_down, other_down = split(t[1], t[3])
    own_down = own_down + t[2]
    own_up, other_up = split(t[7], t[5])
    own_up = own_up + t[6]
    a00 = own0 + jnp.where(first, 0.0, own_up) + jnp.where(last, 0.0, own_down)
    a01 = other0 + jnp.where(first, 0.0, other_up) + jnp.where(last, 0.0, other_down)
    a10 = jnp.where(first, own_up, jnp.where(last, own_down, 0.0))
    a11 = jnp.where(first, other_up, jnp.where(last, other_down, 0.0))
    return a00, a01, a10, a11


def block_rows(tiles):
    sub = iota(tiles[0].shape, 0)
    level = [tiles[t] for t in (0, 4, 2, 6, 1, 5, 3, 7)]
    for shift in (4, 2, 1):
        low = (sub & shift) == 0
        level = [
            jnp.where(low, a + pltpu.roll(a, 8 - shift, 0), b + pltpu.roll(b, shift, 0))
            for a, b in zip(level[0::2], level[1::2])
        ]
    return level[0]


PIECES = 8
PARTS = 4


def overview_kernel(tie_hbm, el_hbm, mk_hbm, msg, el, mk, coef, tie, tie_sem, el_sem, mk_sem):
    rows, cols = el.shape
    chunks = cols // LANES
    size = rows // PIECES
    fetch = []
    for p in range(PIECES):
        at = pl.ds(p * size, size)
        fetch.append(
            (
                pltpu.make_async_copy(el_hbm.at[at, :], el.at[at, :], el_sem.at[p]),
                pltpu.make_async_copy(mk_hbm.at[at, :], mk.at[at, :], mk_sem.at[p]),
            )
        )
    for pair in fetch:
        for copy in pair:
            copy.start()
    tie_copy = pltpu.make_async_copy(tie_hbm, tie, tie_sem)
    tie_copy.start()
    col = iota((cols, LANES), 0) // 8
    pick = jnp.where(col == iota((cols, LANES), 1), 1.0, 0.0).astype(jnp.bfloat16)
    tie_copy.wait()
    coefficients(tie, coef)
    sums, counts = [], []
    waited = 0
    for g in range(rows // 64):
        while waited * size < 64 * (g + 1):
            for copy in fetch[waited]:
                copy.wait()
            waited += 1
        s_parts, n_parts = [], []
        for j in range(chunks):
            s_tiles, n_tiles = [], []
            for t in range(8):
                at = (slice(64 * g + 8 * t, 64 * g + 8 * t + 8), slice(LANES * j, LANES * j + LANES))
                m = mk[at].astype(jnp.float32)
                n_tiles.append(m)
                s_tiles.append(m * el[at])
            s_parts.append(block_rows(s_tiles))
            n_parts.append(block_rows(n_tiles))
        sums.append(jnp.concatenate(s_parts, axis=1))
        counts.append(jnp.concatenate(n_parts, axis=1))
    s = jnp.concatenate(sums, axis=0)
    n = jnp.concatenate(counts, axis=0)
    hi = s.astype(jnp.bfloat16)
    rest = s - hi.astype(jnp.float32)
    mid = rest.astype(jnp.bfloat16)
    low = (rest - mid.astype(jnp.float32)).astype(jnp.bfloat16)
    left = jnp.concatenate([hi, mid, low, n.astype(jnp.bfloat16)], axis=0)
    out = lax.dot_general(left, pick, (((1,), (0,)), ((), ())), preferred_element_type=jnp.float32)
    k = rows // 8
    summed = out[0:k] + (out[k : 2 * k] + out[2 * k : 3 * k])
    count = out[3 * k : 4 * k]
    msg[0:k, :] = summed / (count + 1.0)
    msg[k : 2 * k, :] = count * (1.0 / 64.0)
    first = jnp.transpose(el[:, 0:LANES])
    last = jnp.transpose(el[:, cols - LANES : cols])
    msg[2 * k : 2 * k + 4, :] = first[0:4]
    msg[2 * k + 4 : 2 * k + 8, :] = last[LANES - 4 : LANES]


def row_message_kernel(own, from_a, from_b, el, after, coarse, side, to_n, to_f):
    k = (own.shape[0] - 8) // 2
    rows, cols = el.shape
    chunks = cols // LANES
    r, c = lax.axis_index("rows"), lax.axis_index("cols")
    count = lax.axis_size("cols")
    even = c % 2 == 0
    shape = own.shape
    a, b = from_a[...], from_b[...]
    line = iota(shape, 0)
    missing = jnp.where((line >= k) & (line < 2 * k), 0.0, OUTSIDE)
    right = jnp.where(jnp.full(shape, c == count - 1), missing, jnp.where(jnp.full(shape, even), a, b))
    left = jnp.where(jnp.full(shape, c == 0), missing, jnp.where(jnp.full(shape, even), b, a))
    lane = iota((2 * k, LANES), 1)
    near = jnp.where(lane < LANES // 2, right[0 : 2 * k], left[0 : 2 * k])
    mine = own[...]
    c4 = (mine[0:k], near[0:k], mine[k : 2 * k], near[k : 2 * k])
    for i, part in enumerate(c4):
        coarse[i * k : (i + 1) * k, :] = part
        to_n[i * k : (i + 1) * k, :] = part
        to_f[i * k : (i + 1) * k, :] = part
    cols_t = jnp.concatenate(
        [right[2 * k : 2 * k + 4], jnp.zeros((LANES - 8, LANES), jnp.float32), left[2 * k + 4 : 2 * k + 8]], axis=0
    )
    beyond = jnp.transpose(cols_t)
    side[...] = beyond
    upper = r % 2 == 0
    for j in range(chunks + 1):
        if j < chunks:
            lanes = slice(LANES * j, LANES * j + LANES)
            top, bottom = el[0:2, lanes], el[rows - 2 : rows, lanes]
        else:
            top, bottom = beyond[0:2], beyond[rows - 2 : rows]
        cond = jnp.full((2, LANES), upper)
        to_n[4 * k + 2 * j : 4 * k + 2 * j + 2, :] = jnp.where(cond, bottom, top)
        to_f[4 * k + 2 * j : 4 * k + 2 * j + 2, :] = jnp.where(cond, top, bottom)


def middle_kernel(coefs, el, out, recip, zc, zw, ze, rc, rw, re):
    rows, cols = el.shape
    chunks = cols // LANES
    coef = coefficient_tiles(coefs)
    z_planes, r_planes = (zc, zw, ze), (rc, rw, re)
    inner, core = range(1, chunks - 1), range(2, chunks - 2)
    blank = jnp.zeros((8, LANES), jnp.float32)
    for at in (0, rows + 8):
        for j in inner:
            for ref in z_planes + r_planes:
                ref[j, at : at + 8, :] = blank

    for t in range(rows // 8):
        row = 8 + 8 * t
        for j in range(chunks):
            zc[j, pl.ds(row, 8), :] = el[pl.ds(8 * t, 8), LANES * j : LANES * j + LANES]
        spread(z_planes, inner, row)

    for t in range(rows // 8):
        row = 8 + 8 * t
        for j in inner:
            total = reciprocal_total(z_planes, j, row, coef)
            rc[j, pl.ds(row, 8), :] = total
            recip[j - 1, pl.ds(8 * t, 8), :] = total
        spread(r_planes, core, row)

    for t in range(rows // 8):
        row = 8 + 8 * t
        for j in core:
            for i, field in enumerate(fields(z_planes, r_planes, j, row, coef)):
                out[i, j - 2, pl.ds(8 * t, 8), :] = field


def outer_kernel(coefs, el, side, known, out, recip, zc, zw, ze, rc, rw, re):
    rows, cols = el.shape
    chunks = cols // LANES
    coef = coefficient_tiles(coefs)
    z_planes, r_planes = (zc, zw, ze), (rc, rw, re)
    order = (chunks - 3, chunks - 2, chunks - 1, chunks, 0, 1, 2)
    blank = jnp.zeros((8, LANES), jnp.float32)
    for at in (0, rows + 8):
        for i in range(1, 6):
            for ref in z_planes + r_planes:
                ref[i, at : at + 8, :] = blank

    for t in range(rows // 8):
        row = 8 + 8 * t
        at = pl.ds(8 * t, 8)
        for i, j in enumerate(order):
            zc[i, pl.ds(row, 8), :] = el[at, LANES * j : LANES * j + LANES] if j < chunks else side[at, :]
        spread(z_planes, range(1, 6), row)

    for t in range(rows // 8):
        row = 8 + 8 * t
        at = pl.ds(8 * t, 8)
        for i, j in enumerate(order):
            if i in (2, 3, 4):
                total = reciprocal_total(z_planes, i, row, coef)
                recip[i - 2, at, :] = total
            else:
                total = known[j - 1, at, :]
            rc[i, pl.ds(row, 8), :] = total
        spread(r_planes, (1, 2, 4, 5), row)

    for t in range(rows // 8):
        row = 8 + 8 * t
        for n, i in enumerate((4, 5, 1, 2)):
            for which, field in enumerate(fields(z_planes, r_planes, i, row, coef)):
                out[which, n, pl.ds(8 * t, 8), :] = field


def inflow_kernel(
    coefs, coarse, from_n, from_f, el, side, middle, outer, middle_recip, outer_recip, mk, out_hbm,
    kc, kw, ke, sc, sw, se, run, gain, flow, zc, zw, ze, rc, rw, re, up_ref, vv_ref, out, out_sem,
):
    k = coarse.shape[0] // 4
    rows, cols = mk.shape
    chunks = cols // LANES
    r, count = lax.axis_index("rows"), lax.axis_size("rows")
    upper = r % 2 == 0
    coef = coefficient_tiles(coefs)
    n, f = from_n[...], from_f[...]
    shape = n.shape
    line = iota(shape, 0)
    missing = jnp.where((line >= 2 * k) & (line < 4 * k), 0.0, OUTSIDE)
    cond = jnp.full(shape, upper)
    above = jnp.where(jnp.full(shape, r == 0), missing, jnp.where(cond, f, n))
    below = jnp.where(jnp.full(shape, r == count - 1), missing, jnp.where(cond, n, f))

    k_planes, s_planes = (kc, kw, ke), (sc, sw, se)
    around = lambda size: (lambda j: j % size)
    for j in range(2):
        kc[j, 0:8, :] = jnp.zeros((8, LANES), jnp.float32)
        kc[j, 8 + 3 * k : 16 + 3 * k, :] = jnp.zeros((8, LANES), jnp.float32)
        for ref, base, first in ((kc, 0, 8), (run, 2 * k, 0)):
            lo = base + j * k
            ref[j, first : first + k, :] = above[lo : lo + k]
            ref[j, first + k : first + 2 * k, :] = coarse[lo : lo + k, :]
            ref[j, first + 2 * k : first + 3 * k, :] = below[lo : lo + k]
    for t in range(3 * k // 8 + 2):
        spread(k_planes, range(2), 8 * t, around(2))
    recip = {}
    for j in range(2):
        for t in range(3 * k // 8):
            recip[j, t] = reciprocal_total(k_planes, j, 8 + 8 * t, coef)
    inner = range(1, 3 * k // 8 - 1)
    for j in range(2):
        for t in inner:
            for d in range(8):
                gain[d, j, 8 * t : 8 * t + 8, :] = inward(k_planes, j, 8 + 8 * t, d, coef)

    z_planes, r_planes = (zc, zw, ze), (rc, rw, re)
    ring = around(chunks + 1)
    every = range(chunks + 1)
    for j in every:
        up2, down2 = above[4 * k + 2 * j : 4 * k + 2 * j + 2], below[4 * k + 2 * j : 4 * k + 2 * j + 2]
        if j < chunks:
            first, last = el[0:8, LANES * j : LANES * j + LANES], el[rows - 8 : rows, LANES * j : LANES * j + LANES]
        else:
            first, last = side[0:8, :], side[rows - 8 : rows, :]
        blank = jnp.zeros((8, LANES), jnp.float32)
        for at in (0, 16, 32):
            zc[j, at : at + 8, :] = blank
        zc[j, 8:16, :] = jnp.concatenate([up2, first[0:2], last[6:8], down2], axis=0)
        zc[j, 24:32, :] = jnp.concatenate([up2[1:2], first[0:3], last[5:8], down2[0:1]], axis=0)
    for row in (0, 8, 16, 24, 32):
        spread(z_planes, every, row, ring)
    for j in every:
        total = reciprocal_total(z_planes, j, 8, coef)
        if 1 <= j < chunks - 1:
            near = middle_recip.at[j - 1]
        else:
            near = outer_recip.at[{chunks - 1: 0, chunks: 1, 0: 2}[j]]
        first, last = near[0:8, :], near[rows - 8 : rows, :]
        for at in (0, 16):
            rc[j, at : at + 8, :] = jnp.zeros((8, LANES), jnp.float32)
        rc[j, 8:16, :] = jnp.concatenate([total[1:3], first[1:3], last[5:7], total[5:7]], axis=0)
    for row in (0, 8, 16):
        spread(r_planes, every, row, ring)
    border = {}
    for j in range(chunks):
        border[j] = fields((zc.at[:, 16:40, :], zw.at[:, 16:40, :], ze.at[:, 16:40, :]), r_planes, j, 8, coef, 1, 6)

    for j in range(2):
        for t in range(3 * k // 8):
            sc[j, 8 * t : 8 * t + 8, :] = recip[j, t] * run[j, 8 * t : 8 * t + 8, :]
    for t in range(3 * k // 8):
        spread(s_planes, range(2), 8 * t, around(2))
    for sweep in range(ITERS):
        for j in range(2):
            for t in inner:
                parts = [gain[d, j, 8 * t : 8 * t + 8, :] * neighbour(s_planes, j, 8 * t, d) for d in range(8)]
                total = ((parts[0] + parts[1]) + (parts[2] + parts[3])) + (
                    (parts[4] + parts[5]) + (parts[6] + parts[7])
                )
                flow[j, 8 * t : 8 * t + 8, :] = run[j, 8 * t : 8 * t + 8, :] + total
        if sweep < ITERS - 1:
            for j in range(2):
                for t in inner:
                    sc[j, 8 * t : 8 * t + 8, :] = recip[j, t] * flow[j, 8 * t : 8 * t + 8, :]
            for t in inner:
                spread(s_planes, range(2), 8 * t, around(2))

    lane = iota((8, LANES), 1)
    block = lane // 8
    step = jnp.where(lane % 8 == 7, 1, jnp.where(lane % 8 == 0, -1, 0))
    per = LANES // 8
    for t in inner:
        main = flow[0, 8 * t : 8 * t + 8, :]
        apart = flow[1, 8 * t : 8 * t + 8, :]
        for j in range(chunks):
            here = block + per * j
            over = here + step
            up_ref[j, 8 * t : 8 * t + 8, :] = jnp.take_along_axis(main, here, axis=1, mode="promise_in_bounds")
            v = jnp.take_along_axis(main, over & (LANES - 1), axis=1, mode="promise_in_bounds")
            if j == 0:
                far = jnp.take_along_axis(apart, over & (LANES - 1), axis=1, mode="promise_in_bounds")
                v = jnp.where(lane == 0, far, v)
            if j == chunks - 1:
                far = jnp.take_along_axis(apart, over & (LANES - 1), axis=1, mode="promise_in_bounds")
                v = jnp.where(lane == LANES - 1, far, v)
            vv_ref[j, 8 * t : 8 * t + 8, :] = v

    sub = iota((8, LANES), 0)
    high = sub < 4
    writes = []
    for b in range(rows // 8):
        for j in range(chunks):
            lanes = slice(LANES * j, LANES * j + LANES)
            at = slice(8 * b, 8 * b + 8)
            row = k + b
            wide = [jnp.broadcast_to(up_ref[j, row + i : row + i + 1, :], (8, LANES)) for i in (-1, 0, 1)]
            apart = [jnp.broadcast_to(vv_ref[j, row + i : row + i + 1, :], (8, LANES)) for i in (-1, 0, 1)]
            if 2 <= j < chunks - 2:
                a = [middle[i, j - 2, at, :] for i in range(4)]
            else:
                a = [outer[i, j if j < 2 else j - chunks + 4, at, :] for i in range(4)]
            if b == 0:
                a = [jnp.where(sub < 2, pltpu.roll(border[j][i], 7, 0), a[i]) for i in range(4)]
            if b == rows // 8 - 1:
                a = [jnp.where(sub > 5, pltpu.roll(border[j][i], 1, 0), a[i]) for i in range(4)]
            out[at, lanes] = mk[at, lanes].astype(jnp.float32) + (
                (a[0] * wide[1] + a[1] * apart[1])
                + (a[2] * jnp.where(high, wide[0], wide[2]) + a[3] * jnp.where(high, apart[0], apart[2]))
            )
        size = rows // PARTS
        if (8 * b + 8) % size == 0:
            p = 8 * b // size
            lines = pl.ds(p * size, size)
            copy = pltpu.make_async_copy(out.at[lines, :], out_hbm.at[lines, :], out_sem.at[p])
            copy.start()
            writes.append(copy)
    for copy in writes:
        copy.wait()


def swap(x, axis, far):
    sizes = {name: lax.axis_size(name) for name in ("rows", "cols")}
    pairs = []
    for r in range(sizes["rows"]):
        for c in range(sizes["cols"]):
            to = {"rows": r, "cols": c}
            i = to[axis]
            partner = i ^ 1 if not far else i + 1 if i % 2 else i - 1
            if 0 <= partner < sizes[axis]:
                to[axis] = partner
            else:
                other = "cols" if axis == "rows" else "rows"
                to[other] ^= 1
            pairs.append((r * sizes["cols"] + c, to["rows"] * sizes["cols"] + to["cols"]))
    return lax.ppermute(x, ("rows", "cols"), pairs)


def f32(*shape):
    return jax.ShapeDtypeStruct(shape, jnp.float32)


def whole(count):
    return [pl.BlockSpec(memory_space=VMEM)] * count


def on_device(elevation, data_mask, tie_order):
    rows, cols = elevation.shape
    k, chunks = rows // 8, cols // LANES
    params = pltpu.CompilerParams(vmem_limit_bytes=LIMIT)
    dma = pltpu.SemaphoreType.DMA
    hbm = pl.BlockSpec(memory_space=pltpu.HBM)
    msg, el, mk, coefs = pl.pallas_call(
        overview_kernel,
        out_shape=[f32(2 * k + 8, LANES), f32(rows, cols), jax.ShapeDtypeStruct((rows, cols), jnp.int32), f32(8, LANES)],
        in_specs=[hbm] * 3,
        out_specs=whole(4),
        scratch_shapes=[pltpu.SMEM((8,), jnp.int32), dma, dma((PIECES,)), dma((PIECES,))],
        compiler_params=params,
        name="overview",
    )(*(pltpu.with_memory_space_constraint(x, pltpu.HBM) for x in (tie_order, elevation, data_mask)))
    from_b = swap(msg, "cols", True)
    from_a = swap(msg, "cols", False)
    plane = lambda count, height: VMEM((count, height, LANES), jnp.float32)
    cost = pl.CostEstimate(flops=10_000_000, bytes_accessed=3_000_000, transcendentals=0)
    middle, middle_recip = pl.pallas_call(
        middle_kernel,
        out_shape=[f32(4, chunks - 4, rows, LANES), f32(chunks - 2, rows, LANES)],
        in_specs=whole(2),
        out_specs=whole(2),
        scratch_shapes=[plane(chunks, rows + 16)] * 6,
        compiler_params=params,
        cost_estimate=cost,
        name="middle_fields",
    )(coefs, el)
    size = 4 * k + 24
    coarse, side, to_n, to_f = pl.pallas_call(
        row_message_kernel,
        out_shape=[f32(4 * k, LANES), f32(rows, LANES), f32(size, LANES), f32(size, LANES)],
        in_specs=whole(5),
        out_specs=whole(4),
        compiler_params=params,
        name="row_message",
    )(msg, from_a, from_b, el, middle_recip)
    from_n = swap(to_n, "rows", False)
    from_f = swap(to_f, "rows", True)
    outer, outer_recip = pl.pallas_call(
        outer_kernel,
        out_shape=[f32(4, 4, rows, LANES), f32(3, rows, LANES)],
        in_specs=whole(4),
        out_specs=whole(2),
        scratch_shapes=[plane(7, rows + 16)] * 6,
        compiler_params=params,
        cost_estimate=cost,
        name="outer_fields",
    )(coefs, el, side, middle_recip)
    return pl.pallas_call(
        inflow_kernel,
        out_shape=f32(rows, cols),
        in_specs=whole(11),
        out_specs=hbm,
        scratch_shapes=[plane(2, 3 * k + 16)] * 3
        + [plane(2, 3 * k)] * 4
        + [VMEM((8, 2, 3 * k, LANES), jnp.float32), plane(2, 3 * k)]
        + [plane(chunks + 1, 40)] * 3
        + [plane(chunks + 1, 24)] * 3
        + [plane(chunks, 3 * k)] * 2
        + [VMEM((rows, cols), jnp.float32), dma((PARTS,))],
        compiler_params=params,
        name="inflow",
    )(coefs, coarse, from_n, from_f, el, side, middle, outer, middle_recip, outer_recip, mk)


def solution(mesh):
    in_specs = (P("rows", "cols"), P("rows", "cols"), P())
    out_specs = P("rows", "cols")
    return jax.shard_map(
        on_device, mesh=mesh, in_specs=in_specs, out_specs=out_specs, check_vma=False
    )
```

```python
import jax
import jax.numpy as jnp
from jax import lax
from jax.experimental import pallas as pl
from jax.experimental.pallas import tpu as pltpu
from jax.sharding import PartitionSpec as P

ITERS = 8
OFFSETS = ((0, 1), (1, 1), (1, 0), (1, -1), (0, -1), (-1, -1), (-1, 0), (-1, 1))
DIAGONAL = 0.7071067811865476
RETENTION = 0.1
OUTSIDE = 1e30
LANES = 128
VMEM = pltpu.VMEM
LIMIT = 40 * 1024 * 1024


def iota(shape, dim):
    return lax.broadcasted_iota(jnp.int32, shape, dim)


def coefficients(tie_ref, coef_ref):
    for place in range(8):
        k = tie_ref[place]
        value = 1.0 + 0.5 * (7.0 - place) / 7.0
        scaled = jnp.where(k % 2 == 0, value, value * DIAGONAL).astype(jnp.float32)
        coef_ref[pl.ds(k, 1), :] = jnp.full((1, LANES), scaled)


def coefficient_tiles(coef_ref):
    return [jnp.broadcast_to(coef_ref[k : k + 1, :], (8, LANES)) for k in range(8)]


def neighbour(planes, j, row, k):
    step_row, step_col = OFFSETS[k]
    ref = planes[{0: 0, -1: 1, 1: 2}[step_col]]
    return ref[j, pl.ds(row + step_row, 8), :]


def spread(planes, wanted, row, ring=None):
    centre, west, east = planes
    lane = iota((8, LANES), 1)
    at = pl.ds(row, 8)
    ring = ring or (lambda j: j)
    to_east, to_west = {}, {}
    for j in wanted:
        for i in (ring(j - 1), j):
            if i not in to_east:
                to_east[i] = pltpu.roll(centre[i, at, :], 1, 1)
        for i in (j, ring(j + 1)):
            if i not in to_west:
                to_west[i] = pltpu.roll(centre[i, at, :], LANES - 1, 1)
        west[j, at, :] = jnp.where(lane == 0, to_east[ring(j - 1)], to_east[j])
        east[j, at, :] = jnp.where(lane == LANES - 1, to_west[ring(j + 1)], to_west[j])


def reciprocal_total(planes, j, row, coef):
    z = planes[0][j, pl.ds(row, 8), :]
    parts = [coef[k] * jnp.maximum(z - neighbour(planes, j, row, k), 0.0) for k in range(8)]
    total = ((parts[0] + parts[1]) + (parts[2] + parts[3])) + ((parts[4] + parts[5]) + (parts[6] + parts[7]))
    return 1.0 / (total + RETENTION)


def inward(planes, j, row, k, coef):
    z = planes[0][j, pl.ds(row, 8), :]
    return coef[(k + 4) % 8] * jnp.maximum(neighbour(planes, j, row, k) - z, 0.0)


def fields(z_planes, r_planes, j, row, coef, top=0, bottom=7):
    lane = iota((8, LANES), 1) % 8
    sub = iota((8, LANES), 0)
    at_east, at_west = lane == 7, lane == 0
    first, last = sub == top, sub == bottom
    t = [inward(z_planes, j, row, k, coef) * neighbour(r_planes, j, row, k) for k in range(8)]

    def split(east, west):
        own = jnp.where(at_east, west, jnp.where(at_west, east, east + west))
        other = jnp.where(at_east, east, jnp.where(at_west, west, 0.0))
        return own, other

    own0, other0 = split(t[0], t[4])
    own_down, other_down = split(t[1], t[3])
    own_down = own_down + t[2]
    own_up, other_up = split(t[7], t[5])
    own_up = own_up + t[6]
    a00 = own0 + jnp.where(first, 0.0, own_up) + jnp.where(last, 0.0, own_down)
    a01 = other0 + jnp.where(first, 0.0, other_up) + jnp.where(last, 0.0, other_down)
    a10 = jnp.where(first, own_up, jnp.where(last, own_down, 0.0))
    a11 = jnp.where(first, other_up, jnp.where(last, other_down, 0.0))
    return a00, a01, a10, a11


def block_rows(tiles):
    sub = iota(tiles[0].shape, 0)
    level = [tiles[t] for t in (0, 4, 2, 6, 1, 5, 3, 7)]
    for shift in (4, 2, 1):
        low = (sub & shift) == 0
        level = [
            jnp.where(low, a + pltpu.roll(a, 8 - shift, 0), b + pltpu.roll(b, shift, 0))
            for a, b in zip(level[0::2], level[1::2])
        ]
    return level[0]


DEPTH = ITERS + 2
PIECES = 4
PARTS = 4


def edges(overview, runoff):
    lane = iota(overview.shape, 1)
    outer = (lane < DEPTH) | (lane >= LANES - DEPTH)
    return jnp.where(outer, overview, pltpu.roll(runoff, LANES // 2, 1))


def overview_kernel(tie_hbm, el_hbm, mk_hbm, msg, own, el, mk, coef, tie, tie_sem, el_sem, mk_sem):
    rows, cols = el.shape
    chunks = cols // LANES
    k = rows // 8
    per = chunks // PIECES
    pieces = [0, PIECES - 1, *range(1, PIECES - 1)]
    fetch = []
    for p in pieces:
        at = pl.ds(p * per * LANES, per * LANES)
        pair = (
            pltpu.make_async_copy(el_hbm.at[:, at], el.at[:, at], el_sem.at[p]),
            pltpu.make_async_copy(mk_hbm.at[:, at], mk.at[:, at], mk_sem.at[p]),
        )
        for copy in pair:
            copy.start()
        fetch.append(pair)
    tie_copy = pltpu.make_async_copy(tie_hbm, tie, tie_sem)
    tie_copy.start()
    col = iota((cols, LANES), 0) // 8
    pick = jnp.where(col == iota((cols, LANES), 1), 1.0, 0.0).astype(jnp.bfloat16)
    tie_copy.wait()
    coefficients(tie, coef)
    sums, counts = {}, {}
    for p, pair in zip(pieces, fetch):
        for copy in pair:
            copy.wait()
        for j in range(p * per, (p + 1) * per):
            lanes = slice(LANES * j, LANES * j + LANES)
            s_groups, n_groups = [], []
            for g in range(rows // 64):
                at = [(slice(64 * g + 8 * t, 64 * g + 8 * t + 8), lanes) for t in range(8)]
                flags = [mk[i].astype(jnp.float32) for i in at]
                n_groups.append(block_rows(flags))
                s_groups.append(block_rows([m * el[i] for m, i in zip(flags, at)]))
            sums[j] = jnp.concatenate(s_groups, axis=0)
            counts[j] = jnp.concatenate(n_groups, axis=0)
            if j == 0:
                msg[k : k + 4, :] = jnp.transpose(el[:, lanes])[0:4]
            if j == chunks - 1:
                msg[k + 4 : k + 8, :] = jnp.transpose(el[:, lanes])[LANES - 4 : LANES]
    s = jnp.concatenate([sums[j] for j in range(chunks)], axis=1)
    n = jnp.concatenate([counts[j] for j in range(chunks)], axis=1)
    hi = s.astype(jnp.bfloat16)
    rest = s - hi.astype(jnp.float32)
    mid = rest.astype(jnp.bfloat16)
    low = (rest - mid.astype(jnp.float32)).astype(jnp.bfloat16)
    left = jnp.concatenate([hi, mid, low, n.astype(jnp.bfloat16)], axis=0)
    out = lax.dot_general(left, pick, (((1,), (0,)), ((), ())), preferred_element_type=jnp.float32)
    summed = out[0:k] + (out[k : 2 * k] + out[2 * k : 3 * k])
    count = out[3 * k : 4 * k]
    overview, runoff = summed / (count + 1.0), count * (1.0 / 64.0)
    msg[0:k, :] = edges(overview, runoff)
    own[0:k, :] = overview
    own[k : 2 * k, :] = runoff


def row_message_kernel(own, from_a, from_b, el, after, coarse, side, to_n, to_f):
    k = own.shape[0] // 2
    rows, cols = el.shape
    chunks = cols // LANES
    r, c = lax.axis_index("rows"), lax.axis_index("cols")
    count = lax.axis_size("cols")
    even = jnp.full((k + 8, LANES), c % 2 == 0)
    a, b = from_a[...], from_b[...]
    right, left = jnp.where(even, a, b), jnp.where(even, b, a)
    lane = iota((k, LANES), 1)
    east = lane < LANES // 2
    gone_east, gone_west = jnp.full((k, LANES), c == count - 1), jnp.full((k, LANES), c == 0)
    gone = (east & gone_east) | (~east & gone_west)
    near = jnp.where(gone, OUTSIDE, jnp.where(east, right[0:k], left[0:k]))
    near_run = pltpu.roll(jnp.where(east, left[0:k], right[0:k]), LANES // 2, 1)
    near_run = jnp.where(gone, 0.0, near_run)
    over, run = own[0:k, :], own[k : 2 * k, :]
    for i, part in enumerate((over, near, run, near_run)):
        coarse[i * k : (i + 1) * k, :] = part
    columns = jnp.concatenate(
        [
            jnp.where(jnp.full((4, LANES), c == count - 1), OUTSIDE, right[k : k + 4]),
            jnp.zeros((LANES - 8, LANES), jnp.float32),
            jnp.where(jnp.full((4, LANES), c == 0), OUTSIDE, left[k + 4 : k + 8]),
        ],
        axis=0,
    )
    beyond = jnp.transpose(columns)
    side[...] = beyond
    upper = r % 2 == 0
    packed = edges(near, near_run)
    turned = pltpu.roll(jnp.concatenate([beyond[0:8], beyond[rows - 8 : rows]], axis=0), LANES // 4, 1)
    ends = (turned[0:2], turned[14:16])
    lane2 = iota((2, LANES), 1)
    quarter = (lane2 >= LANES // 4 - 2) & (lane2 < LANES // 4 + 2)

    def put(at, top, bottom):
        cond = jnp.full(top.shape, upper)
        to_n[at : at + top.shape[0], :] = jnp.where(cond, bottom, top)
        to_f[at : at + top.shape[0], :] = jnp.where(cond, top, bottom)

    for i, part in enumerate((over, run, packed)):
        put(i * DEPTH, part[0:DEPTH], part[k - DEPTH : k])
    for j in range(chunks):
        lanes = slice(LANES * j, LANES * j + LANES)
        put(3 * DEPTH + 2 * j, el[0:2, lanes], el[rows - 2 : rows, lanes])
    put(
        2 * DEPTH,
        jnp.where(quarter, ends[0], packed[0:2]),
        jnp.where(quarter, ends[1], packed[k - DEPTH : k - DEPTH + 2]),
    )


def middle_kernel(coefs, el, out, recip, zc, zw, ze, rc, rw, re):
    rows, cols = el.shape
    chunks = cols // LANES
    coef = coefficient_tiles(coefs)
    z_planes, r_planes = (zc, zw, ze), (rc, rw, re)
    inner, core = range(1, chunks - 1), range(2, chunks - 2)
    blank = jnp.zeros((8, LANES), jnp.float32)
    for at in (0, rows + 8):
        for j in inner:
            for ref in z_planes + r_planes:
                ref[j, at : at + 8, :] = blank

    for t in range(rows // 8):
        row = 8 + 8 * t
        for j in range(chunks):
            zc[j, pl.ds(row, 8), :] = el[pl.ds(8 * t, 8), LANES * j : LANES * j + LANES]
        spread(z_planes, inner, row)

    for t in range(rows // 8):
        row = 8 + 8 * t
        for j in inner:
            total = reciprocal_total(z_planes, j, row, coef)
            rc[j, pl.ds(row, 8), :] = total
            recip[j - 1, pl.ds(8 * t, 8), :] = total
        spread(r_planes, core, row)

    for t in range(rows // 8):
        row = 8 + 8 * t
        for j in core:
            for i, field in enumerate(fields(z_planes, r_planes, j, row, coef)):
                out[i, j - 2, pl.ds(8 * t, 8), :] = field


def outer_kernel(coefs, el, side, known, out, recip, zc, zw, ze, rc, rw, re):
    rows, cols = el.shape
    chunks = cols // LANES
    coef = coefficient_tiles(coefs)
    z_planes, r_planes = (zc, zw, ze), (rc, rw, re)
    order = (chunks - 3, chunks - 2, chunks - 1, chunks, 0, 1, 2)
    blank = jnp.zeros((8, LANES), jnp.float32)
    for at in (0, rows + 8):
        for i in range(1, 6):
            for ref in z_planes + r_planes:
                ref[i, at : at + 8, :] = blank

    for t in range(rows // 8):
        row = 8 + 8 * t
        at = pl.ds(8 * t, 8)
        for i, j in enumerate(order):
            zc[i, pl.ds(row, 8), :] = el[at, LANES * j : LANES * j + LANES] if j < chunks else side[at, :]
        spread(z_planes, range(1, 6), row)

    for t in range(rows // 8):
        row = 8 + 8 * t
        at = pl.ds(8 * t, 8)
        for i, j in enumerate(order):
            if i in (2, 3, 4):
                total = reciprocal_total(z_planes, i, row, coef)
                recip[i - 2, at, :] = total
            else:
                total = known[j - 1, at, :]
            rc[i, pl.ds(row, 8), :] = total
        spread(r_planes, (1, 2, 4, 5), row)

    for t in range(rows // 8):
        row = 8 + 8 * t
        for n, i in enumerate((4, 5, 1, 2)):
            for which, field in enumerate(fields(z_planes, r_planes, i, row, coef)):
                out[which, n, pl.ds(8 * t, 8), :] = field


def inflow_kernel(
    coefs, coarse, from_n, from_f, el, side, middle, outer, middle_recip, outer_recip, mk, out_hbm,
    kc, kw, ke, sc, sw, se, run, gain, flow, zc, zw, ze, rc, rw, re, up_ref, vv_ref, out, out_sem,
):
    k = coarse.shape[0] // 4
    rows, cols = mk.shape
    chunks = cols // LANES
    r, count = lax.axis_index("rows"), lax.axis_size("rows")
    upper = r % 2 == 0
    coef = coefficient_tiles(coefs)
    n, f = from_n[...], from_f[...]
    cond = jnp.full(n.shape, upper)

    def unpack(x, gone):
        rest = lambda part, value: jnp.where(jnp.full(part.shape, gone), value, part)
        packed = x[2 * DEPTH : 3 * DEPTH]
        parts = (
            rest(x[0:DEPTH], OUTSIDE),
            rest(packed, OUTSIDE),
            rest(x[DEPTH : 2 * DEPTH], 0.0),
            rest(pltpu.roll(jnp.concatenate([packed, x[0:6]], axis=0), LANES // 2, 1)[0:DEPTH], 0.0),
        )
        lines = rest(x[3 * DEPTH : 3 * DEPTH + 2 * chunks], OUTSIDE)
        turned = pltpu.roll(x[2 * DEPTH : 2 * DEPTH + 8], LANES - LANES // 4, 1)[0:2]
        return parts, [lines[2 * j : 2 * j + 2] for j in range(chunks)] + [rest(turned, OUTSIDE)]

    above, above_lines = unpack(jnp.where(cond, f, n), r == 0)
    below, below_lines = unpack(jnp.where(cond, n, f), r == count - 1)

    k_planes, s_planes = (kc, kw, ke), (sc, sw, se)
    around = lambda size: (lambda j: j % size)
    for j in range(2):
        for ref, base, first, total in ((kc, 0, 8, 3 * k + 16), (run, 2, 0, 3 * k)):
            ref[j, 0 : first + k, :] = jnp.zeros((first + k, LANES), jnp.float32)
            ref[j, first + 2 * k : total, :] = jnp.zeros((total - first - 2 * k, LANES), jnp.float32)
            ref[j, first + k - DEPTH : first + k, :] = above[base + j]
            ref[j, first + k : first + 2 * k, :] = coarse[(base + j) * k : (base + j + 1) * k, :]
            ref[j, first + 2 * k : first + 2 * k + DEPTH, :] = below[base + j]
    for t in range(3 * k // 8 + 2):
        spread(k_planes, range(2), 8 * t, around(2))
    recip = {}
    for j in range(2):
        for t in range(3 * k // 8):
            recip[j, t] = reciprocal_total(k_planes, j, 8 + 8 * t, coef)
    inner = range(1, 3 * k // 8 - 1)
    for j in range(2):
        for t in inner:
            for d in range(8):
                gain[d, j, 8 * t : 8 * t + 8, :] = inward(k_planes, j, 8 + 8 * t, d, coef)

    z_planes, r_planes = (zc, zw, ze), (rc, rw, re)
    ring = around(chunks + 1)
    every = range(chunks + 1)
    for j in every:
        up2, down2 = above_lines[j], below_lines[j]
        if j < chunks:
            first, last = el[0:8, LANES * j : LANES * j + LANES], el[rows - 8 : rows, LANES * j : LANES * j + LANES]
        else:
            first, last = side[0:8, :], side[rows - 8 : rows, :]
        blank = jnp.zeros((8, LANES), jnp.float32)
        for at in (0, 16, 32):
            zc[j, at : at + 8, :] = blank
        zc[j, 8:16, :] = jnp.concatenate([up2, first[0:2], last[6:8], down2], axis=0)
        zc[j, 24:32, :] = jnp.concatenate([up2[1:2], first[0:3], last[5:8], down2[0:1]], axis=0)
    for row in (0, 8, 16, 24, 32):
        spread(z_planes, every, row, ring)
    for j in every:
        total = reciprocal_total(z_planes, j, 8, coef)
        if 1 <= j < chunks - 1:
            near = middle_recip.at[j - 1]
        else:
            near = outer_recip.at[{chunks - 1: 0, chunks: 1, 0: 2}[j]]
        first, last = near[0:8, :], near[rows - 8 : rows, :]
        for at in (0, 16):
            rc[j, at : at + 8, :] = jnp.zeros((8, LANES), jnp.float32)
        rc[j, 8:16, :] = jnp.concatenate([total[1:3], first[1:3], last[5:7], total[5:7]], axis=0)
    for row in (0, 8, 16):
        spread(r_planes, every, row, ring)
    border = {}
    for j in range(chunks):
        border[j] = fields((zc.at[:, 16:40, :], zw.at[:, 16:40, :], ze.at[:, 16:40, :]), r_planes, j, 8, coef, 1, 6)

    for j in range(2):
        for t in range(3 * k // 8):
            sc[j, 8 * t : 8 * t + 8, :] = recip[j, t] * run[j, 8 * t : 8 * t + 8, :]
    for t in range(3 * k // 8):
        spread(s_planes, range(2), 8 * t, around(2))
    for sweep in range(ITERS):
        for j in range(2):
            for t in inner:
                parts = [gain[d, j, 8 * t : 8 * t + 8, :] * neighbour(s_planes, j, 8 * t, d) for d in range(8)]
                total = ((parts[0] + parts[1]) + (parts[2] + parts[3])) + (
                    (parts[4] + parts[5]) + (parts[6] + parts[7])
                )
                flow[j, 8 * t : 8 * t + 8, :] = run[j, 8 * t : 8 * t + 8, :] + total
        if sweep < ITERS - 1:
            for j in range(2):
                for t in inner:
                    sc[j, 8 * t : 8 * t + 8, :] = recip[j, t] * flow[j, 8 * t : 8 * t + 8, :]
            for t in inner:
                spread(s_planes, range(2), 8 * t, around(2))

    lane = iota((8, LANES), 1)
    block = lane // 8
    step = jnp.where(lane % 8 == 7, 1, jnp.where(lane % 8 == 0, -1, 0))
    per = LANES // 8
    for t in inner:
        main = flow[0, 8 * t : 8 * t + 8, :]
        apart = flow[1, 8 * t : 8 * t + 8, :]
        for j in range(chunks):
            here = block + per * j
            over = here + step
            up_ref[j, 8 * t : 8 * t + 8, :] = jnp.take_along_axis(main, here, axis=1, mode="promise_in_bounds")
            v = jnp.take_along_axis(main, over & (LANES - 1), axis=1, mode="promise_in_bounds")
            if j == 0:
                far = jnp.take_along_axis(apart, over & (LANES - 1), axis=1, mode="promise_in_bounds")
                v = jnp.where(lane == 0, far, v)
            if j == chunks - 1:
                far = jnp.take_along_axis(apart, over & (LANES - 1), axis=1, mode="promise_in_bounds")
                v = jnp.where(lane == LANES - 1, far, v)
            vv_ref[j, 8 * t : 8 * t + 8, :] = v

    sub = iota((8, LANES), 0)
    high = sub < 4
    writes = []
    for b in range(rows // 8):
        for j in range(chunks):
            lanes = slice(LANES * j, LANES * j + LANES)
            at = slice(8 * b, 8 * b + 8)
            row = k + b
            wide = [jnp.broadcast_to(up_ref[j, row + i : row + i + 1, :], (8, LANES)) for i in (-1, 0, 1)]
            apart = [jnp.broadcast_to(vv_ref[j, row + i : row + i + 1, :], (8, LANES)) for i in (-1, 0, 1)]
            if 2 <= j < chunks - 2:
                a = [middle[i, j - 2, at, :] for i in range(4)]
            else:
                a = [outer[i, j if j < 2 else j - chunks + 4, at, :] for i in range(4)]
            if b == 0:
                a = [jnp.where(sub < 2, pltpu.roll(border[j][i], 7, 0), a[i]) for i in range(4)]
            if b == rows // 8 - 1:
                a = [jnp.where(sub > 5, pltpu.roll(border[j][i], 1, 0), a[i]) for i in range(4)]
            out[at, lanes] = mk[at, lanes].astype(jnp.float32) + (
                (a[0] * wide[1] + a[1] * apart[1])
                + (a[2] * jnp.where(high, wide[0], wide[2]) + a[3] * jnp.where(high, apart[0], apart[2]))
            )
        size = rows // PARTS
        if (8 * b + 8) % size == 0:
            p = 8 * b // size
            lines = pl.ds(p * size, size)
            copy = pltpu.make_async_copy(out.at[lines, :], out_hbm.at[lines, :], out_sem.at[p])
            copy.start()
            writes.append(copy)
    for copy in writes:
        copy.wait()


def swap(x, axis, far):
    sizes = {name: lax.axis_size(name) for name in ("rows", "cols")}
    pairs = []
    for r in range(sizes["rows"]):
        for c in range(sizes["cols"]):
            to = {"rows": r, "cols": c}
            i = to[axis]
            partner = i ^ 1 if not far else i + 1 if i % 2 else i - 1
            if 0 <= partner < sizes[axis]:
                to[axis] = partner
            else:
                other = "cols" if axis == "rows" else "rows"
                to[other] ^= 1
            pairs.append((r * sizes["cols"] + c, to["rows"] * sizes["cols"] + to["cols"]))
    return lax.ppermute(x, ("rows", "cols"), pairs)


def f32(*shape):
    return jax.ShapeDtypeStruct(shape, jnp.float32)


def whole(count):
    return [pl.BlockSpec(memory_space=VMEM)] * count


def on_device(elevation, data_mask, tie_order):
    rows, cols = elevation.shape
    k, chunks = rows // 8, cols // LANES
    params = pltpu.CompilerParams(vmem_limit_bytes=LIMIT)
    dma = pltpu.SemaphoreType.DMA
    hbm = pl.BlockSpec(memory_space=pltpu.HBM)
    msg, own, el, mk, coefs = pl.pallas_call(
        overview_kernel,
        out_shape=[
            f32(k + 8, LANES),
            f32(2 * k, LANES),
            f32(rows, cols),
            jax.ShapeDtypeStruct((rows, cols), jnp.int32),
            f32(8, LANES),
        ],
        in_specs=[hbm] * 3,
        out_specs=whole(5),
        scratch_shapes=[pltpu.SMEM((8,), jnp.int32), dma, dma((PIECES,)), dma((PIECES,))],
        compiler_params=params,
        name="overview",
    )(*(pltpu.with_memory_space_constraint(x, pltpu.HBM) for x in (tie_order, elevation, data_mask)))
    from_b = swap(msg, "cols", True)
    from_a = swap(msg, "cols", False)
    plane = lambda count, height: VMEM((count, height, LANES), jnp.float32)
    cost = pl.CostEstimate(flops=10_000_000, bytes_accessed=3_000_000, transcendentals=0)
    middle, middle_recip = pl.pallas_call(
        middle_kernel,
        out_shape=[f32(4, chunks - 4, rows, LANES), f32(chunks - 2, rows, LANES)],
        in_specs=whole(2),
        out_specs=whole(2),
        scratch_shapes=[plane(chunks, rows + 16)] * 6,
        compiler_params=params,
        cost_estimate=cost,
        name="middle_fields",
    )(coefs, el)
    size = (3 * DEPTH + 2 * chunks + 7) // 8 * 8
    coarse, side, to_n, to_f = pl.pallas_call(
        row_message_kernel,
        out_shape=[f32(4 * k, LANES), f32(rows, LANES), f32(size, LANES), f32(size, LANES)],
        in_specs=whole(5),
        out_specs=whole(4),
        compiler_params=params,
        name="row_message",
    )(own, from_a, from_b, el, middle_recip)
    from_n = swap(to_n, "rows", False)
    from_f = swap(to_f, "rows", True)
    outer, outer_recip = pl.pallas_call(
        outer_kernel,
        out_shape=[f32(4, 4, rows, LANES), f32(3, rows, LANES)],
        in_specs=whole(4),
        out_specs=whole(2),
        scratch_shapes=[plane(7, rows + 16)] * 6,
        compiler_params=params,
        cost_estimate=cost,
        name="outer_fields",
    )(coefs, el, side, middle_recip)
    return pl.pallas_call(
        inflow_kernel,
        out_shape=f32(rows, cols),
        in_specs=whole(11),
        out_specs=hbm,
        scratch_shapes=[plane(2, 3 * k + 16)] * 3
        + [plane(2, 3 * k)] * 4
        + [VMEM((8, 2, 3 * k, LANES), jnp.float32), plane(2, 3 * k)]
        + [plane(chunks + 1, 40)] * 3
        + [plane(chunks + 1, 24)] * 3
        + [plane(chunks, 3 * k)] * 2
        + [VMEM((rows, cols), jnp.float32), dma((PARTS,))],
        compiler_params=params,
        name="inflow",
    )(coefs, coarse, from_n, from_f, el, side, middle, outer, middle_recip, outer_recip, mk)


def solution(mesh):
    in_specs = (P("rows", "cols"), P("rows", "cols"), P())
    out_specs = P("rows", "cols")
    return jax.shard_map(
        on_device, mesh=mesh, in_specs=in_specs, out_specs=out_specs, check_vma=False
    )
```

```python
import jax
import jax.numpy as jnp
from jax import lax
from jax.experimental import pallas as pl
from jax.experimental.pallas import tpu as pltpu
from jax.sharding import PartitionSpec as P

ITERS = 8
OFFSETS = ((0, 1), (1, 1), (1, 0), (1, -1), (0, -1), (-1, -1), (-1, 0), (-1, 1))
DIAGONAL = 0.7071067811865476
RETENTION = 0.1
OUTSIDE = 1e30
LANES = 128
VMEM = pltpu.VMEM
LIMIT = 40 * 1024 * 1024


def iota(shape, dim):
    return lax.broadcasted_iota(jnp.int32, shape, dim)


def coefficients(tie_ref, coef_ref):
    for place in range(8):
        k = tie_ref[place]
        value = 1.0 + 0.5 * (7.0 - place) / 7.0
        scaled = jnp.where(k % 2 == 0, value, value * DIAGONAL).astype(jnp.float32)
        coef_ref[pl.ds(k, 1), :] = jnp.full((1, LANES), scaled)


def coefficient_tiles(coef_ref):
    return [jnp.broadcast_to(coef_ref[k : k + 1, :], (8, LANES)) for k in range(8)]


def neighbour(planes, j, row, k):
    step_row, step_col = OFFSETS[k]
    ref = planes[{0: 0, -1: 1, 1: 2}[step_col]]
    return ref[j, pl.ds(row + step_row, 8), :]


def spread(planes, wanted, row, ring=None):
    centre, west, east = planes
    lane = iota((8, LANES), 1)
    at = pl.ds(row, 8)
    ring = ring or (lambda j: j)
    to_east, to_west = {}, {}
    for j in wanted:
        for i in (ring(j - 1), j):
            if i not in to_east:
                to_east[i] = pltpu.roll(centre[i, at, :], 1, 1)
        for i in (j, ring(j + 1)):
            if i not in to_west:
                to_west[i] = pltpu.roll(centre[i, at, :], LANES - 1, 1)
        west[j, at, :] = jnp.where(lane == 0, to_east[ring(j - 1)], to_east[j])
        east[j, at, :] = jnp.where(lane == LANES - 1, to_west[ring(j + 1)], to_west[j])


def reciprocal_total(planes, j, row, coef):
    z = planes[0][j, pl.ds(row, 8), :]
    parts = [coef[k] * jnp.maximum(z - neighbour(planes, j, row, k), 0.0) for k in range(8)]
    total = ((parts[0] + parts[1]) + (parts[2] + parts[3])) + ((parts[4] + parts[5]) + (parts[6] + parts[7]))
    return 1.0 / (total + RETENTION)


def inward(planes, j, row, k, coef):
    z = planes[0][j, pl.ds(row, 8), :]
    return coef[(k + 4) % 8] * jnp.maximum(neighbour(planes, j, row, k) - z, 0.0)


def fields(z_planes, r_planes, j, row, coef, top=0, bottom=7):
    lane = iota((8, LANES), 1) % 8
    sub = iota((8, LANES), 0)
    at_east, at_west = lane == 7, lane == 0
    first, last = sub == top, sub == bottom
    t = [inward(z_planes, j, row, k, coef) * neighbour(r_planes, j, row, k) for k in range(8)]

    def split(east, west):
        own = jnp.where(at_east, west, jnp.where(at_west, east, east + west))
        other = jnp.where(at_east, east, jnp.where(at_west, west, 0.0))
        return own, other

    own0, other0 = split(t[0], t[4])
    own_down, other_down = split(t[1], t[3])
    own_down = own_down + t[2]
    own_up, other_up = split(t[7], t[5])
    own_up = own_up + t[6]
    a00 = own0 + jnp.where(first, 0.0, own_up) + jnp.where(last, 0.0, own_down)
    a01 = other0 + jnp.where(first, 0.0, other_up) + jnp.where(last, 0.0, other_down)
    a10 = jnp.where(first, own_up, jnp.where(last, own_down, 0.0))
    a11 = jnp.where(first, other_up, jnp.where(last, other_down, 0.0))
    return a00, a01, a10, a11


def block_rows(tiles):
    sub = iota(tiles[0].shape, 0)
    level = [tiles[t] for t in (0, 4, 2, 6, 1, 5, 3, 7)]
    for shift in (4, 2, 1):
        low = (sub & shift) == 0
        level = [
            jnp.where(low, a + pltpu.roll(a, 8 - shift, 0), b + pltpu.roll(b, shift, 0))
            for a, b in zip(level[0::2], level[1::2])
        ]
    return level[0]


DEPTH = ITERS + 2
PIECES = 4
PARTS = 4


def edges(overview, runoff):
    lane = iota(overview.shape, 1)
    outer = (lane < DEPTH) | (lane >= LANES - DEPTH)
    return jnp.where(outer, overview, pltpu.roll(runoff, LANES // 2, 1))


def overview_kernel(tie_hbm, el_hbm, mk_hbm, msg, own, el, mk, coef, tie, tie_sem, el_sem, mk_sem):
    rows, cols = el.shape
    chunks = cols // LANES
    k = rows // 8
    per = chunks // PIECES
    pieces = [0, PIECES - 1, *range(1, PIECES - 1)]
    fetch = []
    for p in pieces:
        at = pl.ds(p * per * LANES, per * LANES)
        pair = (
            pltpu.make_async_copy(el_hbm.at[:, at], el.at[:, at], el_sem.at[p]),
            pltpu.make_async_copy(mk_hbm.at[:, at], mk.at[:, at], mk_sem.at[p]),
        )
        for copy in pair:
            copy.start()
        fetch.append(pair)
    tie_copy = pltpu.make_async_copy(tie_hbm, tie, tie_sem)
    tie_copy.start()
    col = iota((cols, LANES), 0) // 8
    pick = jnp.where(col == iota((cols, LANES), 1), 1.0, 0.0).astype(jnp.bfloat16)
    tie_copy.wait()
    coefficients(tie, coef)
    sums, counts = {}, {}
    for p, pair in zip(pieces, fetch):
        for copy in pair:
            copy.wait()
        for j in range(p * per, (p + 1) * per):
            lanes = slice(LANES * j, LANES * j + LANES)
            s_groups, n_groups = [], []
            for g in range(rows // 64):
                at = [(slice(64 * g + 8 * t, 64 * g + 8 * t + 8), lanes) for t in range(8)]
                flags = [mk[i].astype(jnp.float32) for i in at]
                n_groups.append(block_rows(flags))
                s_groups.append(block_rows([m * el[i] for m, i in zip(flags, at)]))
            sums[j] = jnp.concatenate(s_groups, axis=0)
            counts[j] = jnp.concatenate(n_groups, axis=0)
            if j == 0:
                msg[k : k + 4, :] = jnp.transpose(el[:, lanes])[0:4]
            if j == chunks - 1:
                msg[k + 4 : k + 8, :] = jnp.transpose(el[:, lanes])[LANES - 4 : LANES]
    s = jnp.concatenate([sums[j] for j in range(chunks)], axis=1)
    n = jnp.concatenate([counts[j] for j in range(chunks)], axis=1)
    hi = s.astype(jnp.bfloat16)
    rest = s - hi.astype(jnp.float32)
    mid = rest.astype(jnp.bfloat16)
    low = (rest - mid.astype(jnp.float32)).astype(jnp.bfloat16)
    left = jnp.concatenate([hi, mid, low, n.astype(jnp.bfloat16)], axis=0)
    out = lax.dot_general(left, pick, (((1,), (0,)), ((), ())), preferred_element_type=jnp.float32)
    summed = out[0:k] + (out[k : 2 * k] + out[2 * k : 3 * k])
    count = out[3 * k : 4 * k]
    overview, runoff = summed / (count + 1.0), count * (1.0 / 64.0)
    msg[0:k, :] = edges(overview, runoff)
    own[0:k, :] = overview
    own[k : 2 * k, :] = runoff


def row_message_kernel(own, from_a, from_b, el, after, coarse, side, to_f):
    k = own.shape[0] // 2
    r, c = lax.axis_index("rows"), lax.axis_index("cols")
    count = lax.axis_size("cols")
    even = jnp.full((k + 8, LANES), c % 2 == 0)
    a, b = from_a[...], from_b[...]
    right, left = jnp.where(even, a, b), jnp.where(even, b, a)
    lane = iota((k, LANES), 1)
    east = lane < LANES // 2
    gone_east, gone_west = jnp.full((k, LANES), c == count - 1), jnp.full((k, LANES), c == 0)
    gone = (east & gone_east) | (~east & gone_west)
    near = jnp.where(gone, OUTSIDE, jnp.where(east, right[0:k], left[0:k]))
    near_run = pltpu.roll(jnp.where(east, left[0:k], right[0:k]), LANES // 2, 1)
    near_run = jnp.where(gone, 0.0, near_run)
    over, run = own[0:k, :], own[k : 2 * k, :]
    for i, part in enumerate((over, near, run, near_run)):
        coarse[i * k : (i + 1) * k, :] = part
    columns = jnp.concatenate(
        [
            jnp.where(jnp.full((4, LANES), c == count - 1), OUTSIDE, right[k : k + 4]),
            jnp.zeros((LANES - 8, LANES), jnp.float32),
            jnp.where(jnp.full((4, LANES), c == 0), OUTSIDE, left[k + 4 : k + 8]),
        ],
        axis=0,
    )
    beyond = jnp.transpose(columns)
    side[...] = beyond
    message((over, run, edges(near, near_run)), beyond, el, r % 2 == 1, to_f)


def message(parts, beyond, el, lower, out):
    rows, cols = el.shape
    k = parts[0].shape[0]
    turned = pltpu.roll(jnp.concatenate([beyond[0:8], beyond[rows - 8 : rows]], axis=0), LANES // 4, 1)
    lane2 = iota((2, LANES), 1)
    quarter = (lane2 >= LANES // 4 - 2) & (lane2 < LANES // 4 + 2)

    def put(at, top, bottom):
        out[at : at + top.shape[0], :] = jnp.where(jnp.full(top.shape, lower), bottom, top)

    for i, part in enumerate(parts):
        put(i * DEPTH, part[0:DEPTH], part[k - DEPTH : k])
    for j in range(cols // LANES):
        lanes = slice(LANES * j, LANES * j + LANES)
        put(3 * DEPTH + 2 * j, el[0:2, lanes], el[rows - 2 : rows, lanes])
    packed = parts[2]
    put(
        2 * DEPTH,
        jnp.where(quarter, turned[0:2], packed[0:2]),
        jnp.where(quarter, turned[14:16], packed[k - DEPTH : k - DEPTH + 2]),
    )


def near_message_kernel(coarse, side, el, after, to_n):
    k = coarse.shape[0] // 4
    over, near, run, near_run = (coarse[i * k : (i + 1) * k, :] for i in range(4))
    message((over, run, edges(near, near_run)), side[...], el, lax.axis_index("rows") % 2 == 0, to_n)


def middle_kernel(coefs, el, out, recip, zc, zw, ze, rc, rw, re):
    rows, cols = el.shape
    chunks = cols // LANES
    coef = coefficient_tiles(coefs)
    z_planes, r_planes = (zc, zw, ze), (rc, rw, re)
    inner, core = range(1, chunks - 1), range(2, chunks - 2)
    blank = jnp.zeros((8, LANES), jnp.float32)
    for at in (0, rows + 8):
        for j in inner:
            for ref in z_planes + r_planes:
                ref[j, at : at + 8, :] = blank

    for t in range(rows // 8):
        row = 8 + 8 * t
        for j in range(chunks):
            zc[j, pl.ds(row, 8), :] = el[pl.ds(8 * t, 8), LANES * j : LANES * j + LANES]
        spread(z_planes, inner, row)

    for t in range(rows // 8):
        row = 8 + 8 * t
        for j in inner:
            total = reciprocal_total(z_planes, j, row, coef)
            rc[j, pl.ds(row, 8), :] = total
            recip[j - 1, pl.ds(8 * t, 8), :] = total
        spread(r_planes, core, row)

    for t in range(rows // 8):
        row = 8 + 8 * t
        for j in core:
            for i, field in enumerate(fields(z_planes, r_planes, j, row, coef)):
                out[i, j - 2, pl.ds(8 * t, 8), :] = field


def outer_kernel(coefs, el, side, known, out, recip, zc, zw, ze, rc, rw, re):
    rows, cols = el.shape
    chunks = cols // LANES
    coef = coefficient_tiles(coefs)
    z_planes, r_planes = (zc, zw, ze), (rc, rw, re)
    order = (chunks - 3, chunks - 2, chunks - 1, chunks, 0, 1, 2)
    blank = jnp.zeros((8, LANES), jnp.float32)
    for at in (0, rows + 8):
        for i in range(1, 6):
            for ref in z_planes + r_planes:
                ref[i, at : at + 8, :] = blank

    for t in range(rows // 8):
        row = 8 + 8 * t
        at = pl.ds(8 * t, 8)
        for i, j in enumerate(order):
            zc[i, pl.ds(row, 8), :] = el[at, LANES * j : LANES * j + LANES] if j < chunks else side[at, :]
        spread(z_planes, range(1, 6), row)

    for t in range(rows // 8):
        row = 8 + 8 * t
        at = pl.ds(8 * t, 8)
        for i, j in enumerate(order):
            if i in (2, 3, 4):
                total = reciprocal_total(z_planes, i, row, coef)
                recip[i - 2, at, :] = total
            else:
                total = known[j - 1, at, :]
            rc[i, pl.ds(row, 8), :] = total
        spread(r_planes, (1, 2, 4, 5), row)

    for t in range(rows // 8):
        row = 8 + 8 * t
        for n, i in enumerate((4, 5, 1, 2)):
            for which, field in enumerate(fields(z_planes, r_planes, i, row, coef)):
                out[which, n, pl.ds(8 * t, 8), :] = field


def inflow_kernel(
    coefs, coarse, from_n, from_f, el, side, middle, outer, middle_recip, outer_recip, mk, out_hbm,
    kc, kw, ke, sc, sw, se, run, gain, flow, zc, zw, ze, rc, rw, re, up_ref, vv_ref, out, out_sem,
):
    k = coarse.shape[0] // 4
    rows, cols = mk.shape
    chunks = cols // LANES
    r, count = lax.axis_index("rows"), lax.axis_size("rows")
    upper = r % 2 == 0
    coef = coefficient_tiles(coefs)
    n, f = from_n[...], from_f[...]
    cond = jnp.full(n.shape, upper)

    def unpack(x, gone):
        rest = lambda part, value: jnp.where(jnp.full(part.shape, gone), value, part)
        packed = x[2 * DEPTH : 3 * DEPTH]
        parts = (
            rest(x[0:DEPTH], OUTSIDE),
            rest(packed, OUTSIDE),
            rest(x[DEPTH : 2 * DEPTH], 0.0),
            rest(pltpu.roll(jnp.concatenate([packed, x[0:6]], axis=0), LANES // 2, 1)[0:DEPTH], 0.0),
        )
        lines = rest(x[3 * DEPTH : 3 * DEPTH + 2 * chunks], OUTSIDE)
        turned = pltpu.roll(x[2 * DEPTH : 2 * DEPTH + 8], LANES - LANES // 4, 1)[0:2]
        return parts, [lines[2 * j : 2 * j + 2] for j in range(chunks)] + [rest(turned, OUTSIDE)]

    above, above_lines = unpack(jnp.where(cond, f, n), r == 0)
    below, below_lines = unpack(jnp.where(cond, n, f), r == count - 1)

    k_planes, s_planes = (kc, kw, ke), (sc, sw, se)
    around = lambda size: (lambda j: j % size)
    for j in range(2):
        for ref, base, first, total in ((kc, 0, 8, 3 * k + 16), (run, 2, 0, 3 * k)):
            ref[j, 0 : first + k, :] = jnp.zeros((first + k, LANES), jnp.float32)
            ref[j, first + 2 * k : total, :] = jnp.zeros((total - first - 2 * k, LANES), jnp.float32)
            ref[j, first + k - DEPTH : first + k, :] = above[base + j]
            ref[j, first + k : first + 2 * k, :] = coarse[(base + j) * k : (base + j + 1) * k, :]
            ref[j, first + 2 * k : first + 2 * k + DEPTH, :] = below[base + j]
    for t in range(3 * k // 8 + 2):
        spread(k_planes, range(2), 8 * t, around(2))
    recip = {}
    for j in range(2):
        for t in range(3 * k // 8):
            recip[j, t] = reciprocal_total(k_planes, j, 8 + 8 * t, coef)
    inner = range(1, 3 * k // 8 - 1)
    for j in range(2):
        for t in inner:
            for d in range(8):
                gain[d, j, 8 * t : 8 * t + 8, :] = inward(k_planes, j, 8 + 8 * t, d, coef)

    z_planes, r_planes = (zc, zw, ze), (rc, rw, re)
    ring = around(chunks + 1)
    every = range(chunks + 1)
    for j in every:
        up2, down2 = above_lines[j], below_lines[j]
        if j < chunks:
            first, last = el[0:8, LANES * j : LANES * j + LANES], el[rows - 8 : rows, LANES * j : LANES * j + LANES]
        else:
            first, last = side[0:8, :], side[rows - 8 : rows, :]
        blank = jnp.zeros((8, LANES), jnp.float32)
        for at in (0, 16, 32):
            zc[j, at : at + 8, :] = blank
        zc[j, 8:16, :] = jnp.concatenate([up2, first[0:2], last[6:8], down2], axis=0)
        zc[j, 24:32, :] = jnp.concatenate([up2[1:2], first[0:3], last[5:8], down2[0:1]], axis=0)
    for row in (0, 8, 16, 24, 32):
        spread(z_planes, every, row, ring)
    for j in every:
        total = reciprocal_total(z_planes, j, 8, coef)
        if 1 <= j < chunks - 1:
            near = middle_recip.at[j - 1]
        else:
            near = outer_recip.at[{chunks - 1: 0, chunks: 1, 0: 2}[j]]
        first, last = near[0:8, :], near[rows - 8 : rows, :]
        for at in (0, 16):
            rc[j, at : at + 8, :] = jnp.zeros((8, LANES), jnp.float32)
        rc[j, 8:16, :] = jnp.concatenate([total[1:3], first[1:3], last[5:7], total[5:7]], axis=0)
    for row in (0, 8, 16):
        spread(r_planes, every, row, ring)
    border = {}
    for j in range(chunks):
        border[j] = fields((zc.at[:, 16:40, :], zw.at[:, 16:40, :], ze.at[:, 16:40, :]), r_planes, j, 8, coef, 1, 6)

    for j in range(2):
        for t in range(3 * k // 8):
            sc[j, 8 * t : 8 * t + 8, :] = recip[j, t] * run[j, 8 * t : 8 * t + 8, :]
    for t in range(3 * k // 8):
        spread(s_planes, range(2), 8 * t, around(2))
    for sweep in range(ITERS):
        for j in range(2):
            for t in inner:
                parts = [gain[d, j, 8 * t : 8 * t + 8, :] * neighbour(s_planes, j, 8 * t, d) for d in range(8)]
                total = ((parts[0] + parts[1]) + (parts[2] + parts[3])) + (
                    (parts[4] + parts[5]) + (parts[6] + parts[7])
                )
                flow[j, 8 * t : 8 * t + 8, :] = run[j, 8 * t : 8 * t + 8, :] + total
        if sweep < ITERS - 1:
            for j in range(2):
                for t in inner:
                    sc[j, 8 * t : 8 * t + 8, :] = recip[j, t] * flow[j, 8 * t : 8 * t + 8, :]
            for t in inner:
                spread(s_planes, range(2), 8 * t, around(2))

    lane = iota((8, LANES), 1)
    block = lane // 8
    step = jnp.where(lane % 8 == 7, 1, jnp.where(lane % 8 == 0, -1, 0))
    per = LANES // 8
    for t in inner:
        main = flow[0, 8 * t : 8 * t + 8, :]
        apart = flow[1, 8 * t : 8 * t + 8, :]
        for j in range(chunks):
            here = block + per * j
            over = here + step
            up_ref[j, 8 * t : 8 * t + 8, :] = jnp.take_along_axis(main, here, axis=1, mode="promise_in_bounds")
            v = jnp.take_along_axis(main, over & (LANES - 1), axis=1, mode="promise_in_bounds")
            if j == 0:
                far = jnp.take_along_axis(apart, over & (LANES - 1), axis=1, mode="promise_in_bounds")
                v = jnp.where(lane == 0, far, v)
            if j == chunks - 1:
                far = jnp.take_along_axis(apart, over & (LANES - 1), axis=1, mode="promise_in_bounds")
                v = jnp.where(lane == LANES - 1, far, v)
            vv_ref[j, 8 * t : 8 * t + 8, :] = v

    sub = iota((8, LANES), 0)
    high = sub < 4
    writes = []
    for b in range(rows // 8):
        for j in range(chunks):
            lanes = slice(LANES * j, LANES * j + LANES)
            at = slice(8 * b, 8 * b + 8)
            row = k + b
            wide = [jnp.broadcast_to(up_ref[j, row + i : row + i + 1, :], (8, LANES)) for i in (-1, 0, 1)]
            apart = [jnp.broadcast_to(vv_ref[j, row + i : row + i + 1, :], (8, LANES)) for i in (-1, 0, 1)]
            if 2 <= j < chunks - 2:
                a = [middle[i, j - 2, at, :] for i in range(4)]
            else:
                a = [outer[i, j if j < 2 else j - chunks + 4, at, :] for i in range(4)]
            if b == 0:
                a = [jnp.where(sub < 2, pltpu.roll(border[j][i], 7, 0), a[i]) for i in range(4)]
            if b == rows // 8 - 1:
                a = [jnp.where(sub > 5, pltpu.roll(border[j][i], 1, 0), a[i]) for i in range(4)]
            out[at, lanes] = mk[at, lanes].astype(jnp.float32) + (
                (a[0] * wide[1] + a[1] * apart[1])
                + (a[2] * jnp.where(high, wide[0], wide[2]) + a[3] * jnp.where(high, apart[0], apart[2]))
            )
        size = rows // PARTS
        if (8 * b + 8) % size == 0:
            p = 8 * b // size
            lines = pl.ds(p * size, size)
            copy = pltpu.make_async_copy(out.at[lines, :], out_hbm.at[lines, :], out_sem.at[p])
            copy.start()
            writes.append(copy)
    for copy in writes:
        copy.wait()


def swap(x, axis, far):
    sizes = {name: lax.axis_size(name) for name in ("rows", "cols")}
    pairs = []
    for r in range(sizes["rows"]):
        for c in range(sizes["cols"]):
            to = {"rows": r, "cols": c}
            i = to[axis]
            partner = i ^ 1 if not far else i + 1 if i % 2 else i - 1
            if 0 <= partner < sizes[axis]:
                to[axis] = partner
            else:
                other = "cols" if axis == "rows" else "rows"
                to[other] ^= 1
            pairs.append((r * sizes["cols"] + c, to["rows"] * sizes["cols"] + to["cols"]))
    return lax.ppermute(x, ("rows", "cols"), pairs)


def f32(*shape):
    return jax.ShapeDtypeStruct(shape, jnp.float32)


def whole(count):
    return [pl.BlockSpec(memory_space=VMEM)] * count


def on_device(elevation, data_mask, tie_order):
    rows, cols = elevation.shape
    k, chunks = rows // 8, cols // LANES
    params = pltpu.CompilerParams(vmem_limit_bytes=LIMIT)
    dma = pltpu.SemaphoreType.DMA
    hbm = pl.BlockSpec(memory_space=pltpu.HBM)
    msg, own, el, mk, coefs = pl.pallas_call(
        overview_kernel,
        out_shape=[
            f32(k + 8, LANES),
            f32(2 * k, LANES),
            f32(rows, cols),
            jax.ShapeDtypeStruct((rows, cols), jnp.int32),
            f32(8, LANES),
        ],
        in_specs=[hbm] * 3,
        out_specs=whole(5),
        scratch_shapes=[pltpu.SMEM((8,), jnp.int32), dma, dma((PIECES,)), dma((PIECES,))],
        compiler_params=params,
        name="overview",
    )(*(pltpu.with_memory_space_constraint(x, pltpu.HBM) for x in (tie_order, elevation, data_mask)))
    from_b = swap(msg, "cols", True)
    from_a = swap(msg, "cols", False)
    plane = lambda count, height: VMEM((count, height, LANES), jnp.float32)
    cost = pl.CostEstimate(flops=10_000_000, bytes_accessed=3_000_000, transcendentals=0)
    middle, middle_recip = pl.pallas_call(
        middle_kernel,
        out_shape=[f32(4, chunks - 4, rows, LANES), f32(chunks - 2, rows, LANES)],
        in_specs=whole(2),
        out_specs=whole(2),
        scratch_shapes=[plane(chunks, rows + 16)] * 6,
        compiler_params=params,
        cost_estimate=cost,
        name="middle_fields",
    )(coefs, el)
    size = (3 * DEPTH + 2 * chunks + 7) // 8 * 8
    coarse, side, to_f = pl.pallas_call(
        row_message_kernel,
        out_shape=[f32(4 * k, LANES), f32(rows, LANES), f32(size, LANES)],
        in_specs=whole(5),
        out_specs=whole(3),
        compiler_params=params,
        name="far_message",
    )(own, from_a, from_b, el, middle_recip)
    from_f = swap(to_f, "rows", True)
    outer, outer_recip = pl.pallas_call(
        outer_kernel,
        out_shape=[f32(4, 4, rows, LANES), f32(3, rows, LANES)],
        in_specs=whole(4),
        out_specs=whole(2),
        scratch_shapes=[plane(7, rows + 16)] * 6,
        compiler_params=params,
        cost_estimate=cost,
        name="outer_fields",
    )(coefs, el, side, middle_recip)
    to_n = pl.pallas_call(
        near_message_kernel,
        out_shape=f32(size, LANES),
        in_specs=whole(4),
        out_specs=whole(1)[0],
        compiler_params=params,
        name="near_message",
    )(coarse, side, el, outer_recip)
    from_n = swap(to_n, "rows", False)
    return pl.pallas_call(
        inflow_kernel,
        out_shape=f32(rows, cols),
        in_specs=whole(11),
        out_specs=hbm,
        scratch_shapes=[plane(2, 3 * k + 16)] * 3
        + [plane(2, 3 * k)] * 4
        + [VMEM((8, 2, 3 * k, LANES), jnp.float32), plane(2, 3 * k)]
        + [plane(chunks + 1, 40)] * 3
        + [plane(chunks + 1, 24)] * 3
        + [plane(chunks, 3 * k)] * 2
        + [VMEM((rows, cols), jnp.float32), dma((PARTS,))],
        compiler_params=params,
        name="inflow",
    )(coefs, coarse, from_n, from_f, el, side, middle, outer, middle_recip, outer_recip, mk)


def solution(mesh):
    in_specs = (P("rows", "cols"), P("rows", "cols"), P())
    out_specs = P("rows", "cols")
    return jax.shard_map(
        on_device, mesh=mesh, in_specs=in_specs, out_specs=out_specs, check_vma=False
    )
```

```python
import jax
import jax.numpy as jnp
from jax import lax
from jax.experimental import pallas as pl
from jax.experimental.pallas import tpu as pltpu
from jax.sharding import PartitionSpec as P

ITERS = 8
OFFSETS = ((0, 1), (1, 1), (1, 0), (1, -1), (0, -1), (-1, -1), (-1, 0), (-1, 1))
DIAGONAL = 0.7071067811865476
RETENTION = 0.1
OUTSIDE = 1e30
LANES = 128
VMEM = pltpu.VMEM
LIMIT = 40 * 1024 * 1024


def iota(shape, dim):
    return lax.broadcasted_iota(jnp.int32, shape, dim)


def coefficients(tie_ref, coef_ref):
    for place in range(8):
        k = tie_ref[place]
        value = 1.0 + 0.5 * (7.0 - place) / 7.0
        scaled = jnp.where(k % 2 == 0, value, value * DIAGONAL).astype(jnp.float32)
        coef_ref[pl.ds(k, 1), :] = jnp.full((1, LANES), scaled)


def coefficient_tiles(coef_ref):
    return [jnp.broadcast_to(coef_ref[k : k + 1, :], (8, LANES)) for k in range(8)]


def neighbour(planes, j, row, k):
    step_row, step_col = OFFSETS[k]
    ref = planes[{0: 0, -1: 1, 1: 2}[step_col]]
    return ref[j, pl.ds(row + step_row, 8), :]


def spread(planes, wanted, row, ring=None):
    centre, west, east = planes
    lane = iota((8, LANES), 1)
    at = pl.ds(row, 8)
    ring = ring or (lambda j: j)
    to_east, to_west = {}, {}
    for j in wanted:
        for i in (ring(j - 1), j):
            if i not in to_east:
                to_east[i] = pltpu.roll(centre[i, at, :], 1, 1)
        for i in (j, ring(j + 1)):
            if i not in to_west:
                to_west[i] = pltpu.roll(centre[i, at, :], LANES - 1, 1)
        west[j, at, :] = jnp.where(lane == 0, to_east[ring(j - 1)], to_east[j])
        east[j, at, :] = jnp.where(lane == LANES - 1, to_west[ring(j + 1)], to_west[j])


def reciprocal_total(planes, j, row, coef):
    z = planes[0][j, pl.ds(row, 8), :]
    parts = [coef[k] * jnp.maximum(z - neighbour(planes, j, row, k), 0.0) for k in range(8)]
    total = ((parts[0] + parts[1]) + (parts[2] + parts[3])) + ((parts[4] + parts[5]) + (parts[6] + parts[7]))
    return 1.0 / (total + RETENTION)


def inward(planes, j, row, k, coef):
    z = planes[0][j, pl.ds(row, 8), :]
    return coef[(k + 4) % 8] * jnp.maximum(neighbour(planes, j, row, k) - z, 0.0)


def fields(z_planes, r_planes, j, row, coef, top=0, bottom=7):
    lane = iota((8, LANES), 1) % 8
    sub = iota((8, LANES), 0)
    at_east, at_west = lane == 7, lane == 0
    first, last = sub == top, sub == bottom
    t = [inward(z_planes, j, row, k, coef) * neighbour(r_planes, j, row, k) for k in range(8)]

    def split(east, west):
        own = jnp.where(at_east, west, jnp.where(at_west, east, east + west))
        other = jnp.where(at_east, east, jnp.where(at_west, west, 0.0))
        return own, other

    own0, other0 = split(t[0], t[4])
    own_down, other_down = split(t[1], t[3])
    own_down = own_down + t[2]
    own_up, other_up = split(t[7], t[5])
    own_up = own_up + t[6]
    a00 = own0 + jnp.where(first, 0.0, own_up) + jnp.where(last, 0.0, own_down)
    a01 = other0 + jnp.where(first, 0.0, other_up) + jnp.where(last, 0.0, other_down)
    a10 = jnp.where(first, own_up, jnp.where(last, own_down, 0.0))
    a11 = jnp.where(first, other_up, jnp.where(last, other_down, 0.0))
    return a00, a01, a10, a11


def block_rows(tiles):
    sub = iota(tiles[0].shape, 0)
    level = [tiles[t] for t in (0, 4, 2, 6, 1, 5, 3, 7)]
    for shift in (4, 2, 1):
        low = (sub & shift) == 0
        level = [
            jnp.where(low, a + pltpu.roll(a, 8 - shift, 0), b + pltpu.roll(b, shift, 0))
            for a, b in zip(level[0::2], level[1::2])
        ]
    return level[0]


DEPTH = ITERS + 2
PIECES = 2
PARTS = 4


def edges(overview, runoff):
    lane = iota(overview.shape, 1)
    outer = (lane < DEPTH) | (lane >= LANES - DEPTH)
    return jnp.where(outer, overview, pltpu.roll(runoff, LANES // 2, 1))


def chunk_sums(el, mk, lanes, rows):
    s_groups, n_groups = [], []
    for g in range(rows // 64):
        at = [(slice(64 * g + 8 * t, 64 * g + 8 * t + 8), lanes) for t in range(8)]
        flags = [mk[i].astype(jnp.float32) for i in at]
        n_groups.append(block_rows(flags))
        s_groups.append(block_rows([m * el[i] for m, i in zip(flags, at)]))
    return jnp.concatenate(s_groups, axis=0), jnp.concatenate(n_groups, axis=0)


def block_means(s, n, place):
    k = s.shape[0]
    pick = jnp.where(place == iota((s.shape[1], LANES), 1), 1.0, 0.0).astype(jnp.bfloat16)
    hi = s.astype(jnp.bfloat16)
    rest = s - hi.astype(jnp.float32)
    mid = rest.astype(jnp.bfloat16)
    low = (rest - mid.astype(jnp.float32)).astype(jnp.bfloat16)
    left = jnp.concatenate([hi, mid, low, n.astype(jnp.bfloat16)], axis=0)
    out = lax.dot_general(left, pick, (((1,), (0,)), ((), ())), preferred_element_type=jnp.float32)
    summed = out[0:k] + (out[k : 2 * k] + out[2 * k : 3 * k])
    count = out[3 * k : 4 * k]
    return summed / (count + 1.0), count * (1.0 / 64.0)


def column_message_kernel(el_hbm, mk_hbm, msg, el, mk, el_sem, mk_sem):
    rows, cols = el_hbm.shape
    k = rows // 8
    fetch = []
    for i, start in enumerate((0, cols - LANES)):
        far, near = pl.ds(start, LANES), pl.ds(i * LANES, LANES)
        fetch.append(pltpu.make_async_copy(el_hbm.at[:, far], el.at[:, near], el_sem.at[i]))
        fetch.append(pltpu.make_async_copy(mk_hbm.at[:, far], mk.at[:, near], mk_sem.at[i]))
    for copy in fetch:
        copy.start()
    for copy in fetch:
        copy.wait()
    first, last = slice(0, LANES), slice(LANES, 2 * LANES)
    (s0, n0), (s1, n1) = chunk_sums(el, mk, first, rows), chunk_sums(el, mk, last, rows)
    column = iota((2 * LANES, LANES), 0)
    place = jnp.where(column < LANES, column // 8, LANES - 2 * LANES // 8 + column // 8)
    overview, runoff = block_means(jnp.concatenate([s0, s1], axis=1), jnp.concatenate([n0, n1], axis=1), place)
    msg[0:k, :] = edges(overview, runoff)
    msg[k : k + 4, :] = jnp.transpose(el[:, first])[0:4]
    msg[k + 4 : k + 8, :] = jnp.transpose(el[:, last])[LANES - 4 : LANES]


def overview_kernel(tie_hbm, el_hbm, mk_hbm, after, own, el, mk, coef, tie, tie_sem, el_sem, mk_sem):
    rows, cols = el.shape
    chunks = cols // LANES
    k = rows // 8
    per = chunks // PIECES
    fetch = []
    for p in range(PIECES):
        at = pl.ds(p * per * LANES, per * LANES)
        pair = (
            pltpu.make_async_copy(el_hbm.at[:, at], el.at[:, at], el_sem.at[p]),
            pltpu.make_async_copy(mk_hbm.at[:, at], mk.at[:, at], mk_sem.at[p]),
        )
        for copy in pair:
            copy.start()
        fetch.append(pair)
    tie_copy = pltpu.make_async_copy(tie_hbm, tie, tie_sem)
    tie_copy.start()
    tie_copy.wait()
    coefficients(tie, coef)
    parts = []
    for p, pair in enumerate(fetch):
        for copy in pair:
            copy.wait()
        for j in range(p * per, (p + 1) * per):
            parts.append(chunk_sums(el, mk, slice(LANES * j, LANES * j + LANES), rows))
    s, n = (jnp.concatenate(x, axis=1) for x in zip(*parts))
    overview, runoff = block_means(s, n, iota((cols, LANES), 0) // 8)
    own[0:k, :] = overview
    own[k : 2 * k, :] = runoff


def row_message_kernel(own, from_a, from_b, el, after, coarse, side, to_f):
    k = own.shape[0] // 2
    r, c = lax.axis_index("rows"), lax.axis_index("cols")
    count = lax.axis_size("cols")
    even = jnp.full((k + 8, LANES), c % 2 == 0)
    a, b = from_a[...], from_b[...]
    right, left = jnp.where(even, a, b), jnp.where(even, b, a)
    lane = iota((k, LANES), 1)
    east = lane < LANES // 2
    gone_east, gone_west = jnp.full((k, LANES), c == count - 1), jnp.full((k, LANES), c == 0)
    gone = (east & gone_east) | (~east & gone_west)
    near = jnp.where(gone, OUTSIDE, jnp.where(east, right[0:k], left[0:k]))
    near_run = pltpu.roll(jnp.where(east, left[0:k], right[0:k]), LANES // 2, 1)
    near_run = jnp.where(gone, 0.0, near_run)
    over, run = own[0:k, :], own[k : 2 * k, :]
    for i, part in enumerate((over, near, run, near_run)):
        coarse[i * k : (i + 1) * k, :] = part
    columns = jnp.concatenate(
        [
            jnp.where(jnp.full((4, LANES), c == count - 1), OUTSIDE, right[k : k + 4]),
            jnp.zeros((LANES - 8, LANES), jnp.float32),
            jnp.where(jnp.full((4, LANES), c == 0), OUTSIDE, left[k + 4 : k + 8]),
        ],
        axis=0,
    )
    beyond = jnp.transpose(columns)
    side[...] = beyond
    message((over, run, edges(near, near_run)), beyond, el, r % 2 == 1, to_f)


def message(parts, beyond, el, lower, out):
    rows, cols = el.shape
    k = parts[0].shape[0]
    turned = pltpu.roll(jnp.concatenate([beyond[0:8], beyond[rows - 8 : rows]], axis=0), LANES // 4, 1)
    lane2 = iota((2, LANES), 1)
    quarter = (lane2 >= LANES // 4 - 2) & (lane2 < LANES // 4 + 2)

    def put(at, top, bottom):
        out[at : at + top.shape[0], :] = jnp.where(jnp.full(top.shape, lower), bottom, top)

    for i, part in enumerate(parts):
        put(i * DEPTH, part[0:DEPTH], part[k - DEPTH : k])
    for j in range(cols // LANES):
        lanes = slice(LANES * j, LANES * j + LANES)
        put(3 * DEPTH + 2 * j, el[0:2, lanes], el[rows - 2 : rows, lanes])
    packed = parts[2]
    put(
        2 * DEPTH,
        jnp.where(quarter, turned[0:2], packed[0:2]),
        jnp.where(quarter, turned[14:16], packed[k - DEPTH : k - DEPTH + 2]),
    )


def near_message_kernel(coarse, side, el, after, to_n):
    k = coarse.shape[0] // 4
    over, near, run, near_run = (coarse[i * k : (i + 1) * k, :] for i in range(4))
    message((over, run, edges(near, near_run)), side[...], el, lax.axis_index("rows") % 2 == 0, to_n)


def middle_kernel(coefs, el, out, recip, zc, zw, ze, rc, rw, re):
    rows, cols = el.shape
    chunks = cols // LANES
    coef = coefficient_tiles(coefs)
    z_planes, r_planes = (zc, zw, ze), (rc, rw, re)
    inner, core = range(1, chunks - 1), range(2, chunks - 2)
    blank = jnp.zeros((8, LANES), jnp.float32)
    for at in (0, rows + 8):
        for j in inner:
            for ref in z_planes + r_planes:
                ref[j, at : at + 8, :] = blank

    for t in range(rows // 8):
        row = 8 + 8 * t
        for j in range(chunks):
            zc[j, pl.ds(row, 8), :] = el[pl.ds(8 * t, 8), LANES * j : LANES * j + LANES]
        spread(z_planes, inner, row)

    for t in range(rows // 8):
        row = 8 + 8 * t
        for j in inner:
            total = reciprocal_total(z_planes, j, row, coef)
            rc[j, pl.ds(row, 8), :] = total
            recip[j - 1, pl.ds(8 * t, 8), :] = total
        spread(r_planes, core, row)

    for t in range(rows // 8):
        row = 8 + 8 * t
        for j in core:
            for i, field in enumerate(fields(z_planes, r_planes, j, row, coef)):
                out[i, j - 2, pl.ds(8 * t, 8), :] = field


def outer_kernel(coefs, el, side, known, out, recip, zc, zw, ze, rc, rw, re):
    rows, cols = el.shape
    chunks = cols // LANES
    coef = coefficient_tiles(coefs)
    z_planes, r_planes = (zc, zw, ze), (rc, rw, re)
    order = (chunks - 3, chunks - 2, chunks - 1, chunks, 0, 1, 2)
    blank = jnp.zeros((8, LANES), jnp.float32)
    for at in (0, rows + 8):
        for i in range(1, 6):
            for ref in z_planes + r_planes:
                ref[i, at : at + 8, :] = blank

    for t in range(rows // 8):
        row = 8 + 8 * t
        at = pl.ds(8 * t, 8)
        for i, j in enumerate(order):
            zc[i, pl.ds(row, 8), :] = el[at, LANES * j : LANES * j + LANES] if j < chunks else side[at, :]
        spread(z_planes, range(1, 6), row)

    for t in range(rows // 8):
        row = 8 + 8 * t
        at = pl.ds(8 * t, 8)
        for i, j in enumerate(order):
            if i in (2, 3, 4):
                total = reciprocal_total(z_planes, i, row, coef)
                recip[i - 2, at, :] = total
            else:
                total = known[j - 1, at, :]
            rc[i, pl.ds(row, 8), :] = total
        spread(r_planes, (1, 2, 4, 5), row)

    for t in range(rows // 8):
        row = 8 + 8 * t
        for n, i in enumerate((4, 5, 1, 2)):
            for which, field in enumerate(fields(z_planes, r_planes, i, row, coef)):
                out[which, n, pl.ds(8 * t, 8), :] = field


def inflow_kernel(
    coefs, coarse, from_n, from_f, el, side, middle, outer, middle_recip, outer_recip, mk, out_hbm,
    kc, kw, ke, sc, sw, se, run, gain, flow, zc, zw, ze, rc, rw, re, up_ref, vv_ref, out, out_sem,
):
    k = coarse.shape[0] // 4
    rows, cols = mk.shape
    chunks = cols // LANES
    r, count = lax.axis_index("rows"), lax.axis_size("rows")
    upper = r % 2 == 0
    coef = coefficient_tiles(coefs)
    n, f = from_n[...], from_f[...]
    cond = jnp.full(n.shape, upper)

    def unpack(x, gone):
        rest = lambda part, value: jnp.where(jnp.full(part.shape, gone), value, part)
        packed = x[2 * DEPTH : 3 * DEPTH]
        parts = (
            rest(x[0:DEPTH], OUTSIDE),
            rest(packed, OUTSIDE),
            rest(x[DEPTH : 2 * DEPTH], 0.0),
            rest(pltpu.roll(jnp.concatenate([packed, x[0:6]], axis=0), LANES // 2, 1)[0:DEPTH], 0.0),
        )
        lines = rest(x[3 * DEPTH : 3 * DEPTH + 2 * chunks], OUTSIDE)
        turned = pltpu.roll(x[2 * DEPTH : 2 * DEPTH + 8], LANES - LANES // 4, 1)[0:2]
        return parts, [lines[2 * j : 2 * j + 2] for j in range(chunks)] + [rest(turned, OUTSIDE)]

    above, above_lines = unpack(jnp.where(cond, f, n), r == 0)
    below, below_lines = unpack(jnp.where(cond, n, f), r == count - 1)

    k_planes, s_planes = (kc, kw, ke), (sc, sw, se)
    around = lambda size: (lambda j: j % size)
    for j in range(2):
        for ref, base, first, total in ((kc, 0, 8, 3 * k + 16), (run, 2, 0, 3 * k)):
            ref[j, 0 : first + k, :] = jnp.zeros((first + k, LANES), jnp.float32)
            ref[j, first + 2 * k : total, :] = jnp.zeros((total - first - 2 * k, LANES), jnp.float32)
            ref[j, first + k - DEPTH : first + k, :] = above[base + j]
            ref[j, first + k : first + 2 * k, :] = coarse[(base + j) * k : (base + j + 1) * k, :]
            ref[j, first + 2 * k : first + 2 * k + DEPTH, :] = below[base + j]
    for t in range(3 * k // 8 + 2):
        spread(k_planes, range(2), 8 * t, around(2))
    recip = {}
    for j in range(2):
        for t in range(3 * k // 8):
            recip[j, t] = reciprocal_total(k_planes, j, 8 + 8 * t, coef)
    inner = range(1, 3 * k // 8 - 1)
    for j in range(2):
        for t in inner:
            for d in range(8):
                gain[d, j, 8 * t : 8 * t + 8, :] = inward(k_planes, j, 8 + 8 * t, d, coef)

    z_planes, r_planes = (zc, zw, ze), (rc, rw, re)
    ring = around(chunks + 1)
    every = range(chunks + 1)
    for j in every:
        up2, down2 = above_lines[j], below_lines[j]
        if j < chunks:
            first, last = el[0:8, LANES * j : LANES * j + LANES], el[rows - 8 : rows, LANES * j : LANES * j + LANES]
        else:
            first, last = side[0:8, :], side[rows - 8 : rows, :]
        blank = jnp.zeros((8, LANES), jnp.float32)
        for at in (0, 16, 32):
            zc[j, at : at + 8, :] = blank
        zc[j, 8:16, :] = jnp.concatenate([up2, first[0:2], last[6:8], down2], axis=0)
        zc[j, 24:32, :] = jnp.concatenate([up2[1:2], first[0:3], last[5:8], down2[0:1]], axis=0)
    for row in (0, 8, 16, 24, 32):
        spread(z_planes, every, row, ring)
    for j in every:
        total = reciprocal_total(z_planes, j, 8, coef)
        if 1 <= j < chunks - 1:
            near = middle_recip.at[j - 1]
        else:
            near = outer_recip.at[{chunks - 1: 0, chunks: 1, 0: 2}[j]]
        first, last = near[0:8, :], near[rows - 8 : rows, :]
        for at in (0, 16):
            rc[j, at : at + 8, :] = jnp.zeros((8, LANES), jnp.float32)
        rc[j, 8:16, :] = jnp.concatenate([total[1:3], first[1:3], last[5:7], total[5:7]], axis=0)
    for row in (0, 8, 16):
        spread(r_planes, every, row, ring)
    border = {}
    for j in range(chunks):
        border[j] = fields((zc.at[:, 16:40, :], zw.at[:, 16:40, :], ze.at[:, 16:40, :]), r_planes, j, 8, coef, 1, 6)

    for j in range(2):
        for t in range(3 * k // 8):
            sc[j, 8 * t : 8 * t + 8, :] = recip[j, t] * run[j, 8 * t : 8 * t + 8, :]
    for t in range(3 * k // 8):
        spread(s_planes, range(2), 8 * t, around(2))
    for sweep in range(ITERS):
        for j in range(2):
            for t in inner:
                parts = [gain[d, j, 8 * t : 8 * t + 8, :] * neighbour(s_planes, j, 8 * t, d) for d in range(8)]
                total = ((parts[0] + parts[1]) + (parts[2] + parts[3])) + (
                    (parts[4] + parts[5]) + (parts[6] + parts[7])
                )
                flow[j, 8 * t : 8 * t + 8, :] = run[j, 8 * t : 8 * t + 8, :] + total
        if sweep < ITERS - 1:
            for j in range(2):
                for t in inner:
                    sc[j, 8 * t : 8 * t + 8, :] = recip[j, t] * flow[j, 8 * t : 8 * t + 8, :]
            for t in inner:
                spread(s_planes, range(2), 8 * t, around(2))

    lane = iota((8, LANES), 1)
    block = lane // 8
    step = jnp.where(lane % 8 == 7, 1, jnp.where(lane % 8 == 0, -1, 0))
    per = LANES // 8
    for t in inner:
        main = flow[0, 8 * t : 8 * t + 8, :]
        apart = flow[1, 8 * t : 8 * t + 8, :]
        for j in range(chunks):
            here = block + per * j
            over = here + step
            up_ref[j, 8 * t : 8 * t + 8, :] = jnp.take_along_axis(main, here, axis=1, mode="promise_in_bounds")
            v = jnp.take_along_axis(main, over & (LANES - 1), axis=1, mode="promise_in_bounds")
            if j == 0:
                far = jnp.take_along_axis(apart, over & (LANES - 1), axis=1, mode="promise_in_bounds")
                v = jnp.where(lane == 0, far, v)
            if j == chunks - 1:
                far = jnp.take_along_axis(apart, over & (LANES - 1), axis=1, mode="promise_in_bounds")
                v = jnp.where(lane == LANES - 1, far, v)
            vv_ref[j, 8 * t : 8 * t + 8, :] = v

    sub = iota((8, LANES), 0)
    high = sub < 4
    writes = []
    for b in range(rows // 8):
        for j in range(chunks):
            lanes = slice(LANES * j, LANES * j + LANES)
            at = slice(8 * b, 8 * b + 8)
            row = k + b
            wide = [jnp.broadcast_to(up_ref[j, row + i : row + i + 1, :], (8, LANES)) for i in (-1, 0, 1)]
            apart = [jnp.broadcast_to(vv_ref[j, row + i : row + i + 1, :], (8, LANES)) for i in (-1, 0, 1)]
            if 2 <= j < chunks - 2:
                a = [middle[i, j - 2, at, :] for i in range(4)]
            else:
                a = [outer[i, j if j < 2 else j - chunks + 4, at, :] for i in range(4)]
            if b == 0:
                a = [jnp.where(sub < 2, pltpu.roll(border[j][i], 7, 0), a[i]) for i in range(4)]
            if b == rows // 8 - 1:
                a = [jnp.where(sub > 5, pltpu.roll(border[j][i], 1, 0), a[i]) for i in range(4)]
            out[at, lanes] = mk[at, lanes].astype(jnp.float32) + (
                (a[0] * wide[1] + a[1] * apart[1])
                + (a[2] * jnp.where(high, wide[0], wide[2]) + a[3] * jnp.where(high, apart[0], apart[2]))
            )
        size = rows // PARTS
        if (8 * b + 8) % size == 0:
            p = 8 * b // size
            lines = pl.ds(p * size, size)
            copy = pltpu.make_async_copy(out.at[lines, :], out_hbm.at[lines, :], out_sem.at[p])
            copy.start()
            writes.append(copy)
    for copy in writes:
        copy.wait()


def swap(x, axis, far):
    sizes = {name: lax.axis_size(name) for name in ("rows", "cols")}
    pairs = []
    for r in range(sizes["rows"]):
        for c in range(sizes["cols"]):
            to = {"rows": r, "cols": c}
            i = to[axis]
            partner = i ^ 1 if not far else i + 1 if i % 2 else i - 1
            if 0 <= partner < sizes[axis]:
                to[axis] = partner
            else:
                other = "cols" if axis == "rows" else "rows"
                to[other] ^= 1
            pairs.append((r * sizes["cols"] + c, to["rows"] * sizes["cols"] + to["cols"]))
    return lax.ppermute(x, ("rows", "cols"), pairs)


def f32(*shape):
    return jax.ShapeDtypeStruct(shape, jnp.float32)


def whole(count):
    return [pl.BlockSpec(memory_space=VMEM)] * count


def on_device(elevation, data_mask, tie_order):
    rows, cols = elevation.shape
    k, chunks = rows // 8, cols // LANES
    params = pltpu.CompilerParams(vmem_limit_bytes=LIMIT)
    dma = pltpu.SemaphoreType.DMA
    hbm = pl.BlockSpec(memory_space=pltpu.HBM)
    tie_order, elevation, data_mask = (
        pltpu.with_memory_space_constraint(x, pltpu.HBM) for x in (tie_order, elevation, data_mask)
    )
    msg = pl.pallas_call(
        column_message_kernel,
        out_shape=f32(k + 8, LANES),
        in_specs=[hbm] * 2,
        out_specs=whole(1)[0],
        scratch_shapes=[
            VMEM((rows, 2 * LANES), jnp.float32),
            VMEM((rows, 2 * LANES), jnp.int32),
            dma((2,)),
            dma((2,)),
        ],
        compiler_params=params,
        name="column_message",
    )(elevation, data_mask)
    from_b = swap(msg, "cols", True)
    from_a = swap(msg, "cols", False)
    cost = pl.CostEstimate(flops=10_000_000, bytes_accessed=3_000_000, transcendentals=0)
    own, el, mk, coefs = pl.pallas_call(
        overview_kernel,
        out_shape=[
            f32(2 * k, LANES),
            f32(rows, cols),
            jax.ShapeDtypeStruct((rows, cols), jnp.int32),
            f32(8, LANES),
        ],
        in_specs=[hbm] * 3 + whole(1),
        out_specs=whole(4),
        scratch_shapes=[pltpu.SMEM((8,), jnp.int32), dma, dma((PIECES,)), dma((PIECES,))],
        compiler_params=params,
        cost_estimate=cost,
        name="overview",
    )(tie_order, elevation, data_mask, msg)
    plane = lambda count, height: VMEM((count, height, LANES), jnp.float32)
    middle, middle_recip = pl.pallas_call(
        middle_kernel,
        out_shape=[f32(4, chunks - 4, rows, LANES), f32(chunks - 2, rows, LANES)],
        in_specs=whole(2),
        out_specs=whole(2),
        scratch_shapes=[plane(chunks, rows + 16)] * 6,
        compiler_params=params,
        cost_estimate=cost,
        name="middle_fields",
    )(coefs, el)
    size = (3 * DEPTH + 2 * chunks + 7) // 8 * 8
    coarse, side, to_f = pl.pallas_call(
        row_message_kernel,
        out_shape=[f32(4 * k, LANES), f32(rows, LANES), f32(size, LANES)],
        in_specs=whole(5),
        out_specs=whole(3),
        compiler_params=params,
        name="far_message",
    )(own, from_a, from_b, el, middle_recip)
    from_f = swap(to_f, "rows", True)
    outer, outer_recip = pl.pallas_call(
        outer_kernel,
        out_shape=[f32(4, 4, rows, LANES), f32(3, rows, LANES)],
        in_specs=whole(4),
        out_specs=whole(2),
        scratch_shapes=[plane(7, rows + 16)] * 6,
        compiler_params=params,
        cost_estimate=cost,
        name="outer_fields",
    )(coefs, el, side, middle_recip)
    to_n = pl.pallas_call(
        near_message_kernel,
        out_shape=f32(size, LANES),
        in_specs=whole(4),
        out_specs=whole(1)[0],
        compiler_params=params,
        name="near_message",
    )(coarse, side, el, outer_recip)
    from_n = swap(to_n, "rows", False)
    return pl.pallas_call(
        inflow_kernel,
        out_shape=f32(rows, cols),
        in_specs=whole(11),
        out_specs=hbm,
        scratch_shapes=[plane(2, 3 * k + 16)] * 3
        + [plane(2, 3 * k)] * 4
        + [VMEM((8, 2, 3 * k, LANES), jnp.float32), plane(2, 3 * k)]
        + [plane(chunks + 1, 40)] * 3
        + [plane(chunks + 1, 24)] * 3
        + [plane(chunks, 3 * k)] * 2
        + [VMEM((rows, cols), jnp.float32), dma((PARTS,))],
        compiler_params=params,
        name="inflow",
    )(coefs, coarse, from_n, from_f, el, side, middle, outer, middle_recip, outer_recip, mk)


def solution(mesh):
    in_specs = (P("rows", "cols"), P("rows", "cols"), P())
    out_specs = P("rows", "cols")
    return jax.shard_map(
        on_device, mesh=mesh, in_specs=in_specs, out_specs=out_specs, check_vma=False
    )
```

```python
import jax
import jax.numpy as jnp
from jax import lax
from jax.experimental import pallas as pl
from jax.experimental.pallas import tpu as pltpu
from jax.sharding import PartitionSpec as P

ITERS = 8
OFFSETS = ((0, 1), (1, 1), (1, 0), (1, -1), (0, -1), (-1, -1), (-1, 0), (-1, 1))
DIAGONAL = 0.7071067811865476
RETENTION = 0.1
OUTSIDE = 1e30
LANES = 128
VMEM = pltpu.VMEM
LIMIT = 40 * 1024 * 1024


def iota(shape, dim):
    return lax.broadcasted_iota(jnp.int32, shape, dim)


def coefficients(tie_ref, coef_ref):
    for place in range(8):
        k = tie_ref[place]
        value = 1.0 + 0.5 * (7.0 - place) / 7.0
        scaled = jnp.where(k % 2 == 0, value, value * DIAGONAL).astype(jnp.float32)
        coef_ref[pl.ds(k, 1), :] = jnp.full((1, LANES), scaled)


def coefficient_tiles(coef_ref):
    return [jnp.broadcast_to(coef_ref[k : k + 1, :], (8, LANES)) for k in range(8)]


def neighbour(planes, j, row, k):
    step_row, step_col = OFFSETS[k]
    ref = planes[{0: 0, -1: 1, 1: 2}[step_col]]
    return ref[j, pl.ds(row + step_row, 8), :]


def spread(planes, wanted, row, ring=None):
    centre, west, east = planes
    lane = iota((8, LANES), 1)
    at = pl.ds(row, 8)
    ring = ring or (lambda j: j)
    to_east, to_west = {}, {}
    for j in wanted:
        for i in (ring(j - 1), j):
            if i not in to_east:
                to_east[i] = pltpu.roll(centre[i, at, :], 1, 1)
        for i in (j, ring(j + 1)):
            if i not in to_west:
                to_west[i] = pltpu.roll(centre[i, at, :], LANES - 1, 1)
        west[j, at, :] = jnp.where(lane == 0, to_east[ring(j - 1)], to_east[j])
        east[j, at, :] = jnp.where(lane == LANES - 1, to_west[ring(j + 1)], to_west[j])


def reciprocal_total(planes, j, row, coef):
    z = planes[0][j, pl.ds(row, 8), :]
    parts = [coef[k] * jnp.maximum(z - neighbour(planes, j, row, k), 0.0) for k in range(8)]
    total = ((parts[0] + parts[1]) + (parts[2] + parts[3])) + ((parts[4] + parts[5]) + (parts[6] + parts[7]))
    return 1.0 / (total + RETENTION)


def inward(planes, j, row, k, coef):
    z = planes[0][j, pl.ds(row, 8), :]
    return coef[(k + 4) % 8] * jnp.maximum(neighbour(planes, j, row, k) - z, 0.0)


def fields(z_planes, r_planes, j, row, coef, top=0, bottom=7):
    lane = iota((8, LANES), 1) % 8
    sub = iota((8, LANES), 0)
    at_east, at_west = lane == 7, lane == 0
    first, last = sub == top, sub == bottom
    t = [inward(z_planes, j, row, k, coef) * neighbour(r_planes, j, row, k) for k in range(8)]

    def split(east, west):
        own = jnp.where(at_east, west, jnp.where(at_west, east, east + west))
        other = jnp.where(at_east, east, jnp.where(at_west, west, 0.0))
        return own, other

    own0, other0 = split(t[0], t[4])
    own_down, other_down = split(t[1], t[3])
    own_down = own_down + t[2]
    own_up, other_up = split(t[7], t[5])
    own_up = own_up + t[6]
    a00 = own0 + jnp.where(first, 0.0, own_up) + jnp.where(last, 0.0, own_down)
    a01 = other0 + jnp.where(first, 0.0, other_up) + jnp.where(last, 0.0, other_down)
    a10 = jnp.where(first, own_up, jnp.where(last, own_down, 0.0))
    a11 = jnp.where(first, other_up, jnp.where(last, other_down, 0.0))
    return a00, a01, a10, a11


def block_rows(tiles):
    sub = iota(tiles[0].shape, 0)
    level = [tiles[t] for t in (0, 4, 2, 6, 1, 5, 3, 7)]
    for shift in (4, 2, 1):
        low = (sub & shift) == 0
        level = [
            jnp.where(low, a + pltpu.roll(a, 8 - shift, 0), b + pltpu.roll(b, shift, 0))
            for a, b in zip(level[0::2], level[1::2])
        ]
    return level[0]


DEPTH = ITERS + 2
PIECES = 2
PARTS = 4


def edges(overview, runoff):
    lane = iota(overview.shape, 1)
    outer = (lane < DEPTH) | (lane >= LANES - DEPTH)
    return jnp.where(outer, overview, pltpu.roll(runoff, LANES // 2, 1))


def chunk_sums(el, mk, lanes, rows):
    s_groups, n_groups = [], []
    for g in range(rows // 64):
        at = [(slice(64 * g + 8 * t, 64 * g + 8 * t + 8), lanes) for t in range(8)]
        flags = [mk[i].astype(jnp.float32) for i in at]
        n_groups.append(block_rows(flags))
        s_groups.append(block_rows([m * el[i] for m, i in zip(flags, at)]))
    return jnp.concatenate(s_groups, axis=0), jnp.concatenate(n_groups, axis=0)


def block_means(s, n, place):
    k = s.shape[0]
    pick = jnp.where(place == iota((s.shape[1], LANES), 1), 1.0, 0.0).astype(jnp.bfloat16)
    hi = s.astype(jnp.bfloat16)
    rest = s - hi.astype(jnp.float32)
    mid = rest.astype(jnp.bfloat16)
    low = (rest - mid.astype(jnp.float32)).astype(jnp.bfloat16)
    left = jnp.concatenate([hi, mid, low, n.astype(jnp.bfloat16)], axis=0)
    out = lax.dot_general(left, pick, (((1,), (0,)), ((), ())), preferred_element_type=jnp.float32)
    summed = out[0:k] + (out[k : 2 * k] + out[2 * k : 3 * k])
    count = out[3 * k : 4 * k]
    return summed / (count + 1.0), count * (1.0 / 64.0)


def column_message_kernel(el_hbm, mk_hbm, msg, el, mk, el_sem, mk_sem):
    rows, cols = el_hbm.shape
    k = rows // 8
    fetch = []
    for i, start in enumerate((0, cols - LANES)):
        far, near = pl.ds(start, LANES), pl.ds(i * LANES, LANES)
        fetch.append(pltpu.make_async_copy(el_hbm.at[:, far], el.at[:, near], el_sem.at[i]))
        fetch.append(pltpu.make_async_copy(mk_hbm.at[:, far], mk.at[:, near], mk_sem.at[i]))
    for copy in fetch:
        copy.start()
    for copy in fetch:
        copy.wait()
    first, last = slice(0, LANES), slice(LANES, 2 * LANES)
    (s0, n0), (s1, n1) = chunk_sums(el, mk, first, rows), chunk_sums(el, mk, last, rows)
    column = iota((2 * LANES, LANES), 0)
    place = jnp.where(column < LANES, column // 8, LANES - 2 * LANES // 8 + column // 8)
    overview, runoff = block_means(jnp.concatenate([s0, s1], axis=1), jnp.concatenate([n0, n1], axis=1), place)
    msg[0:k, :] = edges(overview, runoff)
    msg[k : k + 4, :] = jnp.transpose(el[:, first])[0:4]
    msg[k + 4 : k + 8, :] = jnp.transpose(el[:, last])[LANES - 4 : LANES]


def overview_kernel(tie_hbm, el_hbm, mk_hbm, after, own, el, mk, coef, tie, tie_sem, el_sem, mk_sem):
    rows, cols = el.shape
    chunks = cols // LANES
    k = rows // 8
    per = chunks // PIECES
    fetch = []
    for p in range(PIECES):
        at = pl.ds(p * per * LANES, per * LANES)
        pair = (
            pltpu.make_async_copy(el_hbm.at[:, at], el.at[:, at], el_sem.at[p]),
            pltpu.make_async_copy(mk_hbm.at[:, at], mk.at[:, at], mk_sem.at[p]),
        )
        for copy in pair:
            copy.start()
        fetch.append(pair)
    tie_copy = pltpu.make_async_copy(tie_hbm, tie, tie_sem)
    tie_copy.start()
    tie_copy.wait()
    coefficients(tie, coef)
    parts = []
    for p, pair in enumerate(fetch):
        for copy in pair:
            copy.wait()
        for j in range(p * per, (p + 1) * per):
            parts.append(chunk_sums(el, mk, slice(LANES * j, LANES * j + LANES), rows))
    s, n = (jnp.concatenate(x, axis=1) for x in zip(*parts))
    overview, runoff = block_means(s, n, iota((cols, LANES), 0) // 8)
    own[0:k, :] = overview
    own[k : 2 * k, :] = runoff


def row_message_kernel(own, from_a, from_b, el, coarse, side, to_f):
    k = own.shape[0] // 2
    r, c = lax.axis_index("rows"), lax.axis_index("cols")
    count = lax.axis_size("cols")
    even = jnp.full((k + 8, LANES), c % 2 == 0)
    a, b = from_a[...], from_b[...]
    right, left = jnp.where(even, a, b), jnp.where(even, b, a)
    lane = iota((k, LANES), 1)
    east = lane < LANES // 2
    gone_east, gone_west = jnp.full((k, LANES), c == count - 1), jnp.full((k, LANES), c == 0)
    gone = (east & gone_east) | (~east & gone_west)
    near = jnp.where(gone, OUTSIDE, jnp.where(east, right[0:k], left[0:k]))
    near_run = pltpu.roll(jnp.where(east, left[0:k], right[0:k]), LANES // 2, 1)
    near_run = jnp.where(gone, 0.0, near_run)
    over, run = own[0:k, :], own[k : 2 * k, :]
    for i, part in enumerate((over, near, run, near_run)):
        coarse[i * k : (i + 1) * k, :] = part
    columns = jnp.concatenate(
        [
            jnp.where(jnp.full((4, LANES), c == count - 1), OUTSIDE, right[k : k + 4]),
            jnp.zeros((LANES - 8, LANES), jnp.float32),
            jnp.where(jnp.full((4, LANES), c == 0), OUTSIDE, left[k + 4 : k + 8]),
        ],
        axis=0,
    )
    beyond = jnp.transpose(columns)
    side[...] = beyond
    message((over, run, edges(near, near_run)), beyond, el, r % 2 == 1, to_f)


def message(parts, beyond, el, lower, out):
    rows, cols = el.shape
    k = parts[0].shape[0]
    turned = pltpu.roll(jnp.concatenate([beyond[0:8], beyond[rows - 8 : rows]], axis=0), LANES // 4, 1)
    lane2 = iota((2, LANES), 1)
    quarter = (lane2 >= LANES // 4 - 2) & (lane2 < LANES // 4 + 2)

    def put(at, top, bottom):
        out[at : at + top.shape[0], :] = jnp.where(jnp.full(top.shape, lower), bottom, top)

    for i, part in enumerate(parts):
        put(i * DEPTH, part[0:DEPTH], part[k - DEPTH : k])
    for j in range(cols // LANES):
        lanes = slice(LANES * j, LANES * j + LANES)
        put(3 * DEPTH + 2 * j, el[0:2, lanes], el[rows - 2 : rows, lanes])
    packed = parts[2]
    put(
        2 * DEPTH,
        jnp.where(quarter, turned[0:2], packed[0:2]),
        jnp.where(quarter, turned[14:16], packed[k - DEPTH : k - DEPTH + 2]),
    )


def near_message_kernel(coarse, side, el, after, to_n):
    k = coarse.shape[0] // 4
    over, near, run, near_run = (coarse[i * k : (i + 1) * k, :] for i in range(4))
    message((over, run, edges(near, near_run)), side[...], el, lax.axis_index("rows") % 2 == 0, to_n)


def middle_kernel(coefs, el, after, out, recip, zc, zw, ze, rc, rw, re):
    rows, cols = el.shape
    chunks = cols // LANES
    coef = coefficient_tiles(coefs)
    z_planes, r_planes = (zc, zw, ze), (rc, rw, re)
    inner, core = range(1, chunks - 1), range(2, chunks - 2)
    blank = jnp.zeros((8, LANES), jnp.float32)
    for at in (0, rows + 8):
        for j in inner:
            for ref in z_planes + r_planes:
                ref[j, at : at + 8, :] = blank

    for t in range(rows // 8):
        row = 8 + 8 * t
        for j in range(chunks):
            zc[j, pl.ds(row, 8), :] = el[pl.ds(8 * t, 8), LANES * j : LANES * j + LANES]
        spread(z_planes, inner, row)

    for t in range(rows // 8):
        row = 8 + 8 * t
        for j in inner:
            total = reciprocal_total(z_planes, j, row, coef)
            rc[j, pl.ds(row, 8), :] = total
            recip[j - 1, pl.ds(8 * t, 8), :] = total
        spread(r_planes, core, row)

    for t in range(rows // 8):
        row = 8 + 8 * t
        for j in core:
            for i, field in enumerate(fields(z_planes, r_planes, j, row, coef)):
                out[i, j - 2, pl.ds(8 * t, 8), :] = field


def outer_kernel(coefs, el, side, known, out, recip, zc, zw, ze, rc, rw, re):
    rows, cols = el.shape
    chunks = cols // LANES
    coef = coefficient_tiles(coefs)
    z_planes, r_planes = (zc, zw, ze), (rc, rw, re)
    order = (chunks - 3, chunks - 2, chunks - 1, chunks, 0, 1, 2)
    blank = jnp.zeros((8, LANES), jnp.float32)
    for at in (0, rows + 8):
        for i in range(1, 6):
            for ref in z_planes + r_planes:
                ref[i, at : at + 8, :] = blank

    for t in range(rows // 8):
        row = 8 + 8 * t
        at = pl.ds(8 * t, 8)
        for i, j in enumerate(order):
            zc[i, pl.ds(row, 8), :] = el[at, LANES * j : LANES * j + LANES] if j < chunks else side[at, :]
        spread(z_planes, range(1, 6), row)

    for t in range(rows // 8):
        row = 8 + 8 * t
        at = pl.ds(8 * t, 8)
        for i, j in enumerate(order):
            if i in (2, 3, 4):
                total = reciprocal_total(z_planes, i, row, coef)
                recip[i - 2, at, :] = total
            else:
                total = known[j - 1, at, :]
            rc[i, pl.ds(row, 8), :] = total
        spread(r_planes, (1, 2, 4, 5), row)

    for t in range(rows // 8):
        row = 8 + 8 * t
        for n, i in enumerate((4, 5, 1, 2)):
            for which, field in enumerate(fields(z_planes, r_planes, i, row, coef)):
                out[which, n, pl.ds(8 * t, 8), :] = field


def inflow_kernel(
    coefs, coarse, from_n, from_f, el, side, middle, outer, middle_recip, outer_recip, mk, out_hbm,
    kc, kw, ke, sc, sw, se, run, gain, flow, zc, zw, ze, rc, rw, re, up_ref, vv_ref, out, out_sem,
):
    k = coarse.shape[0] // 4
    rows, cols = mk.shape
    chunks = cols // LANES
    r, count = lax.axis_index("rows"), lax.axis_size("rows")
    upper = r % 2 == 0
    coef = coefficient_tiles(coefs)
    n, f = from_n[...], from_f[...]
    cond = jnp.full(n.shape, upper)

    def unpack(x, gone):
        rest = lambda part, value: jnp.where(jnp.full(part.shape, gone), value, part)
        packed = x[2 * DEPTH : 3 * DEPTH]
        parts = (
            rest(x[0:DEPTH], OUTSIDE),
            rest(packed, OUTSIDE),
            rest(x[DEPTH : 2 * DEPTH], 0.0),
            rest(pltpu.roll(jnp.concatenate([packed, x[0:6]], axis=0), LANES // 2, 1)[0:DEPTH], 0.0),
        )
        lines = rest(x[3 * DEPTH : 3 * DEPTH + 2 * chunks], OUTSIDE)
        turned = pltpu.roll(x[2 * DEPTH : 2 * DEPTH + 8], LANES - LANES // 4, 1)[0:2]
        return parts, [lines[2 * j : 2 * j + 2] for j in range(chunks)] + [rest(turned, OUTSIDE)]

    above, above_lines = unpack(jnp.where(cond, f, n), r == 0)
    below, below_lines = unpack(jnp.where(cond, n, f), r == count - 1)

    k_planes, s_planes = (kc, kw, ke), (sc, sw, se)
    around = lambda size: (lambda j: j % size)
    for j in range(2):
        for ref, base, first, total in ((kc, 0, 8, 3 * k + 16), (run, 2, 0, 3 * k)):
            ref[j, 0 : first + k, :] = jnp.zeros((first + k, LANES), jnp.float32)
            ref[j, first + 2 * k : total, :] = jnp.zeros((total - first - 2 * k, LANES), jnp.float32)
            ref[j, first + k - DEPTH : first + k, :] = above[base + j]
            ref[j, first + k : first + 2 * k, :] = coarse[(base + j) * k : (base + j + 1) * k, :]
            ref[j, first + 2 * k : first + 2 * k + DEPTH, :] = below[base + j]
    for t in range(3 * k // 8 + 2):
        spread(k_planes, range(2), 8 * t, around(2))
    recip = {}
    for j in range(2):
        for t in range(3 * k // 8):
            recip[j, t] = reciprocal_total(k_planes, j, 8 + 8 * t, coef)
    inner = range(1, 3 * k // 8 - 1)
    for j in range(2):
        for t in inner:
            for d in range(8):
                gain[d, j, 8 * t : 8 * t + 8, :] = inward(k_planes, j, 8 + 8 * t, d, coef)

    z_planes, r_planes = (zc, zw, ze), (rc, rw, re)
    ring = around(chunks + 1)
    every = range(chunks + 1)
    for j in every:
        up2, down2 = above_lines[j], below_lines[j]
        if j < chunks:
            first, last = el[0:8, LANES * j : LANES * j + LANES], el[rows - 8 : rows, LANES * j : LANES * j + LANES]
        else:
            first, last = side[0:8, :], side[rows - 8 : rows, :]
        blank = jnp.zeros((8, LANES), jnp.float32)
        for at in (0, 16, 32):
            zc[j, at : at + 8, :] = blank
        zc[j, 8:16, :] = jnp.concatenate([up2, first[0:2], last[6:8], down2], axis=0)
        zc[j, 24:32, :] = jnp.concatenate([up2[1:2], first[0:3], last[5:8], down2[0:1]], axis=0)
    for row in (0, 8, 16, 24, 32):
        spread(z_planes, every, row, ring)
    for j in every:
        total = reciprocal_total(z_planes, j, 8, coef)
        if 1 <= j < chunks - 1:
            near = middle_recip.at[j - 1]
        else:
            near = outer_recip.at[{chunks - 1: 0, chunks: 1, 0: 2}[j]]
        first, last = near[0:8, :], near[rows - 8 : rows, :]
        for at in (0, 16):
            rc[j, at : at + 8, :] = jnp.zeros((8, LANES), jnp.float32)
        rc[j, 8:16, :] = jnp.concatenate([total[1:3], first[1:3], last[5:7], total[5:7]], axis=0)
    for row in (0, 8, 16):
        spread(r_planes, every, row, ring)
    border = {}
    for j in range(chunks):
        border[j] = fields((zc.at[:, 16:40, :], zw.at[:, 16:40, :], ze.at[:, 16:40, :]), r_planes, j, 8, coef, 1, 6)

    for j in range(2):
        for t in range(3 * k // 8):
            sc[j, 8 * t : 8 * t + 8, :] = recip[j, t] * run[j, 8 * t : 8 * t + 8, :]
    for t in range(3 * k // 8):
        spread(s_planes, range(2), 8 * t, around(2))
    for sweep in range(ITERS):
        for j in range(2):
            for t in inner:
                parts = [gain[d, j, 8 * t : 8 * t + 8, :] * neighbour(s_planes, j, 8 * t, d) for d in range(8)]
                total = ((parts[0] + parts[1]) + (parts[2] + parts[3])) + (
                    (parts[4] + parts[5]) + (parts[6] + parts[7])
                )
                flow[j, 8 * t : 8 * t + 8, :] = run[j, 8 * t : 8 * t + 8, :] + total
        if sweep < ITERS - 1:
            for j in range(2):
                for t in inner:
                    sc[j, 8 * t : 8 * t + 8, :] = recip[j, t] * flow[j, 8 * t : 8 * t + 8, :]
            for t in inner:
                spread(s_planes, range(2), 8 * t, around(2))

    lane = iota((8, LANES), 1)
    block = lane // 8
    step = jnp.where(lane % 8 == 7, 1, jnp.where(lane % 8 == 0, -1, 0))
    per = LANES // 8
    for t in inner:
        main = flow[0, 8 * t : 8 * t + 8, :]
        apart = flow[1, 8 * t : 8 * t + 8, :]
        for j in range(chunks):
            here = block + per * j
            over = here + step
            up_ref[j, 8 * t : 8 * t + 8, :] = jnp.take_along_axis(main, here, axis=1, mode="promise_in_bounds")
            v = jnp.take_along_axis(main, over & (LANES - 1), axis=1, mode="promise_in_bounds")
            if j == 0:
                far = jnp.take_along_axis(apart, over & (LANES - 1), axis=1, mode="promise_in_bounds")
                v = jnp.where(lane == 0, far, v)
            if j == chunks - 1:
                far = jnp.take_along_axis(apart, over & (LANES - 1), axis=1, mode="promise_in_bounds")
                v = jnp.where(lane == LANES - 1, far, v)
            vv_ref[j, 8 * t : 8 * t + 8, :] = v

    sub = iota((8, LANES), 0)
    high = sub < 4
    writes = []
    for b in range(rows // 8):
        for j in range(chunks):
            lanes = slice(LANES * j, LANES * j + LANES)
            at = slice(8 * b, 8 * b + 8)
            row = k + b
            wide = [jnp.broadcast_to(up_ref[j, row + i : row + i + 1, :], (8, LANES)) for i in (-1, 0, 1)]
            apart = [jnp.broadcast_to(vv_ref[j, row + i : row + i + 1, :], (8, LANES)) for i in (-1, 0, 1)]
            if 2 <= j < chunks - 2:
                a = [middle[i, j - 2, at, :] for i in range(4)]
            else:
                a = [outer[i, j if j < 2 else j - chunks + 4, at, :] for i in range(4)]
            if b == 0:
                a = [jnp.where(sub < 2, pltpu.roll(border[j][i], 7, 0), a[i]) for i in range(4)]
            if b == rows // 8 - 1:
                a = [jnp.where(sub > 5, pltpu.roll(border[j][i], 1, 0), a[i]) for i in range(4)]
            out[at, lanes] = mk[at, lanes].astype(jnp.float32) + (
                (a[0] * wide[1] + a[1] * apart[1])
                + (a[2] * jnp.where(high, wide[0], wide[2]) + a[3] * jnp.where(high, apart[0], apart[2]))
            )
        size = rows // PARTS
        if (8 * b + 8) % size == 0:
            p = 8 * b // size
            lines = pl.ds(p * size, size)
            copy = pltpu.make_async_copy(out.at[lines, :], out_hbm.at[lines, :], out_sem.at[p])
            copy.start()
            writes.append(copy)
    for copy in writes:
        copy.wait()


def swap(x, axis, far):
    sizes = {name: lax.axis_size(name) for name in ("rows", "cols")}
    pairs = []
    for r in range(sizes["rows"]):
        for c in range(sizes["cols"]):
            to = {"rows": r, "cols": c}
            i = to[axis]
            partner = i ^ 1 if not far else i + 1 if i % 2 else i - 1
            if 0 <= partner < sizes[axis]:
                to[axis] = partner
            else:
                other = "cols" if axis == "rows" else "rows"
                to[other] ^= 1
            pairs.append((r * sizes["cols"] + c, to["rows"] * sizes["cols"] + to["cols"]))
    return lax.ppermute(x, ("rows", "cols"), pairs)


def f32(*shape):
    return jax.ShapeDtypeStruct(shape, jnp.float32)


def whole(count):
    return [pl.BlockSpec(memory_space=VMEM)] * count


def on_device(elevation, data_mask, tie_order):
    rows, cols = elevation.shape
    k, chunks = rows // 8, cols // LANES
    params = pltpu.CompilerParams(vmem_limit_bytes=LIMIT)
    dma = pltpu.SemaphoreType.DMA
    hbm = pl.BlockSpec(memory_space=pltpu.HBM)
    tie_order, elevation, data_mask = (
        pltpu.with_memory_space_constraint(x, pltpu.HBM) for x in (tie_order, elevation, data_mask)
    )
    msg = pl.pallas_call(
        column_message_kernel,
        out_shape=f32(k + 8, LANES),
        in_specs=[hbm] * 2,
        out_specs=whole(1)[0],
        scratch_shapes=[
            VMEM((rows, 2 * LANES), jnp.float32),
            VMEM((rows, 2 * LANES), jnp.int32),
            dma((2,)),
            dma((2,)),
        ],
        compiler_params=params,
        name="column_message",
    )(elevation, data_mask)
    from_b = swap(msg, "cols", True)
    from_a = swap(msg, "cols", False)
    cost = pl.CostEstimate(flops=10_000_000, bytes_accessed=3_000_000, transcendentals=0)
    own, el, mk, coefs = pl.pallas_call(
        overview_kernel,
        out_shape=[
            f32(2 * k, LANES),
            f32(rows, cols),
            jax.ShapeDtypeStruct((rows, cols), jnp.int32),
            f32(8, LANES),
        ],
        in_specs=[hbm] * 3 + whole(1),
        out_specs=whole(4),
        scratch_shapes=[pltpu.SMEM((8,), jnp.int32), dma, dma((PIECES,)), dma((PIECES,))],
        compiler_params=params,
        cost_estimate=cost,
        name="overview",
    )(tie_order, elevation, data_mask, msg)
    plane = lambda count, height: VMEM((count, height, LANES), jnp.float32)
    size = (3 * DEPTH + 2 * chunks + 7) // 8 * 8
    coarse, side, to_f = pl.pallas_call(
        row_message_kernel,
        out_shape=[f32(4 * k, LANES), f32(rows, LANES), f32(size, LANES)],
        in_specs=whole(4),
        out_specs=whole(3),
        compiler_params=params,
        name="far_message",
    )(own, from_a, from_b, el)
    from_f = swap(to_f, "rows", True)
    middle, middle_recip = pl.pallas_call(
        middle_kernel,
        out_shape=[f32(4, chunks - 4, rows, LANES), f32(chunks - 2, rows, LANES)],
        in_specs=whole(3),
        out_specs=whole(2),
        scratch_shapes=[plane(chunks, rows + 16)] * 6,
        compiler_params=params,
        cost_estimate=cost,
        name="middle_fields",
    )(coefs, el, to_f)
    to_n = pl.pallas_call(
        near_message_kernel,
        out_shape=f32(size, LANES),
        in_specs=whole(4),
        out_specs=whole(1)[0],
        compiler_params=params,
        name="near_message",
    )(coarse, side, el, middle_recip)
    from_n = swap(to_n, "rows", False)
    outer, outer_recip = pl.pallas_call(
        outer_kernel,
        out_shape=[f32(4, 4, rows, LANES), f32(3, rows, LANES)],
        in_specs=whole(4),
        out_specs=whole(2),
        scratch_shapes=[plane(7, rows + 16)] * 6,
        compiler_params=params,
        cost_estimate=cost,
        name="outer_fields",
    )(coefs, el, side, middle_recip)
    return pl.pallas_call(
        inflow_kernel,
        out_shape=f32(rows, cols),
        in_specs=whole(11),
        out_specs=hbm,
        scratch_shapes=[plane(2, 3 * k + 16)] * 3
        + [plane(2, 3 * k)] * 4
        + [VMEM((8, 2, 3 * k, LANES), jnp.float32), plane(2, 3 * k)]
        + [plane(chunks + 1, 40)] * 3
        + [plane(chunks + 1, 24)] * 3
        + [plane(chunks, 3 * k)] * 2
        + [VMEM((rows, cols), jnp.float32), dma((PARTS,))],
        compiler_params=params,
        name="inflow",
    )(coefs, coarse, from_n, from_f, el, side, middle, outer, middle_recip, outer_recip, mk)


def solution(mesh):
    in_specs = (P("rows", "cols"), P("rows", "cols"), P())
    out_specs = P("rows", "cols")
    return jax.shard_map(
        on_device, mesh=mesh, in_specs=in_specs, out_specs=out_specs, check_vma=False
    )
```

```python
import jax
import jax.numpy as jnp
from jax import lax
from jax.experimental import pallas as pl
from jax.experimental.pallas import tpu as pltpu
from jax.sharding import PartitionSpec as P

ITERS = 8
OFFSETS = ((0, 1), (1, 1), (1, 0), (1, -1), (0, -1), (-1, -1), (-1, 0), (-1, 1))
DIAGONAL = 0.7071067811865476
RETENTION = 0.1
OUTSIDE = 1e30
LANES = 128
VMEM = pltpu.VMEM
LIMIT = 40 * 1024 * 1024


def iota(shape, dim):
    return lax.broadcasted_iota(jnp.int32, shape, dim)


def coefficients(tie_ref, coef_ref):
    for place in range(8):
        k = tie_ref[place]
        value = 1.0 + 0.5 * (7.0 - place) / 7.0
        scaled = jnp.where(k % 2 == 0, value, value * DIAGONAL).astype(jnp.float32)
        coef_ref[pl.ds(k, 1), :] = jnp.full((1, LANES), scaled)


def coefficient_tiles(coef_ref):
    return [jnp.broadcast_to(coef_ref[k : k + 1, :], (8, LANES)) for k in range(8)]


def neighbour(planes, j, row, k):
    step_row, step_col = OFFSETS[k]
    ref = planes[{0: 0, -1: 1, 1: 2}[step_col]]
    return ref[j, pl.ds(row + step_row, 8), :]


def spread(planes, wanted, row, ring=None):
    centre, west, east = planes
    lane = iota((8, LANES), 1)
    at = pl.ds(row, 8)
    ring = ring or (lambda j: j)
    to_east, to_west = {}, {}
    for j in wanted:
        for i in (ring(j - 1), j):
            if i not in to_east:
                to_east[i] = pltpu.roll(centre[i, at, :], 1, 1)
        for i in (j, ring(j + 1)):
            if i not in to_west:
                to_west[i] = pltpu.roll(centre[i, at, :], LANES - 1, 1)
        west[j, at, :] = jnp.where(lane == 0, to_east[ring(j - 1)], to_east[j])
        east[j, at, :] = jnp.where(lane == LANES - 1, to_west[ring(j + 1)], to_west[j])


def reciprocal_total(planes, j, row, coef):
    z = planes[0][j, pl.ds(row, 8), :]
    parts = [coef[k] * jnp.maximum(z - neighbour(planes, j, row, k), 0.0) for k in range(8)]
    total = ((parts[0] + parts[1]) + (parts[2] + parts[3])) + ((parts[4] + parts[5]) + (parts[6] + parts[7]))
    return 1.0 / (total + RETENTION)


def inward(planes, j, row, k, coef):
    z = planes[0][j, pl.ds(row, 8), :]
    return coef[(k + 4) % 8] * jnp.maximum(neighbour(planes, j, row, k) - z, 0.0)


def fields(z_planes, r_planes, j, row, coef, top=0, bottom=7):
    lane = iota((8, LANES), 1) % 8
    sub = iota((8, LANES), 0)
    at_east, at_west = lane == 7, lane == 0
    first, last = sub == top, sub == bottom
    t = [inward(z_planes, j, row, k, coef) * neighbour(r_planes, j, row, k) for k in range(8)]

    def split(east, west):
        own = jnp.where(at_east, west, jnp.where(at_west, east, east + west))
        other = jnp.where(at_east, east, jnp.where(at_west, west, 0.0))
        return own, other

    own0, other0 = split(t[0], t[4])
    own_down, other_down = split(t[1], t[3])
    own_down = own_down + t[2]
    own_up, other_up = split(t[7], t[5])
    own_up = own_up + t[6]
    a00 = own0 + jnp.where(first, 0.0, own_up) + jnp.where(last, 0.0, own_down)
    a01 = other0 + jnp.where(first, 0.0, other_up) + jnp.where(last, 0.0, other_down)
    a10 = jnp.where(first, own_up, jnp.where(last, own_down, 0.0))
    a11 = jnp.where(first, other_up, jnp.where(last, other_down, 0.0))
    return a00, a01, a10, a11


def block_rows(tiles):
    sub = iota(tiles[0].shape, 0)
    level = [tiles[t] for t in (0, 4, 2, 6, 1, 5, 3, 7)]
    for shift in (4, 2, 1):
        low = (sub & shift) == 0
        level = [
            jnp.where(low, a + pltpu.roll(a, 8 - shift, 0), b + pltpu.roll(b, shift, 0))
            for a, b in zip(level[0::2], level[1::2])
        ]
    return level[0]


DEPTH = ITERS + 2
PIECES = 2
PARTS = 4


def edges(overview, runoff):
    lane = iota(overview.shape, 1)
    outer = (lane < DEPTH) | (lane >= LANES - DEPTH)
    return jnp.where(outer, overview, pltpu.roll(runoff, LANES // 2, 1))


def chunk_sums(el, mk, lanes, rows):
    s_groups, n_groups = [], []
    for g in range(rows // 64):
        at = [(slice(64 * g + 8 * t, 64 * g + 8 * t + 8), lanes) for t in range(8)]
        flags = [mk[i].astype(jnp.float32) for i in at]
        n_groups.append(block_rows(flags))
        s_groups.append(block_rows([m * el[i] for m, i in zip(flags, at)]))
    return jnp.concatenate(s_groups, axis=0), jnp.concatenate(n_groups, axis=0)


def block_means(s, n, place):
    k = s.shape[0]
    pick = jnp.where(place == iota((s.shape[1], LANES), 1), 1.0, 0.0).astype(jnp.bfloat16)
    hi = s.astype(jnp.bfloat16)
    rest = s - hi.astype(jnp.float32)
    mid = rest.astype(jnp.bfloat16)
    low = (rest - mid.astype(jnp.float32)).astype(jnp.bfloat16)
    left = jnp.concatenate([hi, mid, low, n.astype(jnp.bfloat16)], axis=0)
    out = lax.dot_general(left, pick, (((1,), (0,)), ((), ())), preferred_element_type=jnp.float32)
    summed = out[0:k] + (out[k : 2 * k] + out[2 * k : 3 * k])
    count = out[3 * k : 4 * k]
    return summed / (count + 1.0), count * (1.0 / 64.0)


def column_message_kernel(el_hbm, mk_hbm, msg, el, mk, el_sem, mk_sem):
    rows, cols = el_hbm.shape
    k = rows // 8
    fetch = []
    for i, start in enumerate((0, cols - LANES)):
        far, near = pl.ds(start, LANES), pl.ds(i * LANES, LANES)
        fetch.append(pltpu.make_async_copy(el_hbm.at[:, far], el.at[:, near], el_sem.at[i]))
        fetch.append(pltpu.make_async_copy(mk_hbm.at[:, far], mk.at[:, near], mk_sem.at[i]))
    for copy in fetch:
        copy.start()
    for copy in fetch:
        copy.wait()
    first, last = slice(0, LANES), slice(LANES, 2 * LANES)
    (s0, n0), (s1, n1) = chunk_sums(el, mk, first, rows), chunk_sums(el, mk, last, rows)
    column = iota((2 * LANES, LANES), 0)
    place = jnp.where(column < LANES, column // 8, LANES - 2 * LANES // 8 + column // 8)
    overview, runoff = block_means(jnp.concatenate([s0, s1], axis=1), jnp.concatenate([n0, n1], axis=1), place)
    msg[0:k, :] = edges(overview, runoff)
    msg[k : k + 4, :] = jnp.transpose(el[:, first])[0:4]
    msg[k + 4 : k + 8, :] = jnp.transpose(el[:, last])[LANES - 4 : LANES]


def overview_kernel(tie_hbm, el_hbm, mk_hbm, after, own, el, mk, coef, tie, tie_sem, el_sem, mk_sem):
    rows, cols = el.shape
    chunks = cols // LANES
    k = rows // 8
    per = chunks // PIECES
    fetch = []
    for p in range(PIECES):
        at = pl.ds(p * per * LANES, per * LANES)
        pair = (
            pltpu.make_async_copy(el_hbm.at[:, at], el.at[:, at], el_sem.at[p]),
            pltpu.make_async_copy(mk_hbm.at[:, at], mk.at[:, at], mk_sem.at[p]),
        )
        for copy in pair:
            copy.start()
        fetch.append(pair)
    tie_copy = pltpu.make_async_copy(tie_hbm, tie, tie_sem)
    tie_copy.start()
    tie_copy.wait()
    coefficients(tie, coef)
    parts = []
    for p, pair in enumerate(fetch):
        for copy in pair:
            copy.wait()
        for j in range(p * per, (p + 1) * per):
            parts.append(chunk_sums(el, mk, slice(LANES * j, LANES * j + LANES), rows))
    s, n = (jnp.concatenate(x, axis=1) for x in zip(*parts))
    overview, runoff = block_means(s, n, iota((cols, LANES), 0) // 8)
    own[0:k, :] = overview
    own[k : 2 * k, :] = runoff


def row_message_kernel(own, from_a, from_b, el, after, coarse, side, to_f):
    k = own.shape[0] // 2
    r, c = lax.axis_index("rows"), lax.axis_index("cols")
    count = lax.axis_size("cols")
    even = jnp.full((k + 8, LANES), c % 2 == 0)
    a, b = from_a[...], from_b[...]
    right, left = jnp.where(even, a, b), jnp.where(even, b, a)
    lane = iota((k, LANES), 1)
    east = lane < LANES // 2
    gone_east, gone_west = jnp.full((k, LANES), c == count - 1), jnp.full((k, LANES), c == 0)
    gone = (east & gone_east) | (~east & gone_west)
    near = jnp.where(gone, OUTSIDE, jnp.where(east, right[0:k], left[0:k]))
    near_run = pltpu.roll(jnp.where(east, left[0:k], right[0:k]), LANES // 2, 1)
    near_run = jnp.where(gone, 0.0, near_run)
    over, run = own[0:k, :], own[k : 2 * k, :]
    for i, part in enumerate((over, near, run, near_run)):
        coarse[i * k : (i + 1) * k, :] = part
    columns = jnp.concatenate(
        [
            jnp.where(jnp.full((4, LANES), c == count - 1), OUTSIDE, right[k : k + 4]),
            jnp.zeros((LANES - 8, LANES), jnp.float32),
            jnp.where(jnp.full((4, LANES), c == 0), OUTSIDE, left[k + 4 : k + 8]),
        ],
        axis=0,
    )
    beyond = jnp.transpose(columns)
    side[...] = beyond
    message((over, run, edges(near, near_run)), beyond, el, r % 2 == 1, to_f)


def message(parts, beyond, el, lower, out):
    rows, cols = el.shape
    k = parts[0].shape[0]
    turned = pltpu.roll(jnp.concatenate([beyond[0:8], beyond[rows - 8 : rows]], axis=0), LANES // 4, 1)
    lane2 = iota((2, LANES), 1)
    quarter = (lane2 >= LANES // 4 - 2) & (lane2 < LANES // 4 + 2)

    def put(at, top, bottom):
        out[at : at + top.shape[0], :] = jnp.where(jnp.full(top.shape, lower), bottom, top)

    for i, part in enumerate(parts):
        put(i * DEPTH, part[0:DEPTH], part[k - DEPTH : k])
    for j in range(cols // LANES):
        lanes = slice(LANES * j, LANES * j + LANES)
        put(3 * DEPTH + 2 * j, el[0:2, lanes], el[rows - 2 : rows, lanes])
    packed = parts[2]
    put(
        2 * DEPTH,
        jnp.where(quarter, turned[0:2], packed[0:2]),
        jnp.where(quarter, turned[14:16], packed[k - DEPTH : k - DEPTH + 2]),
    )


def near_message_kernel(coarse, side, el, after, to_n):
    k = coarse.shape[0] // 4
    over, near, run, near_run = (coarse[i * k : (i + 1) * k, :] for i in range(4))
    message((over, run, edges(near, near_run)), side[...], el, lax.axis_index("rows") % 2 == 0, to_n)


def middle_kernel(coefs, el, out, recip, zc, zw, ze, rc, rw, re):
    rows, cols = el.shape
    chunks = cols // LANES
    coef = coefficient_tiles(coefs)
    z_planes, r_planes = (zc, zw, ze), (rc, rw, re)
    inner, core = range(1, chunks - 1), range(2, chunks - 2)
    blank = jnp.zeros((8, LANES), jnp.float32)
    for at in (0, rows + 8):
        for j in inner:
            for ref in z_planes + r_planes:
                ref[j, at : at + 8, :] = blank

    for t in range(rows // 8):
        row = 8 + 8 * t
        for j in range(chunks):
            zc[j, pl.ds(row, 8), :] = el[pl.ds(8 * t, 8), LANES * j : LANES * j + LANES]
        spread(z_planes, inner, row)

    for t in range(rows // 8):
        row = 8 + 8 * t
        for j in inner:
            total = reciprocal_total(z_planes, j, row, coef)
            rc[j, pl.ds(row, 8), :] = total
            recip[j - 1, pl.ds(8 * t, 8), :] = total
        spread(r_planes, core, row)

    for t in range(rows // 8):
        row = 8 + 8 * t
        for j in core:
            for i, field in enumerate(fields(z_planes, r_planes, j, row, coef)):
                out[i, j - 2, pl.ds(8 * t, 8), :] = field


def outer_kernel(coefs, el, side, known, out, recip, zc, zw, ze, rc, rw, re):
    rows, cols = el.shape
    chunks = cols // LANES
    coef = coefficient_tiles(coefs)
    z_planes, r_planes = (zc, zw, ze), (rc, rw, re)
    order = (chunks - 3, chunks - 2, chunks - 1, chunks, 0, 1, 2)
    blank = jnp.zeros((8, LANES), jnp.float32)
    for at in (0, rows + 8):
        for i in range(1, 6):
            for ref in z_planes + r_planes:
                ref[i, at : at + 8, :] = blank

    for t in range(rows // 8):
        row = 8 + 8 * t
        at = pl.ds(8 * t, 8)
        for i, j in enumerate(order):
            zc[i, pl.ds(row, 8), :] = el[at, LANES * j : LANES * j + LANES] if j < chunks else side[at, :]
        spread(z_planes, range(1, 6), row)

    for t in range(rows // 8):
        row = 8 + 8 * t
        at = pl.ds(8 * t, 8)
        for i, j in enumerate(order):
            if i in (2, 3, 4):
                total = reciprocal_total(z_planes, i, row, coef)
                recip[i - 2, at, :] = total
            else:
                total = known[j - 1, at, :]
            rc[i, pl.ds(row, 8), :] = total
        spread(r_planes, (1, 2, 4, 5), row)

    for t in range(rows // 8):
        row = 8 + 8 * t
        for n, i in enumerate((4, 5, 1, 2)):
            for which, field in enumerate(fields(z_planes, r_planes, i, row, coef)):
                out[which, n, pl.ds(8 * t, 8), :] = field


def inflow_kernel(
    coefs, coarse, from_n, from_f, el, side, middle, outer, middle_recip, outer_recip, mk, out_hbm,
    kc, kw, ke, sc, sw, se, run, gain, flow, zc, zw, ze, rc, rw, re, up_ref, vv_ref, out, out_sem,
):
    k = coarse.shape[0] // 4
    rows, cols = mk.shape
    chunks = cols // LANES
    r, count = lax.axis_index("rows"), lax.axis_size("rows")
    upper = r % 2 == 0
    coef = coefficient_tiles(coefs)
    n, f = from_n[...], from_f[...]
    cond = jnp.full(n.shape, upper)

    def unpack(x, gone):
        rest = lambda part, value: jnp.where(jnp.full(part.shape, gone), value, part)
        packed = x[2 * DEPTH : 3 * DEPTH]
        parts = (
            rest(x[0:DEPTH], OUTSIDE),
            rest(packed, OUTSIDE),
            rest(x[DEPTH : 2 * DEPTH], 0.0),
            rest(pltpu.roll(jnp.concatenate([packed, x[0:6]], axis=0), LANES // 2, 1)[0:DEPTH], 0.0),
        )
        lines = rest(x[3 * DEPTH : 3 * DEPTH + 2 * chunks], OUTSIDE)
        turned = pltpu.roll(x[2 * DEPTH : 2 * DEPTH + 8], LANES - LANES // 4, 1)[0:2]
        return parts, [lines[2 * j : 2 * j + 2] for j in range(chunks)] + [rest(turned, OUTSIDE)]

    above, above_lines = unpack(jnp.where(cond, f, n), r == 0)
    below, below_lines = unpack(jnp.where(cond, n, f), r == count - 1)

    k_planes, s_planes = (kc, kw, ke), (sc, sw, se)
    around = lambda size: (lambda j: j % size)
    for j in range(2):
        for ref, base, first, total in ((kc, 0, 8, 3 * k + 16), (run, 2, 0, 3 * k)):
            ref[j, 0 : first + k, :] = jnp.zeros((first + k, LANES), jnp.float32)
            ref[j, first + 2 * k : total, :] = jnp.zeros((total - first - 2 * k, LANES), jnp.float32)
            ref[j, first + k - DEPTH : first + k, :] = above[base + j]
            ref[j, first + k : first + 2 * k, :] = coarse[(base + j) * k : (base + j + 1) * k, :]
            ref[j, first + 2 * k : first + 2 * k + DEPTH, :] = below[base + j]
    for t in range(3 * k // 8 + 2):
        spread(k_planes, range(2), 8 * t, around(2))
    recip = {}
    for j in range(2):
        for t in range(3 * k // 8):
            recip[j, t] = reciprocal_total(k_planes, j, 8 + 8 * t, coef)
    inner = range(1, 3 * k // 8 - 1)
    for j in range(2):
        for t in inner:
            for d in range(8):
                gain[d, j, 8 * t : 8 * t + 8, :] = inward(k_planes, j, 8 + 8 * t, d, coef)

    z_planes, r_planes = (zc, zw, ze), (rc, rw, re)
    ring = around(chunks + 1)
    every = range(chunks + 1)
    for j in every:
        up2, down2 = above_lines[j], below_lines[j]
        if j < chunks:
            first, last = el[0:8, LANES * j : LANES * j + LANES], el[rows - 8 : rows, LANES * j : LANES * j + LANES]
        else:
            first, last = side[0:8, :], side[rows - 8 : rows, :]
        blank = jnp.zeros((8, LANES), jnp.float32)
        for at in (0, 16, 32):
            zc[j, at : at + 8, :] = blank
        zc[j, 8:16, :] = jnp.concatenate([up2, first[0:2], last[6:8], down2], axis=0)
        zc[j, 24:32, :] = jnp.concatenate([up2[1:2], first[0:3], last[5:8], down2[0:1]], axis=0)
    for row in (0, 8, 16, 24, 32):
        spread(z_planes, every, row, ring)
    for j in every:
        total = reciprocal_total(z_planes, j, 8, coef)
        if 1 <= j < chunks - 1:
            near = middle_recip.at[j - 1]
        else:
            near = outer_recip.at[{chunks - 1: 0, chunks: 1, 0: 2}[j]]
        first, last = near[0:8, :], near[rows - 8 : rows, :]
        for at in (0, 16):
            rc[j, at : at + 8, :] = jnp.zeros((8, LANES), jnp.float32)
        rc[j, 8:16, :] = jnp.concatenate([total[1:3], first[1:3], last[5:7], total[5:7]], axis=0)
    for row in (0, 8, 16):
        spread(r_planes, every, row, ring)
    border = {}
    lifted = (zc.at[:, 16:40, :], zw.at[:, 16:40, :], ze.at[:, 16:40, :])

    for j in range(2):
        for t in range(3 * k // 8):
            sc[j, 8 * t : 8 * t + 8, :] = recip[j, t] * run[j, 8 * t : 8 * t + 8, :]
    for t in range(3 * k // 8):
        spread(s_planes, range(2), 8 * t, around(2))
    for sweep in range(ITERS):
        for j in range(2):
            for t in inner:
                parts = [gain[d, j, 8 * t : 8 * t + 8, :] * neighbour(s_planes, j, 8 * t, d) for d in range(8)]
                total = ((parts[0] + parts[1]) + (parts[2] + parts[3])) + (
                    (parts[4] + parts[5]) + (parts[6] + parts[7])
                )
                flow[j, 8 * t : 8 * t + 8, :] = run[j, 8 * t : 8 * t + 8, :] + total
        for j in range(sweep, chunks, ITERS):
            border[j] = fields(lifted, r_planes, j, 8, coef, 1, 6)
        if sweep < ITERS - 1:
            for j in range(2):
                for t in inner:
                    sc[j, 8 * t : 8 * t + 8, :] = recip[j, t] * flow[j, 8 * t : 8 * t + 8, :]
            for t in inner:
                spread(s_planes, range(2), 8 * t, around(2))

    lane = iota((8, LANES), 1)
    block = lane // 8
    step = jnp.where(lane % 8 == 7, 1, jnp.where(lane % 8 == 0, -1, 0))
    per = LANES // 8
    for t in inner:
        main = flow[0, 8 * t : 8 * t + 8, :]
        apart = flow[1, 8 * t : 8 * t + 8, :]
        for j in range(chunks):
            here = block + per * j
            over = here + step
            up_ref[j, 8 * t : 8 * t + 8, :] = jnp.take_along_axis(main, here, axis=1, mode="promise_in_bounds")
            v = jnp.take_along_axis(main, over & (LANES - 1), axis=1, mode="promise_in_bounds")
            if j == 0:
                far = jnp.take_along_axis(apart, over & (LANES - 1), axis=1, mode="promise_in_bounds")
                v = jnp.where(lane == 0, far, v)
            if j == chunks - 1:
                far = jnp.take_along_axis(apart, over & (LANES - 1), axis=1, mode="promise_in_bounds")
                v = jnp.where(lane == LANES - 1, far, v)
            vv_ref[j, 8 * t : 8 * t + 8, :] = v

    sub = iota((8, LANES), 0)
    high = sub < 4
    writes = []
    for b in range(rows // 8):
        for j in range(chunks):
            lanes = slice(LANES * j, LANES * j + LANES)
            at = slice(8 * b, 8 * b + 8)
            row = k + b
            wide = [jnp.broadcast_to(up_ref[j, row + i : row + i + 1, :], (8, LANES)) for i in (-1, 0, 1)]
            apart = [jnp.broadcast_to(vv_ref[j, row + i : row + i + 1, :], (8, LANES)) for i in (-1, 0, 1)]
            if 2 <= j < chunks - 2:
                a = [middle[i, j - 2, at, :] for i in range(4)]
            else:
                a = [outer[i, j if j < 2 else j - chunks + 4, at, :] for i in range(4)]
            if b == 0:
                a = [jnp.where(sub < 2, pltpu.roll(border[j][i], 7, 0), a[i]) for i in range(4)]
            if b == rows // 8 - 1:
                a = [jnp.where(sub > 5, pltpu.roll(border[j][i], 1, 0), a[i]) for i in range(4)]
            out[at, lanes] = mk[at, lanes].astype(jnp.float32) + (
                (a[0] * wide[1] + a[1] * apart[1])
                + (a[2] * jnp.where(high, wide[0], wide[2]) + a[3] * jnp.where(high, apart[0], apart[2]))
            )
        size = rows // PARTS
        if (8 * b + 8) % size == 0:
            p = 8 * b // size
            lines = pl.ds(p * size, size)
            copy = pltpu.make_async_copy(out.at[lines, :], out_hbm.at[lines, :], out_sem.at[p])
            copy.start()
            writes.append(copy)
    for copy in writes:
        copy.wait()


def swap(x, axis, far):
    sizes = {name: lax.axis_size(name) for name in ("rows", "cols")}
    pairs = []
    for r in range(sizes["rows"]):
        for c in range(sizes["cols"]):
            to = {"rows": r, "cols": c}
            i = to[axis]
            partner = i ^ 1 if not far else i + 1 if i % 2 else i - 1
            if 0 <= partner < sizes[axis]:
                to[axis] = partner
            else:
                other = "cols" if axis == "rows" else "rows"
                to[other] ^= 1
            pairs.append((r * sizes["cols"] + c, to["rows"] * sizes["cols"] + to["cols"]))
    return lax.ppermute(x, ("rows", "cols"), pairs)


def f32(*shape):
    return jax.ShapeDtypeStruct(shape, jnp.float32)


def whole(count):
    return [pl.BlockSpec(memory_space=VMEM)] * count


def on_device(elevation, data_mask, tie_order):
    rows, cols = elevation.shape
    k, chunks = rows // 8, cols // LANES
    params = pltpu.CompilerParams(vmem_limit_bytes=LIMIT)
    dma = pltpu.SemaphoreType.DMA
    hbm = pl.BlockSpec(memory_space=pltpu.HBM)
    tie_order, elevation, data_mask = (
        pltpu.with_memory_space_constraint(x, pltpu.HBM) for x in (tie_order, elevation, data_mask)
    )
    msg = pl.pallas_call(
        column_message_kernel,
        out_shape=f32(k + 8, LANES),
        in_specs=[hbm] * 2,
        out_specs=whole(1)[0],
        scratch_shapes=[
            VMEM((rows, 2 * LANES), jnp.float32),
            VMEM((rows, 2 * LANES), jnp.int32),
            dma((2,)),
            dma((2,)),
        ],
        compiler_params=params,
        name="column_message",
    )(elevation, data_mask)
    from_b = swap(msg, "cols", True)
    from_a = swap(msg, "cols", False)
    cost = pl.CostEstimate(flops=10_000_000, bytes_accessed=3_000_000, transcendentals=0)
    own, el, mk, coefs = pl.pallas_call(
        overview_kernel,
        out_shape=[
            f32(2 * k, LANES),
            f32(rows, cols),
            jax.ShapeDtypeStruct((rows, cols), jnp.int32),
            f32(8, LANES),
        ],
        in_specs=[hbm] * 3 + whole(1),
        out_specs=whole(4),
        scratch_shapes=[pltpu.SMEM((8,), jnp.int32), dma, dma((PIECES,)), dma((PIECES,))],
        compiler_params=params,
        cost_estimate=cost,
        name="overview",
    )(tie_order, elevation, data_mask, msg)
    plane = lambda count, height: VMEM((count, height, LANES), jnp.float32)
    middle, middle_recip = pl.pallas_call(
        middle_kernel,
        out_shape=[f32(4, chunks - 4, rows, LANES), f32(chunks - 2, rows, LANES)],
        in_specs=whole(2),
        out_specs=whole(2),
        scratch_shapes=[plane(chunks, rows + 16)] * 6,
        compiler_params=params,
        cost_estimate=cost,
        name="middle_fields",
    )(coefs, el)
    size = (3 * DEPTH + 2 * chunks + 7) // 8 * 8
    coarse, side, to_f = pl.pallas_call(
        row_message_kernel,
        out_shape=[f32(4 * k, LANES), f32(rows, LANES), f32(size, LANES)],
        in_specs=whole(5),
        out_specs=whole(3),
        compiler_params=params,
        name="far_message",
    )(own, from_a, from_b, el, middle_recip)
    from_f = swap(to_f, "rows", True)
    outer, outer_recip = pl.pallas_call(
        outer_kernel,
        out_shape=[f32(4, 4, rows, LANES), f32(3, rows, LANES)],
        in_specs=whole(4),
        out_specs=whole(2),
        scratch_shapes=[plane(7, rows + 16)] * 6,
        compiler_params=params,
        cost_estimate=cost,
        name="outer_fields",
    )(coefs, el, side, middle_recip)
    to_n = pl.pallas_call(
        near_message_kernel,
        out_shape=f32(size, LANES),
        in_specs=whole(4),
        out_specs=whole(1)[0],
        compiler_params=params,
        name="near_message",
    )(coarse, side, el, outer_recip)
    from_n = swap(to_n, "rows", False)
    return pl.pallas_call(
        inflow_kernel,
        out_shape=f32(rows, cols),
        in_specs=whole(11),
        out_specs=hbm,
        scratch_shapes=[plane(2, 3 * k + 16)] * 3
        + [plane(2, 3 * k)] * 4
        + [VMEM((8, 2, 3 * k, LANES), jnp.float32), plane(2, 3 * k)]
        + [plane(chunks + 1, 40)] * 3
        + [plane(chunks + 1, 24)] * 3
        + [plane(chunks, 3 * k)] * 2
        + [VMEM((rows, cols), jnp.float32), dma((PARTS,))],
        compiler_params=params,
        name="inflow",
    )(coefs, coarse, from_n, from_f, el, side, middle, outer, middle_recip, outer_recip, mk)


def solution(mesh):
    in_specs = (P("rows", "cols"), P("rows", "cols"), P())
    out_specs = P("rows", "cols")
    return jax.shard_map(
        on_device, mesh=mesh, in_specs=in_specs, out_specs=out_specs, check_vma=False
    )
```
